512 devices in a mesh: band: 32 (over y, x), grp: 16 (over z, core).
Axes of the slice: x: 4, y: 8, z: 8, core: 2. Of those that a mesh axis runs over, the one named last changes fastest.
Arguments:
- tokens: bfloat16 [4096, 48, 384], P(('band', 'grp')), may hold values from -6 to 6
- cotangent: bfloat16 [4096, 48, 384], P(('band', 'grp')), may hold values from -6 to 6
- ocean_mask: int32 [4096, 48], P(('band', 'grp')), may hold values 0 or 1
- land_mask: int32 [512, 6], P(('band', 'grp')), may hold values from 0 to 1, as said below
- w_qkv: bfloat16 [384, 1152], replicated, may hold values from -0.3125 to 0.3125
- w_proj: bfloat16 [384, 384], replicated, may hold values from -0.3125 to 0.3125
- rel_bias: float32 [12, 64, 64], replicated, may hold values from -4 to 345
Outputs:
- block_out: bfloat16 [4096, 48, 384], P(('band', 'grp'))
- token_grad: bfloat16 [4096, 48, 384], P(('band', 'grp'))
- grad_qkv: float32 [442368], P(('band', 'grp'))
- grad_proj: float32 [147456], P(('band', 'grp'))
- grad_bias: float32 [49152], P(('band', 'grp'))
The draws below stay inside these ranges and needn't reach their ends.
Inputs may be any that keep to these rules, and one draw needn't show every extreme that they name: `land_mask`: for every r < 256 the windows with land flag 0 in rows r and r + 256 together number at most 8, exactly 8 for r = 0.
All inputs are finite; a program needn't handle non-finite values. No bound on the sum of `ocean_mask` on one device may be relied on, other than what follows from the above.
Results may differ from the reference program's by a relative error of at most 0.0091.
Values may be sent and summed in bfloat16 or wider, within the bound.
A program may use at most 64 MiB of HBM per device.

```python
import math
import jax
import jax.numpy as jnp
from jax import lax

C = 384
HEADS = 12
WB = 6
KEEP = 4
WROWS = 512
LAT = 4096
LON = 48


def draw_land_mask(key, part):
    key = jax.random.fold_in(key, 11)
    first_key, second_key, third_key = jax.random.split(key, 3)
    half_rows = WROWS // 2
    totals = jax.random.randint(first_key, (half_rows,), KEEP, 2 * KEEP + 1)
    totals = totals.at[0].set(2 * KEEP)
    lower = jnp.maximum(totals - WB, 0)
    upper = jnp.minimum(totals, WB) + 1
    firsts = jax.random.randint(second_key, (half_rows,), lower, upper)
    counts = jnp.concatenate([firsts, totals - firsts])
    scores = jax.random.randint(third_key, (WROWS, WB), 0, 1 << 20) * WB
    scores = scores + lax.broadcasted_iota(jnp.int32, (WROWS, WB), 1)
    order = jnp.argsort(scores, axis=1)
    places = jnp.argsort(order, axis=1)
    return jnp.where(places < counts[:, None], 0, 1).astype(jnp.int32)


def draw_rel_bias(key, part):
    key = jax.random.fold_in(key, 23)
    base_key = jax.random.fold_in(key, 0)
    shape = (HEADS, 64, 64)
    return jnp.clip(jax.random.normal(base_key, shape, jnp.float32), -4.0, 4.0)


def place_ends(result, key, low, top_value):
    longest = result.shape.index(max(result.shape))
    spots = []
    for shift in (0, 1):
        where = [jax.random.randint(jax.random.fold_in(key, axis), (), 0, length) for axis, length in enumerate(result.shape)]
        where[longest] = (where[longest] + shift) % result.shape[longest]
        spots.append(tuple(where))
    return result.at[spots[0]].set(low).at[spots[1]].set(top_value)


def block_levels(own_key, dims, shards, least, top_value):
    def one(axis_at, blocks):
        draws = jax.random.uniform(jax.random.fold_in(jax.random.fold_in(own_key, 6), axis_at), (blocks,), jnp.float32, least / len(shards), top_value / len(shards))
        return jnp.repeat(jnp.exp(draws), dims[axis_at] // blocks).reshape((-1,) + (1,) * (len(dims) - axis_at - 1))

    loudness = one(*shards[0])
    for cut in shards[1:]:
        loudness = loudness * one(*cut)
    return loudness


def gaussian(key, extent, width, reach, pieces=(), kind=jnp.bfloat16):
    gain = block_levels(key, extent, pieces, -0.22, 0.18) if pieces else 1.0
    result = jax.random.normal(key, extent, jnp.float32) * width * gain
    return jnp.minimum(jnp.maximum(result, -reach), reach).astype(kind)


def setup_inputs(seed: int = 0) -> dict:
    streams_of = jax.random.split(jax.random.key(seed), 8)
    tokens = gaussian(streams_of[0], (LAT, LON, C), 1.0, 6.0, ((0, 512),))
    cotangent = gaussian(streams_of[1], (LAT, LON, C), 1.0, 6.0, ((0, 512),))
    ocean_mask = place_ends((jax.random.randint(streams_of[2], (LAT, LON), 0, 5) < 4).astype(jnp.int32), jax.random.fold_in(streams_of[2], 1), 0, 1)
    land_mask = draw_land_mask(jax.random.fold_in(streams_of[7], 71), 0)
    w_qkv = gaussian(streams_of[4], (C, 3 * C), C ** -0.5, 0.3125)
    w_proj = gaussian(streams_of[5], (C, C), C ** -0.5, 0.3125)
    rel_bias = draw_rel_bias(jax.random.fold_in(streams_of[7], 71), 0)
    return dict(tokens=tokens, cotangent=cotangent, ocean_mask=ocean_mask, land_mask=land_mask, w_qkv=w_qkv, w_proj=w_proj, rel_bias=rel_bias)


epsilon = 1e-05
masked_score = -1e+30

def window_pass(window_in, window_cot, window_mask, w_qkv, w_proj, rel_bias):
    channels = window_in.shape[-1]
    head_count = rel_bias.shape[0]
    head_size = channels // head_count
    number = window_in.shape[0]
    score_scale = 1.0 / math.sqrt(head_size)
    values_in = window_in.astype(jnp.float32)
    average = lax.optimization_barrier(jnp.mean(values_in, -1, keepdims=True))
    centered = values_in - average
    inv_std = lax.rsqrt(lax.optimization_barrier(jnp.mean(centered * centered, -1, keepdims=True)) + epsilon)
    normed = centered * inv_std
    hidden = normed.astype(jnp.bfloat16).reshape(-1, channels)
    qkv = jnp.dot(hidden, w_qkv, preferred_element_type=jnp.float32).astype(jnp.bfloat16)
    qkv = qkv.reshape(number, 64, 3, head_count, head_size)
    queries = qkv[:, :, 0].astype(jnp.float32)
    key_rows = qkv[:, :, 1].astype(jnp.float32)
    values = qkv[:, :, 2].astype(jnp.float32)
    scores = jnp.einsum('bqhd,bkhd->bhqk', queries, key_rows) * score_scale + rel_bias[None]
    key_live = window_mask[:, None, None, :] > 0.5
    scores = jnp.where(key_live, scores, masked_score)
    row_max = lax.optimization_barrier(jnp.max(scores, -1, keepdims=True))
    weights = jnp.exp(scores - row_max)
    probs = weights / lax.optimization_barrier(jnp.sum(weights, -1, keepdims=True))
    probs_low = probs.astype(jnp.bfloat16)
    attended = jnp.einsum('bhqk,bkhd->bqhd', probs_low.astype(jnp.float32), values)
    attended = attended.astype(jnp.bfloat16).reshape(-1, channels)
    projected = jnp.dot(attended, w_proj, preferred_element_type=jnp.float32)
    query_mask = window_mask.reshape(-1, 1)
    update = (query_mask * projected).astype(jnp.bfloat16)
    out_grad = (query_mask * window_cot.reshape(-1, channels).astype(jnp.float32)).astype(jnp.bfloat16)
    grad_proj = jnp.dot(attended.T, out_grad, preferred_element_type=jnp.float32)
    attended_grad = jnp.dot(out_grad, w_proj.T, preferred_element_type=jnp.float32).astype(jnp.bfloat16)
    attended_grad = attended_grad.reshape(number, 64, head_count, head_size).astype(jnp.float32)
    probs_grad = jnp.einsum('bqhd,bkhd->bhqk', attended_grad, values)
    values_grad = jnp.einsum('bhqk,bqhd->bkhd', probs_low.astype(jnp.float32), attended_grad).astype(jnp.bfloat16)
    scores_grad = probs * (probs_grad - lax.optimization_barrier(jnp.sum(probs * probs_grad, -1, keepdims=True)))
    grad_bias = lax.optimization_barrier(jnp.sum(scores_grad, 0))
    scaled_grad = (scores_grad * score_scale).astype(jnp.bfloat16).astype(jnp.float32)
    queries_grad = jnp.einsum('bhqk,bkhd->bqhd', scaled_grad, key_rows).astype(jnp.bfloat16)
    keys_grad = jnp.einsum('bhqk,bqhd->bkhd', scaled_grad, queries).astype(jnp.bfloat16)
    qkv_grad = jnp.stack([queries_grad, keys_grad, values_grad], axis=2).reshape(-1, 3 * channels)
    grad_qkv = jnp.dot(hidden.T, qkv_grad, preferred_element_type=jnp.float32)
    hidden_grad = jnp.dot(qkv_grad, w_qkv.T, preferred_element_type=jnp.float32).reshape(number, 64, channels)
    window_grad = inv_std * (hidden_grad - lax.optimization_barrier(jnp.mean(hidden_grad, -1, keepdims=True)) - normed * lax.optimization_barrier(jnp.mean(hidden_grad * normed, -1, keepdims=True)))
    return (update.reshape(number, 64, channels), window_grad.astype(jnp.bfloat16), grad_qkv, grad_proj, grad_bias)

def to_windows(grid):
    shifted = jnp.concatenate([grid[4:], jnp.zeros_like(grid[:4])], 0)
    shifted = jnp.roll(shifted, -4, axis=1)
    band_rows = shifted.shape[0] // 8
    band_cols = shifted.shape[1] // 8
    tail = shifted.shape[2:]
    blocks = shifted.reshape((band_rows, 8, band_cols, 8) + tail)
    blocks = jnp.moveaxis(blocks, 2, 1)
    return blocks.reshape((band_rows, band_cols, 64) + tail)

def from_windows(blocks):
    band_rows, band_cols = (blocks.shape[0], blocks.shape[1])
    tail = blocks.shape[3:]
    grid = blocks.reshape((band_rows, band_cols, 8, 8) + tail)
    grid = jnp.moveaxis(grid, 2, 1).reshape((band_rows * 8, band_cols * 8) + tail)
    grid = jnp.roll(grid, 4, axis=1)
    return jnp.concatenate([jnp.zeros_like(grid[:4]), grid[:-4]], 0)

def reference(tokens, cotangent, ocean_mask, land_mask, w_qkv, w_proj, rel_bias):
    channels = tokens.shape[-1]
    windows_x = to_windows(tokens)
    windows_g = to_windows(cotangent)
    windows_m = to_windows(ocean_mask.astype(jnp.float32)) * (1.0 - land_mask.astype(jnp.float32))[:, :, None]
    start = (jnp.zeros((channels, 3 * channels), jnp.float32), jnp.zeros((channels, channels), jnp.float32), jnp.zeros(rel_bias.shape, jnp.float32))

    def advance(running, member):
        update, window_grad, part_qkv, part_proj, part_bias = window_pass(member[0], member[1], member[2], w_qkv, w_proj, rel_bias)
        return ((running[0] + part_qkv, running[1] + part_proj, running[2] + part_bias), (update, window_grad))
    totals, results = lax.scan(advance, start, (windows_x, windows_g, windows_m))
    block_out = (tokens.astype(jnp.float32) + from_windows(results[0]).astype(jnp.float32)).astype(jnp.bfloat16)
    token_grad = (cotangent.astype(jnp.float32) + from_windows(results[1]).astype(jnp.float32)).astype(jnp.bfloat16)
    return (block_out, token_grad, totals[0].reshape(-1), totals[1].reshape(-1), totals[2].reshape(-1))
```

```python
import math

import jax
import jax.numpy as jnp
from jax import lax
from jax.experimental import pallas as pl
from jax.experimental.pallas import tpu as pltpu
from jax.sharding import PartitionSpec as P

EPS = 1e-05
MASKED = -1e30
C = 384
WB = 6
HG = 3
SCALE = 1.0 / math.sqrt(32)
F32 = jnp.float32
BF16 = jnp.bfloat16
MESH = pl.DeviceIdType.MESH

NY, NX, NZ = 8, 4, 8
OWN = 192


def qkv_rows(g):
    return [("qkv", j, k) for j in range(3) for k in (g, 3 + g, 6 + g)]


PROJ_ROWS = [("proj", j, k) for j in range(3) for k in range(3)]
BIAS_ROWS = [("bias", j, 0) for j in range(3)]
PARTS = [
    (qkv_rows(0) + PROJ_ROWS[:7], 16, 16),
    (qkv_rows(1) + qkv_rows(2) + PROJ_ROWS[7:] + BIAS_ROWS, 24, 16),
]


def place_of(kind, j, k):
    return {"qkv": 9 * j + k, "proj": 27 + 3 * j + k, "bias": 36 + j}[kind]


def dot_nt(a, b):
    return lax.dot_general(a, b, (((1,), (1,)), ((), ())), preferred_element_type=F32)


def dot_tn(a, b):
    return lax.dot_general(a, b, (((0,), (0,)), ((), ())), preferred_element_type=F32)


def dot_nn(a, b):
    return lax.dot_general(a, b, (((1,), (0,)), ((), ())), preferred_element_type=F32)


def stage_mask(ocean, land, half, mask_ref):
    place = lax.broadcasted_iota(jnp.int32, (8, 48), 0)
    column = lax.broadcasted_iota(jnp.int32, (8, 48), 1)
    for w in range(WB):
        live = 1.0 - land[:, w : w + 1]
        pick = (column == lax.rem(place + (8 * w + 4), 48)).astype(F32) * live
        for i in range(4):
            row = jnp.broadcast_to(ocean[i : i + 1, :], (8, 48))
            value = jnp.sum(row * pick, axis=1, keepdims=True)
            at = OWN * half + 32 * w + 8 * i
            mask_ref[at : at + 8, :] = jnp.broadcast_to(value, (8, 128))


def stage_rows(rows, half, out_ref):
    for i, row in enumerate(rows):
        rolled = pltpu.roll(row.astype(F32), 44, 0)
        for w in range(WB):
            at = OWN * half + 32 * w + 8 * i
            out_ref[at : at + 8, :] = rolled[8 * w : 8 * w + 8, :]


def grid_row(src_ref, half, i):
    ats = [OWN * half + 32 * w + 8 * i for w in range(WB)]
    return pltpu.roll(jnp.concatenate([src_ref[at : at + 8, :] for at in ats], 0), 4, 0)


class Part:
    def __init__(self, rows, count, along_y, refs, here, send, sources, red_ref):
        (
            self.pk, self.pack, self.r0, self.s1, self.ra, self.ta, self.ra2, self.rb, self.tb, self.rb2,
            self.f, self.r3, self.tot, self.core_s, self.core_r, self.a1_s, self.a1_r, self.a2_s, self.a2_r,
            self.b1_s, self.b1_r, self.b2_s, self.b2_r, self.z_s, self.z_r,
        ) = refs
        self.rows, self.count, self.na = rows, count, along_y
        self.half = 2 * count
        self.nb = self.half - along_y
        self.here, self.send, self.sources, self.red = here, send, sources, red_ref
        self.sent = []

    def start(self):
        band, grp, y, x, z, core = self.here
        n = self.count
        grad_ref, bt_ref = self.sources
        lane = lax.broadcasted_iota(jnp.int32, (128, 128), 1)
        for i, (kind, j, k) in enumerate(self.rows):
            if kind == "bias":
                even = bt_ref[pl.ds(2 * j, 128, stride=6), :]
                odd = bt_ref[pl.ds(2 * j + 1, 128, stride=6), :]
                value = jnp.where(lane < 64, even, pltpu.roll(odd, 64, 1))
            else:
                at = k if kind == "qkv" else 9 + k
                value = grad_ref.at[at][pl.ds(j, 128, stride=3), :]
            self.pk[pl.ds(i, 128, stride=n), :] = value
        for i in range(len(self.rows), n):
            self.pk[pl.ds(i, 128, stride=n), :] = jnp.zeros((128, 128), F32)
        theirs = (1 - core) * self.half

        def narrow(i, carry):
            for j in range(NX):
                at = pl.multiple_of((i * NX + j) * 4 * n + theirs, 16)
                self.pack[i, j] = self.pk[pl.ds(at, self.half), :].astype(BF16)
            return carry

        lax.fori_loop(0, NY, narrow, 0)
        self.core_copy = self.send(
            self.pack, self.r0, self.core_s.at[0], self.core_r.at[0], (band, z * 2 + 1 - core)
        )

    def spread(self):
        band, grp, y, x, z, core = self.here
        n, na = self.count, self.na
        mine = core * self.half
        self.core_copy.wait()

        def add(i, carry):
            for j in range(NX):
                at = pl.multiple_of((i * NX + j) * 4 * n + mine, 16)
                total = self.pk[pl.ds(at, self.half), :] + self.r0[i, j].astype(F32)
                self.s1[i, j] = total.astype(BF16)
            return carry

        lax.fori_loop(0, NY, add, 0)
        self.b1, self.a1 = [], []
        for d in range(1, NX):
            to = lax.rem(x + d, NX)
            self.b1.append(
                self.send(
                    self.s1.at[:, to, pl.ds(na, self.nb), :], self.rb.at[d - 1],
                    self.b1_s.at[d - 1], self.b1_r.at[d - 1], (y * NX + to, grp),
                )
            )
        for d in range(1, NY):
            to = lax.rem(y + d, NY)
            self.a1.append(
                self.send(
                    self.s1.at[to, :, pl.ds(0, na), :], self.ra.at[d - 1],
                    self.a1_s.at[d - 1], self.a1_r.at[d - 1], (to * NX + x, grp),
                )
            )

    def turn(self):
        band, grp, y, x, z, core = self.here
        na = self.na
        total = self.s1[:, x, na : self.half, :].astype(F32)
        for d in range(1, NX):
            self.b1[d - 1].wait_recv()
            total = total + self.rb[d - 1].astype(F32)
        self.tb[...] = total.astype(BF16)
        self.b2, self.a2 = [], []
        for d in range(1, NY):
            to = lax.rem(y + d, NY)
            self.b2.append(
                self.send(
                    self.tb.at[to], self.rb2.at[d - 1],
                    self.b2_s.at[d - 1], self.b2_r.at[d - 1], (to * NX + x, grp),
                )
            )
        total = self.s1[y, :, 0:na, :].astype(F32)
        for d in range(1, NY):
            self.a1[d - 1].wait_recv()
            total = total + self.ra[d - 1].astype(F32)
        self.ta[...] = total.astype(BF16)
        for d in range(1, NX):
            to = lax.rem(x + d, NX)
            self.a2.append(
                self.send(
                    self.ta.at[to], self.ra2.at[d - 1],
                    self.a2_s.at[d - 1], self.a2_r.at[d - 1], (y * NX + to, grp),
                )
            )

    def last(self, i):
        band, grp, y, x, z, core = self.here
        quarter, zi, to_core = i // 4, (i // 2) % 2, i % 2
        to_z = 2 * (2 * core + quarter) + zi
        copy = pltpu.make_async_remote_copy(
            src_ref=self.f.at[quarter],
            dst_ref=self.r3.at[z],
            send_sem=self.z_s.at[i],
            recv_sem=self.z_r.at[z],
            device_id=(band, to_z * 2 + to_core),
            device_id_type=MESH,
        )
        return copy, jnp.logical_or(to_z != z, core != to_core)

    def share(self):
        band, grp, y, x, z, core = self.here
        n, na = self.count, self.na
        total = self.tb[y].astype(F32)
        for d in range(1, NY):
            self.b2[d - 1].wait_recv()
            total = total + self.rb2[d - 1].astype(F32)
        low = self.ta[x].astype(F32)
        for d in range(1, NX):
            self.a2[d - 1].wait_recv()
            low = low + self.ra2[d - 1].astype(F32)
        both = jnp.concatenate([low, total], 0)
        self.f[0] = both[0:n]
        self.f[1] = both[n : 2 * n]
        for i in range(8):
            copy, away = self.last(i)
            pl.when(away)(copy.start)

    def finish(self):
        band, grp, y, x, z, core = self.here
        own_core = z // 4
        for s in range(NZ):
            come = pltpu.make_async_remote_copy(
                src_ref=self.f.at[0],
                dst_ref=self.r3.at[s],
                send_sem=self.z_s.at[0],
                recv_sem=self.z_r.at[s],
                device_id=(band, z * 2 + 1 - core),
                device_id_type=MESH,
            )
            pl.when(jnp.logical_or(z != s, core != own_core))(come.wait_recv)

        @pl.when(core == own_core)
        def _():
            self.r3[z] = self.f[lax.rem(z // 2, 2)]

        total = self.r3[0]
        for s in range(1, NZ):
            total = total + self.r3[s]
        for i, row in enumerate(self.rows):
            at = place_of(*row)
            self.red[at : at + 1, :] = total[i : i + 1, :]

    def drain(self):
        for copy in self.a1 + self.a2 + self.b1 + self.b2:
            copy.wait_send()
        for i in range(8):
            copy, away = self.last(i)
            pl.when(away)(copy.wait_send)


def part_scratch(count, na):
    half = 2 * count
    nb = half - na
    dma = pltpu.SemaphoreType.DMA
    return [
        pltpu.VMEM((128 * count, 128), F32),
        pltpu.VMEM((NY, NX, half, 128), BF16),
        pltpu.VMEM((NY, NX, half, 128), BF16),
        pltpu.VMEM((NY, NX, half, 128), BF16),
        pltpu.VMEM((NY - 1, NX, na, 128), BF16),
        pltpu.VMEM((NX, na, 128), BF16),
        pltpu.VMEM((NX - 1, na, 128), BF16),
        pltpu.VMEM((NX - 1, NY, nb, 128), BF16),
        pltpu.VMEM((NY, nb, 128), BF16),
        pltpu.VMEM((NY - 1, nb, 128), BF16),
        pltpu.VMEM((2, count, 128), F32),
        pltpu.VMEM((NZ, count, 128), F32),
        pltpu.VMEM((count, 128), F32),
        dma((1,)), dma((1,)),
        dma((NY - 1,)), dma((NY - 1,)),
        dma((NX - 1,)), dma((NX - 1,)),
        dma((NX - 1,)), dma((NX - 1,)),
        dma((NY - 1,)), dma((NY - 1,)),
        dma((8,)), dma((NZ,)),
    ]


def kernel(
    tok_hbm, cot_hbm, oce_hbm, land_hbm, wqkv_hbm, wproj_hbm, rb_hbm,
    block_ref, grad_out_ref, red_ref,
    tok_ref, cot_ref, oce_ref, land_ref, wqkv_ref, wproj_ref, rb_ref,
    htok_ref, hcot_ref, hoce_ref, uu_ref, ug_ref, hu_ref, hg_ref,
    x_ref, c_ref, n_ref, inv_ref, mask_ref, h_ref, qkv_ref, dz_ref, do_ref, o_ref, dqkv_ref,
    p_ref, bias_ref, db_ref, grad_ref, bt_ref, load_sem, halo_s, halo_r, *rest,
):
    band = lax.axis_index("band")
    grp = lax.axis_index("grp")
    y, x = band // NX, lax.rem(band, NX)
    z, core = grp // 2, lax.rem(grp, 2)
    linear = band * 16 + grp
    after = lax.rem(linear + 1, 512)
    before = lax.rem(linear + 511, 512)
    after_id = (after // 16, lax.rem(after, 16))
    before_id = (before // 16, lax.rem(before, 16))

    loads = []
    for i, (src, dst) in enumerate(
        (
            (tok_hbm, tok_ref), (oce_hbm, oce_ref), (land_hbm, land_ref), (wqkv_hbm, wqkv_ref),
            (cot_hbm, cot_ref), (wproj_hbm, wproj_ref), (rb_hbm, rb_ref),
        )
    ):
        loads.append(pltpu.make_async_copy(src, dst, load_sem.at[i]))
        loads[-1].start()

    barrier = pltpu.get_barrier_semaphore()
    peers = [after_id, before_id]
    peers += [(band, lax.rem(grp + d, 16)) for d in range(1, 16)]
    peers += [(lax.rem(y + d, NY) * NX + x, grp) for d in range(1, NY)]
    peers += [(y * NX + lax.rem(x + d, NX), grp) for d in range(1, NX)]
    for peer in peers:
        pl.semaphore_signal(barrier, inc=1, device_id=peer, device_id_type=MESH)

    def send(src, dst, s, r, to):
        copy = pltpu.make_async_remote_copy(
            src_ref=src, dst_ref=dst, send_sem=s, recv_sem=r, device_id=to, device_id_type=MESH
        )
        copy.start()
        return copy

    loads[0].wait()
    stage_rows([tok_ref[4 + i] for i in range(4)], 0, x_ref)

    pl.semaphore_wait(barrier, len(peers))
    halos = [
        send(tok_hbm.at[pl.ds(0, 4)], htok_ref, halo_s.at[0], halo_r.at[0], before_id),
        send(oce_hbm, hoce_ref, halo_s.at[1], halo_r.at[1], before_id),
        send(cot_hbm.at[pl.ds(0, 4)], hcot_ref, halo_s.at[2], halo_r.at[2], before_id),
    ]

    def norm(i, carry):
        rows = pl.ds(pl.multiple_of(i * 64, 64), 64)
        value = x_ref[rows, :]
        centered = value - jnp.mean(value, -1, keepdims=True)
        inv = lax.rsqrt(jnp.mean(centered * centered, -1, keepdims=True) + EPS)
        n = centered * inv
        n_ref[rows, :] = n
        inv_ref[rows, :] = jnp.broadcast_to(inv, (64, 128))
        h_ref[rows, :] = n.astype(BF16)
        return carry

    def project(half):
        rows = slice(OWN * half, OWN * half + OWN)
        qkv_ref[rows, :] = dot_nn(h_ref[rows, :], wqkv_ref[...]).astype(BF16)

    def pull(half):
        rows = slice(OWN * half, OWN * half + OWN)
        wide = jnp.concatenate([mask_ref[rows, :]] * 3, 1)
        dz_ref[rows, :] = (wide * c_ref[rows, :]).astype(BF16)
        do_ref[rows, :] = dot_nt(dz_ref[rows, :], wproj_ref[...]).astype(BF16)

    lax.fori_loop(0, 3, norm, 0)
    loads[1].wait()
    loads[2].wait()
    land = land_ref[...].astype(F32)
    stage_mask(oce_ref[4:8, :].astype(F32), land, 0, mask_ref)
    loads[3].wait()
    project(0)
    loads[4].wait()
    stage_rows([cot_ref[4 + i] for i in range(4)], 0, c_ref)
    loads[5].wait()
    pull(0)
    loads[6].wait()
    for i in range(6):
        pair = jnp.concatenate([rb_ref[2 * i], rb_ref[2 * i + 1]], 0)
        bias_ref[:, 128 * i : 128 * i + 128] = pair.T
    db_ref[...] = jnp.zeros_like(db_ref)

    here_lower = jnp.broadcast_to(linear, (48, C)) < 511
    halos[0].wait_recv()
    stage_rows([jnp.where(here_lower, htok_ref[i].astype(F32), 0.0) for i in range(4)], 1, x_ref)
    lax.fori_loop(3, 6, norm, 0)
    project(1)
    halos[1].wait_recv()
    ocean = jnp.where(jnp.broadcast_to(linear, (4, 48)) < 511, hoce_ref[0:4, :].astype(F32), 0.0)
    stage_mask(ocean, land, 1, mask_ref)

    head = lax.broadcasted_iota(jnp.int32, (64, 128), 1) // 32
    picks = [(head == i).astype(F32) for i in range(4)]
    picks_low = [p.astype(BF16) for p in picks]

    def spread(a):
        return jnp.concatenate([a * p for p in picks_low], 0)

    def fold(value):
        total = value[0:64] * picks[0]
        for i in range(1, 4):
            total = total + value[64 * i : 64 * i + 64] * picks[i]
        return total

    def two(w):
        first = pl.ds(pl.multiple_of(w * 32, 32), 32)
        second = pl.ds(pl.multiple_of(OWN + w * 32, 32), 32)
        return first, second

    def load(ref, w, lanes):
        first, second = two(w)
        return jnp.concatenate([ref[first, lanes], ref[second, lanes]], 0)

    def store(ref, w, lanes, value):
        first, second = two(w)
        ref[first, lanes] = value[0:32]
        ref[second, lanes] = value[32:64]

    def lanes_of(g):
        return [slice(C * i + 128 * g, C * i + 128 * g + 128) for i in range(3)] + [
            slice(256 * g, 256 * g + 256)
        ]

    def forward(w, carry):
        whole = pl.ds(pl.multiple_of(w * 64, 64), 64)
        live = jnp.concatenate([load(mask_ref, w, slice(0, 128))] * 2, 1) > 0.5
        for g in range(HG):
            q_lanes, k_lanes, v_lanes, wide = lanes_of(g)
            q4 = spread(load(qkv_ref, w, q_lanes))
            s = dot_nt(load(qkv_ref, w, k_lanes), q4) * SCALE + bias_ref[:, wide]
            s = jnp.where(live, s, MASKED)
            weights = jnp.exp(s - jnp.max(s, 0, keepdims=True))
            p = weights * (1.0 / jnp.sum(weights, 0, keepdims=True))
            p_ref[whole, wide] = p
            store(o_ref, w, q_lanes, fold(dot_tn(p.astype(BF16), load(qkv_ref, w, v_lanes))).astype(BF16))
        return carry

    def backward(g):
        q_lanes, k_lanes, v_lanes, wide = lanes_of(g)

        def step(w, carry):
            whole = pl.ds(pl.multiple_of(w * 64, 64), 64)
            q4 = spread(load(qkv_ref, w, q_lanes))
            do4 = spread(load(do_ref, w, q_lanes))
            p = p_ref[whole, wide]
            dp = dot_nt(load(qkv_ref, w, v_lanes), do4)
            store(dqkv_ref, w, v_lanes, dot_nn(p.astype(BF16), do4).astype(BF16))
            ds = p * (dp - jnp.sum(p * dp, 0, keepdims=True))
            db_ref[:, wide] += ds
            dsc = (ds * SCALE).astype(BF16)
            store(dqkv_ref, w, k_lanes, dot_nn(dsc, q4).astype(BF16))
            dq = fold(dot_tn(dsc, load(qkv_ref, w, k_lanes)))
            store(dqkv_ref, w, q_lanes, dq.astype(BF16))
            return carry

        lax.fori_loop(0, WB, step, 0, unroll=3)
        for k in (g, 3 + g, 6 + g):
            grad_ref[k] = dot_tn(h_ref[...], dqkv_ref[:, 128 * k : 128 * k + 128])

    lax.fori_loop(0, WB, forward, 0, unroll=2)

    halos[2].wait_recv()
    stage_rows([jnp.where(here_lower, hcot_ref[i].astype(F32), 0.0) for i in range(4)], 1, c_ref)
    pull(1)

    here = (band, grp, y, x, z, core)
    parts = []
    at = 0
    for rows, count, na in PARTS:
        parts.append(Part(rows, count, na, rest[at : at + 25], here, send, (grad_ref, bt_ref), red_ref))
        at += 25
    first, second = parts

    for k in range(3):
        grad_ref[9 + k] = dot_tn(o_ref[...], dz_ref[:, 128 * k : 128 * k + 128])
    backward(0)
    first.start()
    wide_mask = jnp.concatenate([mask_ref[...]] * 3, 1)
    x_ref[...] = wide_mask * dot_nn(o_ref[...], wproj_ref[...])
    for i in range(4):
        uu_ref[i] = grid_row(x_ref, 1, i).astype(BF16)
    halo_u = send(uu_ref, hu_ref, halo_s.at[3], halo_r.at[3], after_id)
    for i in range(4):
        row = grid_row(x_ref, 0, i).astype(BF16).astype(F32)
        block_ref[4 + i] = (tok_ref[4 + i].astype(F32) + row).astype(BF16)
    first.spread()
    backward(1)
    backward(2)
    for i in range(6):
        bt_ref[128 * i : 128 * i + 128, 0:64] = db_ref[:, 128 * i : 128 * i + 128].T
    second.start()
    first.turn()

    x_ref[...] = dot_nt(dqkv_ref[...], wqkv_ref[...])
    second.spread()

    def back(i, carry):
        rows = pl.ds(pl.multiple_of(i * 64, 64), 64)
        dh = x_ref[rows, :]
        n = n_ref[rows, :]
        inv = jnp.concatenate([inv_ref[rows, :]] * 3, 1)
        slope = jnp.mean(dh * n, -1, keepdims=True)
        x_ref[rows, :] = inv * (dh - jnp.mean(dh, -1, keepdims=True) - n * slope)
        return carry

    lax.fori_loop(0, WB, back, 0)
    for i in range(4):
        ug_ref[i] = grid_row(x_ref, 1, i).astype(BF16)
    halo_g = send(ug_ref, hg_ref, halo_s.at[4], halo_r.at[4], after_id)
    first.share()
    for i in range(4):
        row = grid_row(x_ref, 0, i).astype(BF16).astype(F32)
        grad_out_ref[4 + i] = (cot_ref[4 + i].astype(F32) + row).astype(BF16)
    second.turn()
    inner = jnp.broadcast_to(linear, (4, 48, C)) > 0
    halo_u.wait_recv()
    low = jnp.where(inner, hu_ref[...].astype(F32), 0.0)
    block_ref[0:4] = (tok_ref[0:4].astype(F32) + low).astype(BF16)
    first.finish()
    second.share()
    halo_g.wait_recv()
    low = jnp.where(inner, hg_ref[...].astype(F32), 0.0)
    grad_out_ref[0:4] = (cot_ref[0:4].astype(F32) + low).astype(BF16)
    red_ref[39:40, :] = jnp.zeros((1, 128), F32)
    second.finish()
    for copy in halos + [halo_u, halo_g]:
        copy.wait_send()
    first.drain()
    second.drain()


def local(tokens, cotangent, ocean_mask, land_mask, w_qkv, w_proj, rel_bias):
    grid = jax.ShapeDtypeStruct((8, 48, C), BF16)
    dma = pltpu.SemaphoreType.DMA
    half = pltpu.VMEM((4, 48, C), BF16)
    scratch = [
        pltpu.VMEM((8, 48, C), BF16),
        pltpu.VMEM((8, 48, C), BF16),
        pltpu.VMEM((8, 48), jnp.int32),
        pltpu.VMEM((1, 6), jnp.int32),
        pltpu.VMEM((C, 3 * C), BF16),
        pltpu.VMEM((C, C), BF16),
        pltpu.VMEM((12, 64, 64), F32),
        half, half, pltpu.VMEM((8, 48), jnp.int32), half, half, half, half,
        pltpu.VMEM((C, C), F32),
        pltpu.VMEM((C, C), F32),
        pltpu.VMEM((C, C), F32),
        pltpu.VMEM((C, 128), F32),
        pltpu.VMEM((C, 128), F32),
        pltpu.VMEM((C, C), BF16),
        pltpu.VMEM((C, 3 * C), BF16),
        pltpu.VMEM((C, C), BF16),
        pltpu.VMEM((C, C), BF16),
        pltpu.VMEM((C, C), BF16),
        pltpu.VMEM((C, 3 * C), BF16),
        pltpu.VMEM((C, 768), F32),
        pltpu.VMEM((64, 768), F32),
        pltpu.VMEM((64, 768), F32),
        pltpu.VMEM((12, C, 128), F32),
        pltpu.VMEM((768, 128), F32),
        dma((7,)), dma((5,)), dma((5,)),
    ]
    for rows, count, na in PARTS:
        scratch += part_scratch(count, na)
    block_out, token_grad, red = pl.pallas_call(
        kernel,
        out_shape=[grid, grid, jax.ShapeDtypeStruct((40, 128), F32)],
        in_specs=[pl.BlockSpec(memory_space=pltpu.HBM)] * 7,
        out_specs=[pl.BlockSpec(memory_space=pltpu.VMEM)] * 3,
        scratch_shapes=scratch,
        compiler_params=pltpu.CompilerParams(
            collective_id=0, has_side_effects=True, vmem_limit_bytes=48 * 2**20
        ),
        cost_estimate=pl.CostEstimate(flops=15 * 10**8, bytes_accessed=5 * 10**6, transcendentals=300000),
        name="window_block",
    )(tokens, cotangent, ocean_mask, land_mask, w_qkv, w_proj, rel_bias)

    place = lax.rem(lax.axis_index("grp"), 4)
    outs = []
    for first, rows, size in ((0, 27, 864), (27, 9, 288), (36, 3, 96)):
        flat = red[first : first + rows].reshape(-1)
        outs.append(lax.dynamic_slice(flat, (place * size,), (size,)))
    return (block_out, token_grad, *outs)


def solution(mesh):
    split = ("band", "grp")
    placed = (
        P(split, None, None),
        P(split, None, None),
        P(split, None),
        P(split, None),
        P(),
        P(),
        P(),
    )
    return jax.shard_map(
        local,
        mesh=mesh,
        in_specs=placed,
        out_specs=(P(split, None, None), P(split, None, None), P(split), P(split), P(split)),
        check_vma=False,
    )
```

```python
import math

import jax
import jax.numpy as jnp
from jax import lax
from jax.experimental import pallas as pl
from jax.experimental.pallas import tpu as pltpu
from jax.sharding import PartitionSpec as P

EPS = 1e-05
MASKED = -1e30
C = 384
WB = 6
HG = 3
SCALE = 1.0 / math.sqrt(32)
F32 = jnp.float32
BF16 = jnp.bfloat16
MESH = pl.DeviceIdType.MESH

NY, NX, NZ = 8, 4, 8
OWN = 192
VMEM_BYTES = 62 * 2**20


def qkv_rows(g):
    return [("qkv", j, k) for j in range(3) for k in (g, 3 + g, 6 + g)]


PROJ_ROWS = [("proj", j, k) for j in range(3) for k in range(3)]
BIAS_ROWS = [("bias", j, 0) for j in range(3)]
PARTS = [
    (qkv_rows(0) + PROJ_ROWS[:7], 16, 16),
    (qkv_rows(1) + qkv_rows(2) + PROJ_ROWS[7:] + BIAS_ROWS, 24, 16),
]


def owned(g):
    qkv = [min(27 * g // 4 + i, 26) for i in range(8)]
    proj = [min(9 * g // 4 + i, 8) for i in range(3)]
    bias = [min(3 * g // 4 + i, 2) for i in range(2)]
    return (
        [("qkv", r // 9, r % 9) for r in qkv]
        + [("proj", r // 3, r % 3) for r in proj]
        + [("bias", r, 0) for r in bias]
    )


def carried(rows, g):
    need = owned(g)
    return [i for i, row in enumerate(rows) if row in need]


def dot_nt(a, b):
    return lax.dot_general(a, b, (((1,), (1,)), ((), ())), preferred_element_type=F32)


def dot_tn(a, b):
    return lax.dot_general(a, b, (((0,), (0,)), ((), ())), preferred_element_type=F32)


def dot_nn(a, b):
    return lax.dot_general(a, b, (((1,), (0,)), ((), ())), preferred_element_type=F32)


def stage_mask(ocean, land, half, mask_ref):
    place = lax.broadcasted_iota(jnp.int32, (8, 48), 0)
    column = lax.broadcasted_iota(jnp.int32, (8, 48), 1)
    for w in range(WB):
        live = 1.0 - land[:, w : w + 1]
        pick = (column == lax.rem(place + (8 * w + 4), 48)).astype(F32) * live
        for i in range(4):
            row = jnp.broadcast_to(ocean[i : i + 1, :], (8, 48))
            value = jnp.sum(row * pick, axis=1, keepdims=True)
            at = OWN * half + 32 * w + 8 * i
            mask_ref[at : at + 8, :] = jnp.broadcast_to(value, (8, 128))


def stage_rows(rows, half, out_ref):
    for i, row in enumerate(rows):
        rolled = pltpu.roll(row.astype(F32), 44, 0)
        for w in range(WB):
            at = OWN * half + 32 * w + 8 * i
            out_ref[at : at + 8, :] = rolled[8 * w : 8 * w + 8, :]


def grid_row(src_ref, half, i):
    ats = [OWN * half + 32 * w + 8 * i for w in range(WB)]
    return pltpu.roll(jnp.concatenate([src_ref[at : at + 8, :] for at in ats], 0), 4, 0)


class Part:
    def __init__(self, rows, count, along_y, refs, here, send, sources, red_ref):
        (
            self.pk, self.pack, self.r0, self.s1, self.ra, self.ta, self.ra2, self.rb, self.tb, self.rb2,
            self.f, self.r3, self.core_s, self.core_r, self.a1_s, self.a1_r, self.a2_s, self.a2_r,
            self.b1_s, self.b1_r, self.b2_s, self.b2_r, self.z_s, self.z_r,
        ) = refs
        self.rows, self.count, self.na = rows, count, along_y
        self.half = 2 * count
        self.nb = self.half - along_y
        self.here, self.send, self.sources, self.red = here, send, sources, red_ref
        self.sent = []

    def start(self):
        band, grp, y, x, z, core = self.here
        n = self.count
        grad_ref, bt_ref = self.sources
        lane = lax.broadcasted_iota(jnp.int32, (128, 128), 1)
        for i, (kind, j, k) in enumerate(self.rows):
            if kind == "bias":
                even = bt_ref[pl.ds(2 * j, 128, stride=6), :]
                odd = bt_ref[pl.ds(2 * j + 1, 128, stride=6), :]
                value = jnp.where(lane < 64, even, pltpu.roll(odd, 64, 1))
            else:
                at = k if kind == "qkv" else 9 + k
                value = grad_ref.at[at][pl.ds(j, 128, stride=3), :]
            self.pk[pl.ds(i, 128, stride=n), :] = value
        for i in range(len(self.rows), n):
            self.pk[pl.ds(i, 128, stride=n), :] = jnp.zeros((128, 128), F32)
        theirs = (1 - core) * self.half

        def narrow(i, carry):
            for j in range(NX):
                at = pl.multiple_of((i * NX + j) * 4 * n + theirs, 16)
                self.pack[i, j] = self.pk[pl.ds(at, self.half), :].astype(BF16)
            return carry

        lax.fori_loop(0, NY, narrow, 0)
        for i in range(8):
            self.f[i] = jnp.zeros((8, 128), F32)
        self.core_copy = self.send(
            self.pack, self.r0, self.core_s.at[0], self.core_r.at[0], (band, z * 2 + 1 - core)
        )

    def spread(self):
        band, grp, y, x, z, core = self.here
        n, na = self.count, self.na
        mine = core * self.half
        self.core_copy.wait()

        def add(i, carry):
            for j in range(NX):
                at = pl.multiple_of((i * NX + j) * 4 * n + mine, 16)
                total = self.pk[pl.ds(at, self.half), :] + self.r0[i, j].astype(F32)
                self.s1[i, j] = total.astype(BF16)
            return carry

        lax.fori_loop(0, NY, add, 0)
        self.b1, self.a1 = [], []
        for d in range(1, NX):
            to = lax.rem(x + d, NX)
            self.b1.append(
                self.send(
                    self.s1.at[:, to, pl.ds(na, self.nb), :], self.rb.at[d - 1],
                    self.b1_s.at[d - 1], self.b1_r.at[d - 1], (y * NX + to, grp),
                )
            )
        for d in range(1, NY):
            to = lax.rem(y + d, NY)
            self.a1.append(
                self.send(
                    self.s1.at[to, :, pl.ds(0, na), :], self.ra.at[d - 1],
                    self.a1_s.at[d - 1], self.a1_r.at[d - 1], (to * NX + x, grp),
                )
            )

    def turn(self):
        band, grp, y, x, z, core = self.here
        na = self.na
        total = self.s1[:, x, na : self.half, :].astype(F32)
        for d in range(1, NX):
            self.b1[d - 1].wait_recv()
            total = total + self.rb[d - 1].astype(F32)
        self.tb[...] = total.astype(BF16)
        self.b2, self.a2 = [], []
        for d in range(1, NY):
            to = lax.rem(y + d, NY)
            self.b2.append(
                self.send(
                    self.tb.at[to], self.rb2.at[d - 1],
                    self.b2_s.at[d - 1], self.b2_r.at[d - 1], (to * NX + x, grp),
                )
            )
        total = self.s1[y, :, 0:na, :].astype(F32)
        for d in range(1, NY):
            self.a1[d - 1].wait_recv()
            total = total + self.ra[d - 1].astype(F32)
        self.ta[...] = total.astype(BF16)
        for d in range(1, NX):
            to = lax.rem(x + d, NX)
            self.a2.append(
                self.send(
                    self.ta.at[to], self.ra2.at[d - 1],
                    self.a2_s.at[d - 1], self.a2_r.at[d - 1], (y * NX + to, grp),
                )
            )

    def last(self, i):
        band, grp, y, x, z, core = self.here
        quarter, zi, to_core = i // 4, (i // 2) % 2, i % 2
        to_z = 2 * (2 * core + quarter) + zi
        copy = pltpu.make_async_remote_copy(
            src_ref=self.f.at[i],
            dst_ref=self.r3.at[z],
            send_sem=self.z_s.at[i],
            recv_sem=self.z_r.at[z],
            device_id=(band, to_z * 2 + to_core),
            device_id_type=MESH,
        )
        return copy, jnp.logical_or(to_z != z, core != to_core)

    def share(self):
        band, grp, y, x, z, core = self.here
        n, na = self.count, self.na
        total = self.tb[y].astype(F32)
        for d in range(1, NY):
            self.b2[d - 1].wait_recv()
            total = total + self.rb2[d - 1].astype(F32)
        low = self.ta[x].astype(F32)
        for d in range(1, NX):
            self.a2[d - 1].wait_recv()
            low = low + self.ra2[d - 1].astype(F32)
        both = jnp.concatenate([low, total], 0)
        for i in range(8):
            for at, row in enumerate(carried(self.rows, i % 4)):
                first = n * (i // 4) + row
                self.f[i, at : at + 1, :] = both[first : first + 1, :]
        for i in range(8):
            copy, away = self.last(i)
            pl.when(away)(copy.start)

    def finish(self):
        band, grp, y, x, z, core = self.here
        own_core = z // 4
        for s in range(NZ):
            come = pltpu.make_async_remote_copy(
                src_ref=self.f.at[0],
                dst_ref=self.r3.at[s],
                send_sem=self.z_s.at[0],
                recv_sem=self.z_r.at[s],
                device_id=(band, z * 2 + 1 - core),
                device_id_type=MESH,
            )
            pl.when(jnp.logical_or(z != s, core != own_core))(come.wait_recv)

        @pl.when(core == own_core)
        def _():
            self.r3[z] = self.f[4 * lax.rem(z // 2, 2) + lax.rem(grp, 4)]

        total = self.r3[0]
        for s in range(1, NZ):
            total = total + self.r3[s]
        for g in range(4):
            kept = [self.rows[i] for i in carried(self.rows, g)]

            @pl.when(lax.rem(grp, 4) == g)
            def _(g=g, kept=kept):
                for at, row in enumerate(owned(g)):
                    if row in kept:
                        i = kept.index(row)
                        self.red[at : at + 1, :] = total[i : i + 1, :]

    def drain(self):
        for copy in self.a1 + self.a2 + self.b1 + self.b2:
            copy.wait_send()
        for i in range(8):
            copy, away = self.last(i)
            pl.when(away)(copy.wait_send)


def part_scratch(count, na):
    half = 2 * count
    nb = half - na
    dma = pltpu.SemaphoreType.DMA
    return [
        pltpu.VMEM((128 * count, 128), F32),
        pltpu.VMEM((NY, NX, half, 128), BF16),
        pltpu.VMEM((NY, NX, half, 128), BF16),
        pltpu.VMEM((NY, NX, half, 128), BF16),
        pltpu.VMEM((NY - 1, NX, na, 128), BF16),
        pltpu.VMEM((NX, na, 128), BF16),
        pltpu.VMEM((NX - 1, na, 128), BF16),
        pltpu.VMEM((NX - 1, NY, nb, 128), BF16),
        pltpu.VMEM((NY, nb, 128), BF16),
        pltpu.VMEM((NY - 1, nb, 128), BF16),
        pltpu.VMEM((8, 8, 128), F32),
        pltpu.VMEM((NZ, 8, 128), F32),
        dma((1,)), dma((1,)),
        dma((NY - 1,)), dma((NY - 1,)),
        dma((NX - 1,)), dma((NX - 1,)),
        dma((NX - 1,)), dma((NX - 1,)),
        dma((NY - 1,)), dma((NY - 1,)),
        dma((8,)), dma((NZ,)),
    ]


def kernel(
    tok_hbm, cot_hbm, oce_hbm, land_hbm, wqkv_hbm, wproj_hbm, rb_hbm,
    block_hbm, grad_hbm, red_hbm,
    block_ref, grad_out_ref, red_ref,
    tok_ref, cot_ref, oce_ref, land_ref, wqkv_ref, wproj_ref, rb_ref,
    htok_ref, hcot_ref, hoce_ref, uu_ref, ug_ref, hu_ref, hg_ref,
    x_ref, c_ref, n_ref, inv_ref, mask_ref, h_ref, qkv_ref, dz_ref, do_ref, o_ref, dqkv_ref,
    p_ref, bias_ref, db_ref, grad_ref, bt_ref, load_sem, store_sem, halo_s, halo_r, *rest,
):
    band = lax.axis_index("band")
    grp = lax.axis_index("grp")
    y, x = band // NX, lax.rem(band, NX)
    z, core = grp // 2, lax.rem(grp, 2)
    linear = band * 16 + grp
    after = lax.rem(linear + 1, 512)
    before = lax.rem(linear + 511, 512)
    after_id = (after // 16, lax.rem(after, 16))
    before_id = (before // 16, lax.rem(before, 16))

    loads = []
    for i, (src, dst) in enumerate(
        (
            (tok_hbm, tok_ref), (oce_hbm, oce_ref), (land_hbm, land_ref), (wqkv_hbm, wqkv_ref),
            (cot_hbm, cot_ref), (wproj_hbm, wproj_ref), (rb_hbm, rb_ref),
        )
    ):
        loads.append(pltpu.make_async_copy(src, dst, load_sem.at[i]))
        loads[-1].start()

    barrier = pltpu.get_barrier_semaphore()
    peers = [after_id, before_id]
    peers += [(band, lax.rem(grp + d, 16)) for d in range(1, 16)]
    peers += [(lax.rem(y + d, NY) * NX + x, grp) for d in range(1, NY)]
    peers += [(y * NX + lax.rem(x + d, NX), grp) for d in range(1, NX)]
    for peer in peers:
        pl.semaphore_signal(barrier, inc=1, device_id=peer, device_id_type=MESH)

    def send(src, dst, s, r, to):
        copy = pltpu.make_async_remote_copy(
            src_ref=src, dst_ref=dst, send_sem=s, recv_sem=r, device_id=to, device_id_type=MESH
        )
        copy.start()
        return copy

    kept = []

    def keep(src, dst):
        kept.append(pltpu.make_async_copy(src, dst, store_sem.at[len(kept)]))
        kept[-1].start()

    loads[0].wait()
    stage_rows([tok_ref[4 + i] for i in range(4)], 0, x_ref)

    pl.semaphore_wait(barrier, len(peers))
    halos = [
        send(tok_hbm.at[pl.ds(0, 4)], htok_ref, halo_s.at[0], halo_r.at[0], before_id),
        send(oce_hbm, hoce_ref, halo_s.at[1], halo_r.at[1], before_id),
        send(cot_hbm.at[pl.ds(0, 4)], hcot_ref, halo_s.at[2], halo_r.at[2], before_id),
    ]

    def norm(i, carry):
        rows = pl.ds(pl.multiple_of(i * 64, 64), 64)
        value = x_ref[rows, :]
        centered = value - jnp.mean(value, -1, keepdims=True)
        inv = lax.rsqrt(jnp.mean(centered * centered, -1, keepdims=True) + EPS)
        n = centered * inv
        n_ref[rows, :] = n
        inv_ref[rows, :] = jnp.broadcast_to(inv, (64, 128))
        h_ref[rows, :] = n.astype(BF16)
        return carry

    def project(half):
        rows = slice(OWN * half, OWN * half + OWN)
        qkv_ref[rows, :] = dot_nn(h_ref[rows, :], wqkv_ref[...]).astype(BF16)

    def pull(half):
        rows = slice(OWN * half, OWN * half + OWN)
        wide = jnp.concatenate([mask_ref[rows, :]] * 3, 1)
        dz_ref[rows, :] = (wide * c_ref[rows, :]).astype(BF16)
        do_ref[rows, :] = dot_nt(dz_ref[rows, :], wproj_ref[...]).astype(BF16)

    lax.fori_loop(0, 3, norm, 0)
    loads[1].wait()
    loads[2].wait()
    land = land_ref[...].astype(F32)
    stage_mask(oce_ref[4:8, :].astype(F32), land, 0, mask_ref)
    loads[3].wait()
    project(0)
    loads[4].wait()
    stage_rows([cot_ref[4 + i] for i in range(4)], 0, c_ref)
    loads[5].wait()
    pull(0)
    loads[6].wait()
    for i in range(6):
        pair = jnp.concatenate([rb_ref[2 * i], rb_ref[2 * i + 1]], 0)
        bias_ref[:, 128 * i : 128 * i + 128] = pair.T
    db_ref[...] = jnp.zeros_like(db_ref)

    here_lower = jnp.broadcast_to(linear, (48, C)) < 511
    halos[0].wait_recv()
    stage_rows([jnp.where(here_lower, htok_ref[i].astype(F32), 0.0) for i in range(4)], 1, x_ref)
    lax.fori_loop(3, 6, norm, 0)
    project(1)
    halos[1].wait_recv()
    ocean = jnp.where(jnp.broadcast_to(linear, (4, 48)) < 511, hoce_ref[0:4, :].astype(F32), 0.0)
    stage_mask(ocean, land, 1, mask_ref)

    head = lax.broadcasted_iota(jnp.int32, (64, 128), 1) // 32
    picks = [(head == i).astype(F32) for i in range(4)]
    picks_low = [p.astype(BF16) for p in picks]

    def spread(a):
        return jnp.concatenate([a * p for p in picks_low], 0)

    def fold(value):
        total = value[0:64] * picks[0]
        for i in range(1, 4):
            total = total + value[64 * i : 64 * i + 64] * picks[i]
        return total

    def two(w):
        first = pl.ds(pl.multiple_of(w * 32, 32), 32)
        second = pl.ds(pl.multiple_of(OWN + w * 32, 32), 32)
        return first, second

    def load(ref, w, lanes):
        first, second = two(w)
        return jnp.concatenate([ref[first, lanes], ref[second, lanes]], 0)

    def store(ref, w, lanes, value):
        first, second = two(w)
        ref[first, lanes] = value[0:32]
        ref[second, lanes] = value[32:64]

    def lanes_of(g):
        return [slice(C * i + 128 * g, C * i + 128 * g + 128) for i in range(3)] + [
            slice(256 * g, 256 * g + 256)
        ]

    def forward(w, carry):
        whole = pl.ds(pl.multiple_of(w * 64, 64), 64)
        live = jnp.concatenate([load(mask_ref, w, slice(0, 128))] * 2, 1) > 0.5
        for g in range(HG):
            q_lanes, k_lanes, v_lanes, wide = lanes_of(g)
            q4 = spread(load(qkv_ref, w, q_lanes))
            s = dot_nt(load(qkv_ref, w, k_lanes), q4) * SCALE + bias_ref[:, wide]
            s = jnp.where(live, s, MASKED)
            weights = jnp.exp(s - jnp.max(s, 0, keepdims=True))
            p = weights * (1.0 / jnp.sum(weights, 0, keepdims=True))
            p_ref[whole, wide] = p
            store(o_ref, w, q_lanes, fold(dot_tn(p.astype(BF16), load(qkv_ref, w, v_lanes))).astype(BF16))
        return carry

    def backward(g):
        q_lanes, k_lanes, v_lanes, wide = lanes_of(g)

        def step(w, carry):
            whole = pl.ds(pl.multiple_of(w * 64, 64), 64)
            q4 = spread(load(qkv_ref, w, q_lanes))
            do4 = spread(load(do_ref, w, q_lanes))
            p = p_ref[whole, wide]
            dp = dot_nt(load(qkv_ref, w, v_lanes), do4)
            store(dqkv_ref, w, v_lanes, dot_nn(p.astype(BF16), do4).astype(BF16))
            ds = p * (dp - jnp.sum(p * dp, 0, keepdims=True))
            db_ref[:, wide] += ds
            dsc = (ds * SCALE).astype(BF16)
            store(dqkv_ref, w, k_lanes, dot_nn(dsc, q4).astype(BF16))
            dq = fold(dot_tn(dsc, load(qkv_ref, w, k_lanes)))
            store(dqkv_ref, w, q_lanes, dq.astype(BF16))
            return carry

        lax.fori_loop(0, WB, step, 0, unroll=3)
        for k in (g, 3 + g, 6 + g):
            grad_ref[k] = dot_tn(h_ref[...], dqkv_ref[:, 128 * k : 128 * k + 128])

    lax.fori_loop(0, WB, forward, 0, unroll=2)

    halos[2].wait_recv()
    stage_rows([jnp.where(here_lower, hcot_ref[i].astype(F32), 0.0) for i in range(4)], 1, c_ref)
    pull(1)

    here = (band, grp, y, x, z, core)
    parts = []
    at = 0
    for rows, count, na in PARTS:
        parts.append(Part(rows, count, na, rest[at : at + 24], here, send, (grad_ref, bt_ref), red_ref))
        at += 24
    first, second = parts

    for k in range(3):
        grad_ref[9 + k] = dot_tn(o_ref[...], dz_ref[:, 128 * k : 128 * k + 128])
    backward(0)
    first.start()
    backward(1)
    first.spread()
    backward(2)
    for i in range(6):
        bt_ref[128 * i : 128 * i + 128, 0:64] = db_ref[:, 128 * i : 128 * i + 128].T
    second.start()
    first.turn()

    wide_mask = jnp.concatenate([mask_ref[...]] * 3, 1)
    x_ref[...] = wide_mask * dot_nn(o_ref[...], wproj_ref[...])
    for i in range(4):
        uu_ref[i] = grid_row(x_ref, 1, i).astype(BF16)
    second.spread()
    halo_u = send(uu_ref, hu_ref, halo_s.at[3], halo_r.at[3], after_id)
    c_ref[...] = dot_nt(dqkv_ref[...], wqkv_ref[...])

    def back(i, carry):
        rows = pl.ds(pl.multiple_of(i * 64, 64), 64)
        dh = c_ref[rows, :]
        n = n_ref[rows, :]
        inv = jnp.concatenate([inv_ref[rows, :]] * 3, 1)
        slope = jnp.mean(dh * n, -1, keepdims=True)
        c_ref[rows, :] = inv * (dh - jnp.mean(dh, -1, keepdims=True) - n * slope)
        return carry

    lax.fori_loop(0, WB, back, 0)
    for i in range(4):
        ug_ref[i] = grid_row(c_ref, 1, i).astype(BF16)
    halo_g = send(ug_ref, hg_ref, halo_s.at[4], halo_r.at[4], after_id)
    first.share()
    second.turn()
    for i in range(4):
        row = grid_row(x_ref, 0, i).astype(BF16).astype(F32)
        block_ref[4 + i] = (tok_ref[4 + i].astype(F32) + row).astype(BF16)
        row = grid_row(c_ref, 0, i).astype(BF16).astype(F32)
        grad_out_ref[4 + i] = (cot_ref[4 + i].astype(F32) + row).astype(BF16)
    upper, lower = pl.ds(4, 4), pl.ds(0, 4)
    keep(block_ref.at[upper], block_hbm.at[upper])
    keep(grad_out_ref.at[upper], grad_hbm.at[upper])
    second.share()
    inner = jnp.broadcast_to(linear, (4, 48, C)) > 0
    halo_u.wait_recv()
    low = jnp.where(inner, hu_ref[...].astype(F32), 0.0)
    block_ref[0:4] = (tok_ref[0:4].astype(F32) + low).astype(BF16)
    keep(block_ref.at[lower], block_hbm.at[lower])
    halo_g.wait_recv()
    low = jnp.where(inner, hg_ref[...].astype(F32), 0.0)
    grad_out_ref[0:4] = (cot_ref[0:4].astype(F32) + low).astype(BF16)
    keep(grad_out_ref.at[lower], grad_hbm.at[lower])
    first.finish()
    red_ref[13:16, :] = jnp.zeros((3, 128), F32)
    second.finish()
    keep(red_ref, red_hbm)
    for copy in halos + [halo_u, halo_g]:
        copy.wait_send()
    first.drain()
    second.drain()
    for copy in kept:
        copy.wait()


def place_kernel(
    block_ref, grad_ref, red_hbm, block_out, grad_out, qkv_out, proj_out, bias_out, red_ref, sem
):
    load = pltpu.make_async_copy(red_hbm, red_ref, sem.at[2])
    load.start()
    copies = [
        pltpu.make_async_copy(block_ref, block_out, sem.at[0]),
        pltpu.make_async_copy(grad_ref, grad_out, sem.at[1]),
    ]
    for copy in copies:
        copy.start()
    g = lax.rem(lax.axis_index("grp"), 4)
    lane = lax.broadcasted_iota(jnp.int32, (16, 128), 1)
    load.wait()
    red = red_ref[...]
    following = jnp.concatenate([red[1:16], red[0:1]], 0)
    rolled = [red]
    for quarter in range(1, 4):
        shift = 128 - 32 * quarter
        value = jnp.where(lane < shift, pltpu.roll(red, shift, 1), pltpu.roll(following, shift, 1))
        rolled.append(value)

    def pick(step):
        which = jnp.broadcast_to(lax.rem(step * g, 4), (16, 128))
        value = rolled[0]
        for quarter in range(1, 4):
            value = jnp.where(which == quarter, rolled[quarter], value)
        return value

    for out, step, first, size in ((qkv_out, 27, 0, 864), (proj_out, 9, 8, 288), (bias_out, 3, 11, 96)):
        value = pick(step)
        for i in range(-(-size // 128)):
            n = min(128, size - 128 * i)
            out[pl.ds(128 * i, n)] = value[first + i, 0:n]
    for copy in copies:
        copy.wait()


def local(tokens, cotangent, ocean_mask, land_mask, w_qkv, w_proj, rel_bias):
    grid = jax.ShapeDtypeStruct((8, 48, C), BF16)
    dma = pltpu.SemaphoreType.DMA
    half = pltpu.VMEM((4, 48, C), BF16)
    scratch = [
        pltpu.VMEM((8, 48, C), BF16),
        pltpu.VMEM((8, 48, C), BF16),
        pltpu.VMEM((16, 128), F32),
        pltpu.VMEM((8, 48, C), BF16),
        pltpu.VMEM((8, 48, C), BF16),
        pltpu.VMEM((8, 48), jnp.int32),
        pltpu.VMEM((1, 6), jnp.int32),
        pltpu.VMEM((C, 3 * C), BF16),
        pltpu.VMEM((C, C), BF16),
        pltpu.VMEM((12, 64, 64), F32),
        half, half, pltpu.VMEM((8, 48), jnp.int32), half, half, half, half,
        pltpu.VMEM((C, C), F32),
        pltpu.VMEM((C, C), F32),
        pltpu.VMEM((C, C), F32),
        pltpu.VMEM((C, 128), F32),
        pltpu.VMEM((C, 128), F32),
        pltpu.VMEM((C, C), BF16),
        pltpu.VMEM((C, 3 * C), BF16),
        pltpu.VMEM((C, C), BF16),
        pltpu.VMEM((C, C), BF16),
        pltpu.VMEM((C, C), BF16),
        pltpu.VMEM((C, 3 * C), BF16),
        pltpu.VMEM((C, 768), F32),
        pltpu.VMEM((64, 768), F32),
        pltpu.VMEM((64, 768), F32),
        pltpu.VMEM((12, C, 128), F32),
        pltpu.VMEM((768, 128), F32),
        dma((7,)), dma((5,)), dma((5,)), dma((5,)),
    ]
    for rows, count, na in PARTS:
        scratch += part_scratch(count, na)
    block_out, token_grad, red = pl.pallas_call(
        kernel,
        out_shape=[grid, grid, jax.ShapeDtypeStruct((16, 128), F32)],
        in_specs=[pl.BlockSpec(memory_space=pltpu.HBM)] * 7,
        out_specs=[pl.BlockSpec(memory_space=pltpu.HBM)] * 3,
        scratch_shapes=scratch,
        compiler_params=pltpu.CompilerParams(
            collective_id=0, has_side_effects=True, vmem_limit_bytes=VMEM_BYTES
        ),
        cost_estimate=pl.CostEstimate(flops=15 * 10**8, bytes_accessed=5 * 10**6, transcendentals=300000),
        name="window_block",
    )(tokens, cotangent, ocean_mask, land_mask, w_qkv, w_proj, rel_bias)

    whole = pl.BlockSpec(memory_space=pltpu.VMEM)
    hbm = pl.BlockSpec(memory_space=pltpu.HBM)
    return tuple(
        pl.pallas_call(
            place_kernel,
            out_shape=[grid, grid] + [jax.ShapeDtypeStruct((n,), F32) for n in (864, 288, 96)],
            in_specs=[hbm] * 3,
            out_specs=[hbm, hbm, whole, whole, whole],
            scratch_shapes=[pltpu.VMEM((16, 128), F32), dma((3,))],
            compiler_params=pltpu.CompilerParams(vmem_limit_bytes=VMEM_BYTES),
            cost_estimate=pl.CostEstimate(flops=10**4, bytes_accessed=12 * 10**5, transcendentals=0),
            name="outputs",
        )(block_out, token_grad, red)
    )


def solution(mesh):
    split = ("band", "grp")
    placed = (
        P(split, None, None),
        P(split, None, None),
        P(split, None),
        P(split, None),
        P(),
        P(),
        P(),
    )
    return jax.shard_map(
        local,
        mesh=mesh,
        in_specs=placed,
        out_specs=(P(split, None, None), P(split, None, None), P(split), P(split), P(split)),
        check_vma=False,
    )
```

```python
import math

import jax
import jax.numpy as jnp
from jax import lax
from jax.experimental import pallas as pl
from jax.experimental.pallas import tpu as pltpu
from jax.sharding import PartitionSpec as P

EPS = 1e-05
MASKED = -1e30
C = 384
WB = 6
HG = 3
SCALE = 1.0 / math.sqrt(32)
F32 = jnp.float32
BF16 = jnp.bfloat16
MESH = pl.DeviceIdType.MESH

NY, NX, NZ = 8, 4, 8
OWN = 192
VMEM_BYTES = 62 * 2**20


def qkv_rows(g):
    return [("qkv", j, k) for j in range(3) for k in (g, 3 + g, 6 + g)]


PROJ_ROWS = [("proj", j, k) for j in range(3) for k in range(3)]
BIAS_ROWS = [("bias", j, 0) for j in range(3)]
PARTS = [
    (qkv_rows(0) + PROJ_ROWS[:7], 16, 16),
    (qkv_rows(1) + qkv_rows(2) + PROJ_ROWS[7:] + BIAS_ROWS, 24, 16),
]


def owned(g):
    qkv = [min(27 * g // 4 + i, 26) for i in range(8)]
    proj = [min(9 * g // 4 + i, 8) for i in range(3)]
    bias = [min(3 * g // 4 + i, 2) for i in range(2)]
    return (
        [("qkv", r // 9, r % 9) for r in qkv]
        + [("proj", r // 3, r % 3) for r in proj]
        + [("bias", r, 0) for r in bias]
    )


def carried(rows, g):
    need = owned(g)
    return [i for i, row in enumerate(rows) if row in need]


def dot_nt(a, b):
    return lax.dot_general(a, b, (((1,), (1,)), ((), ())), preferred_element_type=F32)


def dot_tn(a, b):
    return lax.dot_general(a, b, (((0,), (0,)), ((), ())), preferred_element_type=F32)


def dot_nn(a, b):
    return lax.dot_general(a, b, (((1,), (0,)), ((), ())), preferred_element_type=F32)


def stage_mask(ocean, land, half, mask_ref):
    place = lax.broadcasted_iota(jnp.int32, (8, 48), 0)
    column = lax.broadcasted_iota(jnp.int32, (8, 48), 1)
    for w in range(WB):
        live = 1.0 - land[:, w : w + 1]
        pick = (column == lax.rem(place + (8 * w + 4), 48)).astype(F32) * live
        for i in range(4):
            row = jnp.broadcast_to(ocean[i : i + 1, :], (8, 48))
            value = jnp.sum(row * pick, axis=1, keepdims=True)
            at = OWN * half + 32 * w + 8 * i
            mask_ref[at : at + 8, :] = jnp.broadcast_to(value, (8, 128))


def stage_rows(rows, half, out_ref):
    for i, row in enumerate(rows):
        rolled = pltpu.roll(row.astype(F32), 44, 0)
        for w in range(WB):
            at = OWN * half + 32 * w + 8 * i
            out_ref[at : at + 8, :] = rolled[8 * w : 8 * w + 8, :]


def grid_row(src_ref, half, i):
    ats = [OWN * half + 32 * w + 8 * i for w in range(WB)]
    return pltpu.roll(jnp.concatenate([src_ref[at : at + 8, :] for at in ats], 0), 4, 0)


class Part:
    def __init__(self, rows, count, along_y, refs, here, send, sources, red_ref):
        (
            self.pk, self.pack, self.r0, self.s1, self.ra, self.ta, self.ra2, self.rb, self.tb, self.rb2,
            self.f, self.r3, self.core_s, self.core_r, self.a1_s, self.a1_r, self.a2_s, self.a2_r,
            self.b1_s, self.b1_r, self.b2_s, self.b2_r, self.z_s, self.z_r,
        ) = refs
        self.rows, self.count, self.na = rows, count, along_y
        self.half = 2 * count
        self.nb = self.half - along_y
        self.here, self.send, self.sources, self.red = here, send, sources, red_ref
        self.sent = []

    def start(self):
        band, grp, y, x, z, core = self.here
        n = self.count
        grad_ref, bt_ref = self.sources
        lane = lax.broadcasted_iota(jnp.int32, (128, 128), 1)
        for i, (kind, j, k) in enumerate(self.rows):
            if kind == "bias":
                even = bt_ref[pl.ds(2 * j, 128, stride=6), :]
                odd = bt_ref[pl.ds(2 * j + 1, 128, stride=6), :]
                value = jnp.where(lane < 64, even, pltpu.roll(odd, 64, 1))
            else:
                at = k if kind == "qkv" else 9 + k
                value = grad_ref.at[at][pl.ds(j, 128, stride=3), :]
            self.pk[pl.ds(i, 128, stride=n), :] = value
        for i in range(len(self.rows), n):
            self.pk[pl.ds(i, 128, stride=n), :] = jnp.zeros((128, 128), F32)
        theirs = (1 - core) * self.half

        def narrow(i, carry):
            for j in range(NX):
                at = pl.multiple_of((i * NX + j) * 4 * n + theirs, 16)
                self.pack[i, j] = self.pk[pl.ds(at, self.half), :].astype(BF16)
            return carry

        lax.fori_loop(0, NY, narrow, 0)
        for i in range(8):
            self.f[i] = jnp.zeros((8, 128), F32)
        self.core_copy = self.send(
            self.pack, self.r0, self.core_s.at[0], self.core_r.at[0], (band, z * 2 + 1 - core)
        )

    def spread(self):
        band, grp, y, x, z, core = self.here
        n, na = self.count, self.na
        mine = core * self.half
        self.core_copy.wait()

        def add(i, carry):
            for j in range(NX):
                at = pl.multiple_of((i * NX + j) * 4 * n + mine, 16)
                total = self.pk[pl.ds(at, self.half), :] + self.r0[i, j].astype(F32)
                self.s1[i, j] = total.astype(BF16)
            return carry

        lax.fori_loop(0, NY, add, 0)
        self.b1, self.a1 = [], []
        for d in range(1, NX):
            to = lax.rem(x + d, NX)
            self.b1.append(
                self.send(
                    self.s1.at[:, to, pl.ds(na, self.nb), :], self.rb.at[d - 1],
                    self.b1_s.at[d - 1], self.b1_r.at[d - 1], (y * NX + to, grp),
                )
            )
        for d in range(1, NY):
            to = lax.rem(y + d, NY)
            self.a1.append(
                self.send(
                    self.s1.at[to, :, pl.ds(0, na), :], self.ra.at[d - 1],
                    self.a1_s.at[d - 1], self.a1_r.at[d - 1], (to * NX + x, grp),
                )
            )

    def turn(self):
        band, grp, y, x, z, core = self.here
        na = self.na
        total = self.s1[:, x, na : self.half, :].astype(F32)
        for d in range(1, NX):
            self.b1[d - 1].wait_recv()
            total = total + self.rb[d - 1].astype(F32)
        self.tb[...] = total.astype(BF16)
        self.b2, self.a2 = [], []
        for d in range(1, NY):
            to = lax.rem(y + d, NY)
            self.b2.append(
                self.send(
                    self.tb.at[to], self.rb2.at[d - 1],
                    self.b2_s.at[d - 1], self.b2_r.at[d - 1], (to * NX + x, grp),
                )
            )
        total = self.s1[y, :, 0:na, :].astype(F32)
        for d in range(1, NY):
            self.a1[d - 1].wait_recv()
            total = total + self.ra[d - 1].astype(F32)
        self.ta[...] = total.astype(BF16)
        for d in range(1, NX):
            to = lax.rem(x + d, NX)
            self.a2.append(
                self.send(
                    self.ta.at[to], self.ra2.at[d - 1],
                    self.a2_s.at[d - 1], self.a2_r.at[d - 1], (y * NX + to, grp),
                )
            )

    def last(self, i):
        band, grp, y, x, z, core = self.here
        quarter, zi, to_core = i // 4, (i // 2) % 2, i % 2
        to_z = 2 * (2 * core + quarter) + zi
        copy = pltpu.make_async_remote_copy(
            src_ref=self.f.at[i],
            dst_ref=self.r3.at[z],
            send_sem=self.z_s.at[i],
            recv_sem=self.z_r.at[z],
            device_id=(band, to_z * 2 + to_core),
            device_id_type=MESH,
        )
        return copy, jnp.logical_or(to_z != z, core != to_core)

    def share(self):
        band, grp, y, x, z, core = self.here
        n, na = self.count, self.na
        total = self.tb[y].astype(F32)
        for d in range(1, NY):
            self.b2[d - 1].wait_recv()
            total = total + self.rb2[d - 1].astype(F32)
        low = self.ta[x].astype(F32)
        for d in range(1, NX):
            self.a2[d - 1].wait_recv()
            low = low + self.ra2[d - 1].astype(F32)
        both = jnp.concatenate([low, total], 0)
        for i in range(8):
            for at, row in enumerate(carried(self.rows, i % 4)):
                first = n * (i // 4) + row
                self.f[i, at : at + 1, :] = both[first : first + 1, :]
        for i in range(8):
            copy, away = self.last(i)
            pl.when(away)(copy.start)

    def finish(self):
        band, grp, y, x, z, core = self.here
        own_core = z // 4
        for s in range(NZ):
            come = pltpu.make_async_remote_copy(
                src_ref=self.f.at[0],
                dst_ref=self.r3.at[s],
                send_sem=self.z_s.at[0],
                recv_sem=self.z_r.at[s],
                device_id=(band, z * 2 + 1 - core),
                device_id_type=MESH,
            )
            pl.when(jnp.logical_or(z != s, core != own_core))(come.wait_recv)

        @pl.when(core == own_core)
        def _():
            self.r3[z] = self.f[4 * lax.rem(z // 2, 2) + lax.rem(grp, 4)]

        total = self.r3[0]
        for s in range(1, NZ):
            total = total + self.r3[s]
        for g in range(4):
            kept = [self.rows[i] for i in carried(self.rows, g)]

            @pl.when(lax.rem(grp, 4) == g)
            def _(g=g, kept=kept):
                for at, row in enumerate(owned(g)):
                    if row in kept:
                        i = kept.index(row)
                        self.red[at : at + 1, :] = total[i : i + 1, :]

    def drain(self):
        for copy in self.a1 + self.a2 + self.b1 + self.b2:
            copy.wait_send()
        for i in range(8):
            copy, away = self.last(i)
            pl.when(away)(copy.wait_send)


def part_scratch(count, na):
    half = 2 * count
    nb = half - na
    dma = pltpu.SemaphoreType.DMA
    return [
        pltpu.VMEM((128 * count, 128), F32),
        pltpu.VMEM((NY, NX, half, 128), BF16),
        pltpu.VMEM((NY, NX, half, 128), BF16),
        pltpu.VMEM((NY, NX, half, 128), BF16),
        pltpu.VMEM((NY - 1, NX, na, 128), BF16),
        pltpu.VMEM((NX, na, 128), BF16),
        pltpu.VMEM((NX - 1, na, 128), BF16),
        pltpu.VMEM((NX - 1, NY, nb, 128), BF16),
        pltpu.VMEM((NY, nb, 128), BF16),
        pltpu.VMEM((NY - 1, nb, 128), BF16),
        pltpu.VMEM((8, 8, 128), F32),
        pltpu.VMEM((NZ, 8, 128), F32),
        dma((1,)), dma((1,)),
        dma((NY - 1,)), dma((NY - 1,)),
        dma((NX - 1,)), dma((NX - 1,)),
        dma((NX - 1,)), dma((NX - 1,)),
        dma((NY - 1,)), dma((NY - 1,)),
        dma((8,)), dma((NZ,)),
    ]


def kernel(
    tok_hbm, cot_hbm, oce_hbm, land_hbm, wqkv_hbm, wproj_hbm, rb_hbm,
    block_hbm, grad_hbm, red_hbm,
    block_ref, grad_out_ref, red_ref,
    tok_ref, cot_ref, oce_ref, land_ref, wqkv_ref, wproj_ref, rb_ref,
    htok_ref, hcot_ref, hoce_ref, uu_ref, ug_ref, hu_ref, hg_ref,
    x_ref, c_ref, n_ref, inv_ref, mask_ref, h_ref, ht_ref, qkv_ref, dz_ref, do_ref, o_ref, dqkv_ref,
    p_ref, bias_ref, db_ref, grad_ref, bt_ref, load_sem, store_sem, halo_s, halo_r, *rest,
):
    band = lax.axis_index("band")
    grp = lax.axis_index("grp")
    y, x = band // NX, lax.rem(band, NX)
    z, core = grp // 2, lax.rem(grp, 2)
    linear = band * 16 + grp
    after = lax.rem(linear + 1, 512)
    before = lax.rem(linear + 511, 512)
    after_id = (after // 16, lax.rem(after, 16))
    before_id = (before // 16, lax.rem(before, 16))

    loads = []
    for i, (src, dst) in enumerate(
        (
            (tok_hbm, tok_ref), (oce_hbm, oce_ref), (land_hbm, land_ref), (wqkv_hbm, wqkv_ref),
            (cot_hbm, cot_ref), (wproj_hbm, wproj_ref), (rb_hbm, rb_ref),
        )
    ):
        loads.append(pltpu.make_async_copy(src, dst, load_sem.at[i]))
        loads[-1].start()

    barrier = pltpu.get_barrier_semaphore()
    peers = [after_id, before_id]
    peers += [(band, lax.rem(grp + d, 16)) for d in range(1, 16)]
    peers += [(lax.rem(y + d, NY) * NX + x, grp) for d in range(1, NY)]
    peers += [(y * NX + lax.rem(x + d, NX), grp) for d in range(1, NX)]
    for peer in peers:
        pl.semaphore_signal(barrier, inc=1, device_id=peer, device_id_type=MESH)

    def send(src, dst, s, r, to):
        copy = pltpu.make_async_remote_copy(
            src_ref=src, dst_ref=dst, send_sem=s, recv_sem=r, device_id=to, device_id_type=MESH
        )
        copy.start()
        return copy

    kept = []

    def keep(src, dst):
        kept.append(pltpu.make_async_copy(src, dst, store_sem.at[len(kept)]))
        kept[-1].start()

    loads[0].wait()
    stage_rows([tok_ref[4 + i] for i in range(4)], 0, x_ref)

    pl.semaphore_wait(barrier, len(peers))
    halos = [
        send(tok_hbm.at[pl.ds(0, 4)], htok_ref, halo_s.at[0], halo_r.at[0], before_id),
        send(oce_hbm, hoce_ref, halo_s.at[1], halo_r.at[1], before_id),
        send(cot_hbm.at[pl.ds(0, 4)], hcot_ref, halo_s.at[2], halo_r.at[2], before_id),
    ]

    def norm(i, carry):
        rows = pl.ds(pl.multiple_of(i * 64, 64), 64)
        value = x_ref[rows, :]
        centered = value - jnp.mean(value, -1, keepdims=True)
        inv = lax.rsqrt(jnp.mean(centered * centered, -1, keepdims=True) + EPS)
        n = centered * inv
        n_ref[rows, :] = n
        inv_ref[rows, :] = jnp.broadcast_to(inv, (64, 128))
        h_ref[rows, :] = n.astype(BF16)
        return carry

    def project(half):
        rows = slice(OWN * half, OWN * half + OWN)
        qkv_ref[rows, :] = dot_nn(h_ref[rows, :], wqkv_ref[...]).astype(BF16)

    def pull(half):
        rows = slice(OWN * half, OWN * half + OWN)
        wide = jnp.concatenate([mask_ref[rows, :]] * 3, 1)
        dz_ref[rows, :] = (wide * c_ref[rows, :]).astype(BF16)
        do_ref[rows, :] = dot_nt(dz_ref[rows, :], wproj_ref[...]).astype(BF16)

    lax.fori_loop(0, 3, norm, 0, unroll=3)
    loads[1].wait()
    loads[2].wait()
    land = land_ref[...].astype(F32)
    stage_mask(oce_ref[4:8, :].astype(F32), land, 0, mask_ref)
    loads[3].wait()
    project(0)
    loads[4].wait()
    stage_rows([cot_ref[4 + i] for i in range(4)], 0, c_ref)
    loads[5].wait()
    pull(0)
    loads[6].wait()
    for i in range(6):
        pair = jnp.concatenate([rb_ref[2 * i], rb_ref[2 * i + 1]], 0)
        bias_ref[:, 128 * i : 128 * i + 128] = pair.T
    db_ref[...] = jnp.zeros_like(db_ref)

    here_lower = jnp.broadcast_to(linear, (48, C)) < 511
    halos[0].wait_recv()
    stage_rows([jnp.where(here_lower, htok_ref[i].astype(F32), 0.0) for i in range(4)], 1, x_ref)
    lax.fori_loop(3, 6, norm, 0, unroll=3)
    project(1)
    ht_ref[...] = h_ref[...].T
    halos[1].wait_recv()
    ocean = jnp.where(jnp.broadcast_to(linear, (4, 48)) < 511, hoce_ref[0:4, :].astype(F32), 0.0)
    stage_mask(ocean, land, 1, mask_ref)

    head = lax.broadcasted_iota(jnp.int32, (64, 128), 1) // 32
    picks = [(head == i).astype(F32) for i in range(4)]
    picks_low = [p.astype(BF16) for p in picks]

    def spread(a):
        return jnp.concatenate([a * p for p in picks_low], 0)

    def fold(value):
        total = value[0:64] * picks[0]
        for i in range(1, 4):
            total = total + value[64 * i : 64 * i + 64] * picks[i]
        return total

    def two(w):
        first = pl.ds(pl.multiple_of(w * 32, 32), 32)
        second = pl.ds(pl.multiple_of(OWN + w * 32, 32), 32)
        return first, second

    def load(ref, w, lanes):
        first, second = two(w)
        return jnp.concatenate([ref[first, lanes], ref[second, lanes]], 0)

    def store(ref, w, lanes, value):
        first, second = two(w)
        ref[first, lanes] = value[0:32]
        ref[second, lanes] = value[32:64]

    def lanes_of(g):
        return [slice(C * i + 128 * g, C * i + 128 * g + 128) for i in range(3)] + [
            slice(256 * g, 256 * g + 256)
        ]

    def forward(w, carry):
        whole = pl.ds(pl.multiple_of(w * 64, 64), 64)
        live = jnp.concatenate([load(mask_ref, w, slice(0, 128))] * 2, 1) > 0.5
        for g in range(HG):
            q_lanes, k_lanes, v_lanes, wide = lanes_of(g)
            q4 = spread(load(qkv_ref, w, q_lanes))
            s = dot_nt(load(qkv_ref, w, k_lanes), q4) * SCALE + bias_ref[:, wide]
            s = jnp.where(live, s, MASKED)
            weights = jnp.exp(s - jnp.max(s, 0, keepdims=True))
            p = weights * (1.0 / jnp.sum(weights, 0, keepdims=True))
            p_ref[whole, wide] = p
            store(o_ref, w, q_lanes, fold(dot_tn(p.astype(BF16), load(qkv_ref, w, v_lanes))).astype(BF16))
        return carry

    def backward(g):
        q_lanes, k_lanes, v_lanes, wide = lanes_of(g)

        def step(w, carry):
            whole = pl.ds(pl.multiple_of(w * 64, 64), 64)
            q4 = spread(load(qkv_ref, w, q_lanes))
            do4 = spread(load(do_ref, w, q_lanes))
            p = p_ref[whole, wide]
            dp = dot_nt(load(qkv_ref, w, v_lanes), do4)
            store(dqkv_ref, w, v_lanes, dot_nn(p.astype(BF16), do4).astype(BF16))
            ds = p * (dp - jnp.sum(p * dp, 0, keepdims=True))
            db_ref[:, wide] += ds
            dsc = (ds * SCALE).astype(BF16)
            store(dqkv_ref, w, k_lanes, dot_nn(dsc, q4).astype(BF16))
            dq = fold(dot_tn(dsc, load(qkv_ref, w, k_lanes)))
            store(dqkv_ref, w, q_lanes, dq.astype(BF16))
            return carry

        lax.fori_loop(0, WB, step, 0, unroll=6)
        for k in (g, 3 + g, 6 + g):
            grad_ref[k] = dot_nn(ht_ref[...], dqkv_ref[:, 128 * k : 128 * k + 128])

    lax.fori_loop(0, WB, forward, 0, unroll=2)

    halos[2].wait_recv()
    stage_rows([jnp.where(here_lower, hcot_ref[i].astype(F32), 0.0) for i in range(4)], 1, c_ref)
    pull(1)

    here = (band, grp, y, x, z, core)
    parts = []
    at = 0
    for rows, count, na in PARTS:
        parts.append(Part(rows, count, na, rest[at : at + 24], here, send, (grad_ref, bt_ref), red_ref))
        at += 24
    first, second = parts

    proj = dot_tn(o_ref[...], dz_ref[...])
    for k in range(3):
        grad_ref[9 + k] = proj[:, 128 * k : 128 * k + 128]
    backward(0)
    first.start()
    backward(1)
    first.spread()
    backward(2)
    for i in range(6):
        bt_ref[128 * i : 128 * i + 128, 0:64] = db_ref[:, 128 * i : 128 * i + 128].T
    second.start()
    first.turn()

    wide_mask = jnp.concatenate([mask_ref[...]] * 3, 1)
    x_ref[...] = wide_mask * dot_nn(o_ref[...], wproj_ref[...])
    for i in range(4):
        uu_ref[i] = grid_row(x_ref, 1, i).astype(BF16)
    second.spread()
    halo_u = send(uu_ref, hu_ref, halo_s.at[3], halo_r.at[3], after_id)
    c_ref[...] = dot_nt(dqkv_ref[...], wqkv_ref[...])

    def back(i, carry):
        rows = pl.ds(pl.multiple_of(i * 64, 64), 64)
        dh = c_ref[rows, :]
        n = n_ref[rows, :]
        inv = jnp.concatenate([inv_ref[rows, :]] * 3, 1)
        slope = jnp.mean(dh * n, -1, keepdims=True)
        c_ref[rows, :] = inv * (dh - jnp.mean(dh, -1, keepdims=True) - n * slope)
        return carry

    lax.fori_loop(0, WB, back, 0, unroll=3)
    for i in range(4):
        ug_ref[i] = grid_row(c_ref, 1, i).astype(BF16)
    halo_g = send(ug_ref, hg_ref, halo_s.at[4], halo_r.at[4], after_id)
    first.share()
    second.turn()
    for i in range(4):
        row = grid_row(x_ref, 0, i).astype(BF16).astype(F32)
        block_ref[4 + i] = (tok_ref[4 + i].astype(F32) + row).astype(BF16)
        row = grid_row(c_ref, 0, i).astype(BF16).astype(F32)
        grad_out_ref[4 + i] = (cot_ref[4 + i].astype(F32) + row).astype(BF16)
    upper, lower = pl.ds(4, 4), pl.ds(0, 4)
    keep(block_ref.at[upper], block_hbm.at[upper])
    keep(grad_out_ref.at[upper], grad_hbm.at[upper])
    second.share()
    inner = jnp.broadcast_to(linear, (4, 48, C)) > 0
    halo_u.wait_recv()
    low = jnp.where(inner, hu_ref[...].astype(F32), 0.0)
    block_ref[0:4] = (tok_ref[0:4].astype(F32) + low).astype(BF16)
    keep(block_ref.at[lower], block_hbm.at[lower])
    halo_g.wait_recv()
    low = jnp.where(inner, hg_ref[...].astype(F32), 0.0)
    grad_out_ref[0:4] = (cot_ref[0:4].astype(F32) + low).astype(BF16)
    keep(grad_out_ref.at[lower], grad_hbm.at[lower])
    first.finish()
    red_ref[13:16, :] = jnp.zeros((3, 128), F32)
    second.finish()
    keep(red_ref, red_hbm)
    for copy in halos + [halo_u, halo_g]:
        copy.wait_send()
    first.drain()
    second.drain()
    for copy in kept:
        copy.wait()


def place_kernel(
    block_hbm, grad_hbm, red_hbm, block_out, grad_out, qkv_out, proj_out, bias_out,
    block_ref, grad_ref, red_ref, in_sem, out_sem,
):
    load = pltpu.make_async_copy(red_hbm, red_ref, in_sem.at[4])
    load.start()
    moves = []
    for i, (src, via, dst) in enumerate(((block_hbm, block_ref, block_out), (grad_hbm, grad_ref, grad_out))):
        for j in range(2):
            part = pl.ds(4 * j, 4)
            into = pltpu.make_async_copy(src.at[part], via.at[part], in_sem.at[2 * i + j])
            into.start()
            moves.append((into, pltpu.make_async_copy(via.at[part], dst.at[part], out_sem.at[2 * i + j])))
    load.wait()
    for into, out in moves:
        into.wait()
        out.start()
    g = lax.rem(lax.axis_index("grp"), 4)
    lane = lax.broadcasted_iota(jnp.int32, (16, 128), 1)
    red = red_ref[...]
    following = jnp.concatenate([red[1:16], red[0:1]], 0)
    rolled = [red]
    for quarter in range(1, 4):
        shift = 128 - 32 * quarter
        value = jnp.where(lane < shift, pltpu.roll(red, shift, 1), pltpu.roll(following, shift, 1))
        rolled.append(value)

    def pick(step):
        which = jnp.broadcast_to(lax.rem(step * g, 4), (16, 128))
        value = rolled[0]
        for quarter in range(1, 4):
            value = jnp.where(which == quarter, rolled[quarter], value)
        return value

    for out, step, first, size in ((qkv_out, 27, 0, 864), (proj_out, 9, 8, 288), (bias_out, 3, 11, 96)):
        value = pick(step)
        for i in range(-(-size // 128)):
            n = min(128, size - 128 * i)
            out[pl.ds(128 * i, n)] = value[first + i, 0:n]
    for into, out in moves:
        out.wait()


def local(tokens, cotangent, ocean_mask, land_mask, w_qkv, w_proj, rel_bias):
    grid = jax.ShapeDtypeStruct((8, 48, C), BF16)
    dma = pltpu.SemaphoreType.DMA
    half = pltpu.VMEM((4, 48, C), BF16)
    scratch = [
        pltpu.VMEM((8, 48, C), BF16),
        pltpu.VMEM((8, 48, C), BF16),
        pltpu.VMEM((16, 128), F32),
        pltpu.VMEM((8, 48, C), BF16),
        pltpu.VMEM((8, 48, C), BF16),
        pltpu.VMEM((8, 48), jnp.int32),
        pltpu.VMEM((1, 6), jnp.int32),
        pltpu.VMEM((C, 3 * C), BF16),
        pltpu.VMEM((C, C), BF16),
        pltpu.VMEM((12, 64, 64), F32),
        half, half, pltpu.VMEM((8, 48), jnp.int32), half, half, half, half,
        pltpu.VMEM((C, C), F32),
        pltpu.VMEM((C, C), F32),
        pltpu.VMEM((C, C), F32),
        pltpu.VMEM((C, 128), F32),
        pltpu.VMEM((C, 128), F32),
        pltpu.VMEM((C, C), BF16),
        pltpu.VMEM((C, C), BF16),
        pltpu.VMEM((C, 3 * C), BF16),
        pltpu.VMEM((C, C), BF16),
        pltpu.VMEM((C, C), BF16),
        pltpu.VMEM((C, C), BF16),
        pltpu.VMEM((C, 3 * C), BF16),
        pltpu.VMEM((C, 768), F32),
        pltpu.VMEM((64, 768), F32),
        pltpu.VMEM((64, 768), F32),
        pltpu.VMEM((12, C, 128), F32),
        pltpu.VMEM((768, 128), F32),
        dma((7,)), dma((5,)), dma((5,)), dma((5,)),
    ]
    for rows, count, na in PARTS:
        scratch += part_scratch(count, na)
    block_out, token_grad, red = pl.pallas_call(
        kernel,
        out_shape=[grid, grid, jax.ShapeDtypeStruct((16, 128), F32)],
        in_specs=[pl.BlockSpec(memory_space=pltpu.HBM)] * 7,
        out_specs=[pl.BlockSpec(memory_space=pltpu.HBM)] * 3,
        scratch_shapes=scratch,
        compiler_params=pltpu.CompilerParams(
            collective_id=0, has_side_effects=True, vmem_limit_bytes=VMEM_BYTES
        ),
        cost_estimate=pl.CostEstimate(flops=15 * 10**8, bytes_accessed=5 * 10**6, transcendentals=300000),
        name="window_block",
    )(tokens, cotangent, ocean_mask, land_mask, w_qkv, w_proj, rel_bias)

    whole = pl.BlockSpec(memory_space=pltpu.VMEM)
    hbm = pl.BlockSpec(memory_space=pltpu.HBM)
    return tuple(
        pl.pallas_call(
            place_kernel,
            out_shape=[grid, grid] + [jax.ShapeDtypeStruct((n,), F32) for n in (864, 288, 96)],
            in_specs=[hbm] * 3,
            out_specs=[hbm, hbm, whole, whole, whole],
            scratch_shapes=[
                pltpu.VMEM((8, 48, C), BF16),
                pltpu.VMEM((8, 48, C), BF16),
                pltpu.VMEM((16, 128), F32),
                dma((5,)),
                dma((4,)),
            ],
            compiler_params=pltpu.CompilerParams(vmem_limit_bytes=VMEM_BYTES),
            cost_estimate=pl.CostEstimate(flops=10**4, bytes_accessed=12 * 10**5, transcendentals=0),
            name="outputs",
        )(block_out, token_grad, red)
    )


def solution(mesh):
    split = ("band", "grp")
    placed = (
        P(split, None, None),
        P(split, None, None),
        P(split, None),
        P(split, None),
        P(),
        P(),
        P(),
    )
    return jax.shard_map(
        local,
        mesh=mesh,
        in_specs=placed,
        out_specs=(P(split, None, None), P(split, None, None), P(split), P(split), P(split)),
        check_vma=False,
    )
```

```python
import math

import jax
import jax.numpy as jnp
from jax import lax
from jax.experimental import pallas as pl
from jax.experimental.pallas import tpu as pltpu
from jax.sharding import PartitionSpec as P

EPS = 1e-05
MASKED = -1e30
C = 384
WB = 6
HG = 3
SCALE = 1.0 / math.sqrt(32)
F32 = jnp.float32
BF16 = jnp.bfloat16
MESH = pl.DeviceIdType.MESH

NY, NX, NZ = 8, 4, 8
OWN = 192
VMEM_BYTES = 62 * 2**20


def qkv_rows(g):
    return [("qkv", j, k) for j in range(3) for k in (g, 3 + g, 6 + g)]


PROJ_ROWS = [("proj", j, k) for j in range(3) for k in range(3)]
BIAS_ROWS = [("bias", j, 0) for j in range(3)]
PARTS = [
    (qkv_rows(0) + PROJ_ROWS[:7], 16, 16),
    (qkv_rows(1)[:8], 8, 0),
    (qkv_rows(1)[8:] + qkv_rows(2) + PROJ_ROWS[7:] + BIAS_ROWS, 16, 16),
]
SLOTS = 13


def owned(g):
    qkv = [min(27 * g // 4 + i, 26) for i in range(8)]
    proj = [min(9 * g // 4 + i, 8) for i in range(3)]
    bias = [min(3 * g // 4 + i, 2) for i in range(2)]
    return (
        [("qkv", r // 9, r % 9) for r in qkv]
        + [("proj", r // 3, r % 3) for r in proj]
        + [("bias", r, 0) for r in bias]
    )


def dot_nt(a, b):
    return lax.dot_general(a, b, (((1,), (1,)), ((), ())), preferred_element_type=F32)


def dot_tn(a, b):
    return lax.dot_general(a, b, (((0,), (0,)), ((), ())), preferred_element_type=F32)


def dot_nn(a, b):
    return lax.dot_general(a, b, (((1,), (0,)), ((), ())), preferred_element_type=F32)


def stage_mask(ocean, land, half, mask_ref):
    place = lax.broadcasted_iota(jnp.int32, (8, 48), 0)
    column = lax.broadcasted_iota(jnp.int32, (8, 48), 1)
    for w in range(WB):
        live = 1.0 - land[:, w : w + 1]
        pick = (column == lax.rem(place + (8 * w + 4), 48)).astype(F32) * live
        for i in range(4):
            row = jnp.broadcast_to(ocean[i : i + 1, :], (8, 48))
            value = jnp.sum(row * pick, axis=1, keepdims=True)
            at = OWN * half + 32 * w + 8 * i
            mask_ref[at : at + 8, :] = jnp.broadcast_to(value, (8, 128))


def stage_rows(rows, half, out_ref):
    for i, row in enumerate(rows):
        rolled = pltpu.roll(row.astype(F32), 44, 0)
        for w in range(WB):
            at = OWN * half + 32 * w + 8 * i
            out_ref[at : at + 8, :] = rolled[8 * w : 8 * w + 8, :]


def grid_row(src_ref, half, i):
    ats = [OWN * half + 32 * w + 8 * i for w in range(WB)]
    return pltpu.roll(jnp.concatenate([src_ref[at : at + 8, :] for at in ats], 0), 4, 0)


class Part:
    def __init__(self, rows, count, along_y, refs, here, send, sources):
        (
            self.pk, self.pack, self.r0, self.s1, self.ra, self.ta, self.ra2, self.rb, self.tb, self.rb2,
            self.core_s, self.core_r, self.a1_s, self.a1_r, self.a2_s, self.a2_r,
            self.b1_s, self.b1_r, self.b2_s, self.b2_r,
        ) = refs
        self.rows, self.count, self.na = rows, count, along_y
        self.half = 2 * count
        self.nb = self.half - along_y
        self.here, self.send, self.sources = here, send, sources
        self.a1, self.a2, self.b1, self.b2 = [], [], [], []

    def start(self):
        band, grp, y, x, z, core = self.here
        n = self.count
        grad_ref, bt_ref = self.sources
        lane = lax.broadcasted_iota(jnp.int32, (128, 128), 1)
        for i, (kind, j, k) in enumerate(self.rows):
            if kind == "bias":
                even = bt_ref[pl.ds(2 * j, 128, stride=6), :]
                odd = bt_ref[pl.ds(2 * j + 1, 128, stride=6), :]
                value = jnp.where(lane < 64, even, pltpu.roll(odd, 64, 1))
            else:
                at = k if kind == "qkv" else 9 + k
                value = grad_ref.at[at][pl.ds(j, 128, stride=3), :]
            self.pk[pl.ds(i, 128, stride=n), :] = value
        for i in range(len(self.rows), n):
            self.pk[pl.ds(i, 128, stride=n), :] = jnp.zeros((128, 128), F32)
        theirs = (1 - core) * self.half

        def narrow(i, carry):
            for j in range(NX):
                at = pl.multiple_of((i * NX + j) * 4 * n + theirs, 16)
                self.pack[i, j] = self.pk[pl.ds(at, self.half), :].astype(BF16)
            return carry

        lax.fori_loop(0, NY, narrow, 0)
        self.core_copy = self.send(
            self.pack, self.r0, self.core_s.at[0], self.core_r.at[0], (band, z * 2 + 1 - core)
        )

    def spread(self):
        band, grp, y, x, z, core = self.here
        n, na = self.count, self.na
        mine = core * self.half
        self.core_copy.wait()

        def add(i, carry):
            for j in range(NX):
                at = pl.multiple_of((i * NX + j) * 4 * n + mine, 16)
                total = self.pk[pl.ds(at, self.half), :] + self.r0[i, j].astype(F32)
                self.s1[i, j] = total.astype(BF16)
            return carry

        lax.fori_loop(0, NY, add, 0)
        for d in range(1, NX):
            to = lax.rem(x + d, NX)
            self.b1.append(
                self.send(
                    self.s1.at[:, to, pl.ds(na, self.nb), :], self.rb.at[d - 1],
                    self.b1_s.at[d - 1], self.b1_r.at[d - 1], (y * NX + to, grp),
                )
            )
        for d in range(1, NY if na else 1):
            to = lax.rem(y + d, NY)
            self.a1.append(
                self.send(
                    self.s1.at[to, :, pl.ds(0, na), :], self.ra.at[d - 1],
                    self.a1_s.at[d - 1], self.a1_r.at[d - 1], (to * NX + x, grp),
                )
            )

    def turn(self):
        band, grp, y, x, z, core = self.here
        na = self.na
        total = self.s1[:, x, na : self.half, :].astype(F32)
        for d in range(1, NX):
            self.b1[d - 1].wait_recv()
            total = total + self.rb[d - 1].astype(F32)
        self.tb[...] = total.astype(BF16)
        for d in range(1, NY):
            to = lax.rem(y + d, NY)
            self.b2.append(
                self.send(
                    self.tb.at[to], self.rb2.at[d - 1],
                    self.b2_s.at[d - 1], self.b2_r.at[d - 1], (to * NX + x, grp),
                )
            )
        if not na:
            return
        total = self.s1[y, :, 0:na, :].astype(F32)
        for d in range(1, NY):
            self.a1[d - 1].wait_recv()
            total = total + self.ra[d - 1].astype(F32)
        self.ta[...] = total.astype(BF16)
        for d in range(1, NX):
            to = lax.rem(x + d, NX)
            self.a2.append(
                self.send(
                    self.ta.at[to], self.ra2.at[d - 1],
                    self.a2_s.at[d - 1], self.a2_r.at[d - 1], (y * NX + to, grp),
                )
            )

    def collect(self, f_ref):
        band, grp, y, x, z, core = self.here
        n, na = self.count, self.na
        total = self.tb[y].astype(F32)
        for d in range(1, NY):
            self.b2[d - 1].wait_recv()
            total = total + self.rb2[d - 1].astype(F32)
        if na:
            low = self.ta[x].astype(F32)
            for d in range(1, NX):
                self.a2[d - 1].wait_recv()
                low = low + self.ra2[d - 1].astype(F32)
            total = jnp.concatenate([low, total], 0)
        for i in range(8):
            for at, row in enumerate(owned(i % 4)):
                if row in self.rows:
                    first = n * (i // 4) + self.rows.index(row)
                    f_ref[i, at : at + 1, :] = total[first : first + 1, :]

    def drain(self):
        for copy in self.a1 + self.a2 + self.b1 + self.b2:
            copy.wait_send()


class Share:
    def __init__(self, f_ref, r3_ref, z_s, z_r, here):
        self.f, self.r3, self.z_s, self.z_r, self.here = f_ref, r3_ref, z_s, z_r, here

    def last(self, i):
        band, grp, y, x, z, core = self.here
        quarter, zi, to_core = i // 4, (i // 2) % 2, i % 2
        to_z = 2 * (2 * core + quarter) + zi
        copy = pltpu.make_async_remote_copy(
            src_ref=self.f.at[i],
            dst_ref=self.r3.at[z],
            send_sem=self.z_s.at[i],
            recv_sem=self.z_r.at[z],
            device_id=(band, to_z * 2 + to_core),
            device_id_type=MESH,
        )
        return copy, jnp.logical_or(to_z != z, core != to_core)

    def start(self):
        for i in range(8):
            copy, away = self.last(i)
            pl.when(away)(copy.start)

    def finish(self, red_ref):
        band, grp, y, x, z, core = self.here
        own_core = z // 4

        @pl.when(core == own_core)
        def _():
            self.r3[z] = self.f[4 * lax.rem(z // 2, 2) + lax.rem(grp, 4)]

        for s in range(NZ):
            come = pltpu.make_async_remote_copy(
                src_ref=self.f.at[0],
                dst_ref=self.r3.at[s],
                send_sem=self.z_s.at[0],
                recv_sem=self.z_r.at[s],
                device_id=(band, z * 2 + 1 - core),
                device_id_type=MESH,
            )
            pl.when(jnp.logical_or(z != s, core != own_core))(come.wait_recv)
        total = self.r3[0]
        for s in range(1, NZ):
            total = total + self.r3[s]
        red_ref[...] = total

    def drain(self):
        for i in range(8):
            copy, away = self.last(i)
            pl.when(away)(copy.wait_send)


def part_scratch(count, na):
    half = 2 * count
    nb = half - na
    dma = pltpu.SemaphoreType.DMA
    return [
        pltpu.VMEM((128 * count, 128), F32),
        pltpu.VMEM((NY, NX, half, 128), BF16),
        pltpu.VMEM((NY, NX, half, 128), BF16),
        pltpu.VMEM((NY, NX, half, 128), BF16),
        pltpu.VMEM((NY - 1, NX, max(na, 16), 128), BF16),
        pltpu.VMEM((NX, max(na, 16), 128), BF16),
        pltpu.VMEM((NX - 1, max(na, 16), 128), BF16),
        pltpu.VMEM((NX - 1, NY, nb, 128), BF16),
        pltpu.VMEM((NY, nb, 128), BF16),
        pltpu.VMEM((NY - 1, nb, 128), BF16),
        dma((1,)), dma((1,)),
        dma((NY - 1,)), dma((NY - 1,)),
        dma((NX - 1,)), dma((NX - 1,)),
        dma((NX - 1,)), dma((NX - 1,)),
        dma((NY - 1,)), dma((NY - 1,)),
    ]


def kernel(
    tok_hbm, cot_hbm, oce_hbm, land_hbm, wqkv_hbm, wproj_hbm, rb_hbm,
    block_hbm, grad_hbm, red_hbm,
    block_ref, grad_out_ref, red_ref,
    tok_ref, cot_ref, oce_ref, land_ref, wqkv_ref, wproj_ref, rb_ref,
    htok_ref, hcot_ref, hoce_ref, uu_ref, ug_ref, hu_ref, hg_ref,
    x_ref, c_ref, n_ref, inv_ref, mask_ref, h_ref, ht_ref, qkv_ref, dz_ref, do_ref, o_ref, dqkv_ref,
    p_ref, bias_ref, db_ref, grad_ref, bt_ref, f_ref, r3_ref, load_sem, store_sem, halo_s, halo_r, z_s, z_r, *rest,
):
    band = lax.axis_index("band")
    grp = lax.axis_index("grp")
    y, x = band // NX, lax.rem(band, NX)
    z, core = grp // 2, lax.rem(grp, 2)
    linear = band * 16 + grp
    after = lax.rem(linear + 1, 512)
    before = lax.rem(linear + 511, 512)
    after_id = (after // 16, lax.rem(after, 16))
    before_id = (before // 16, lax.rem(before, 16))

    loads = []
    for i, (src, dst) in enumerate(
        (
            (tok_hbm, tok_ref), (oce_hbm, oce_ref), (land_hbm, land_ref), (wqkv_hbm, wqkv_ref),
            (cot_hbm, cot_ref), (wproj_hbm, wproj_ref), (rb_hbm, rb_ref),
        )
    ):
        loads.append(pltpu.make_async_copy(src, dst, load_sem.at[i]))
        loads[-1].start()

    barrier = pltpu.get_barrier_semaphore()
    peers = [after_id, before_id]
    peers += [(band, lax.rem(grp + d, 16)) for d in range(1, 16)]
    peers += [(lax.rem(y + d, NY) * NX + x, grp) for d in range(1, NY)]
    peers += [(y * NX + lax.rem(x + d, NX), grp) for d in range(1, NX)]
    for peer in peers:
        pl.semaphore_signal(barrier, inc=1, device_id=peer, device_id_type=MESH)

    def send(src, dst, s, r, to):
        copy = pltpu.make_async_remote_copy(
            src_ref=src, dst_ref=dst, send_sem=s, recv_sem=r, device_id=to, device_id_type=MESH
        )
        copy.start()
        return copy

    kept = []

    def keep(src, dst):
        kept.append(pltpu.make_async_copy(src, dst, store_sem.at[len(kept)]))
        kept[-1].start()

    loads[0].wait()
    stage_rows([tok_ref[4 + i] for i in range(4)], 0, x_ref)

    pl.semaphore_wait(barrier, len(peers))
    halos = [
        send(tok_hbm.at[pl.ds(0, 4)], htok_ref, halo_s.at[0], halo_r.at[0], before_id),
        send(oce_hbm, hoce_ref, halo_s.at[1], halo_r.at[1], before_id),
        send(cot_hbm.at[pl.ds(0, 4)], hcot_ref, halo_s.at[2], halo_r.at[2], before_id),
    ]

    def norm(i, carry):
        rows = pl.ds(pl.multiple_of(i * 64, 64), 64)
        value = x_ref[rows, :]
        centered = value - jnp.mean(value, -1, keepdims=True)
        inv = lax.rsqrt(jnp.mean(centered * centered, -1, keepdims=True) + EPS)
        n = centered * inv
        n_ref[rows, :] = n
        inv_ref[rows, :] = jnp.broadcast_to(inv, (64, 128))
        h_ref[rows, :] = n.astype(BF16)
        return carry

    def project(half):
        rows = slice(OWN * half, OWN * half + OWN)
        qkv_ref[rows, :] = dot_nn(h_ref[rows, :], wqkv_ref[...]).astype(BF16)

    def pull(half):
        rows = slice(OWN * half, OWN * half + OWN)
        wide = jnp.concatenate([mask_ref[rows, :]] * 3, 1)
        dz_ref[rows, :] = (wide * c_ref[rows, :]).astype(BF16)
        do_ref[rows, :] = dot_nt(dz_ref[rows, :], wproj_ref[...]).astype(BF16)

    lax.fori_loop(0, 3, norm, 0, unroll=3)
    loads[1].wait()
    loads[2].wait()
    land = land_ref[...].astype(F32)
    stage_mask(oce_ref[4:8, :].astype(F32), land, 0, mask_ref)
    loads[3].wait()
    project(0)
    loads[4].wait()
    stage_rows([cot_ref[4 + i] for i in range(4)], 0, c_ref)
    loads[5].wait()
    pull(0)
    loads[6].wait()
    for i in range(6):
        pair = jnp.concatenate([rb_ref[2 * i], rb_ref[2 * i + 1]], 0)
        bias_ref[:, 128 * i : 128 * i + 128] = pair.T
    db_ref[...] = jnp.zeros_like(db_ref)

    here_lower = jnp.broadcast_to(linear, (48, C)) < 511
    halos[0].wait_recv()
    stage_rows([jnp.where(here_lower, htok_ref[i].astype(F32), 0.0) for i in range(4)], 1, x_ref)
    lax.fori_loop(3, 6, norm, 0, unroll=3)
    project(1)
    ht_ref[...] = h_ref[...].T
    halos[1].wait_recv()
    ocean = jnp.where(jnp.broadcast_to(linear, (4, 48)) < 511, hoce_ref[0:4, :].astype(F32), 0.0)
    stage_mask(ocean, land, 1, mask_ref)

    head = lax.broadcasted_iota(jnp.int32, (64, 128), 1) // 32
    picks = [(head == i).astype(F32) for i in range(4)]
    picks_low = [p.astype(BF16) for p in picks]

    def spread(a):
        return jnp.concatenate([a * p for p in picks_low], 0)

    def fold(value):
        total = value[0:64] * picks[0]
        for i in range(1, 4):
            total = total + value[64 * i : 64 * i + 64] * picks[i]
        return total

    def two(w):
        first = pl.ds(pl.multiple_of(w * 32, 32), 32)
        second = pl.ds(pl.multiple_of(OWN + w * 32, 32), 32)
        return first, second

    def load(ref, w, lanes):
        first, second = two(w)
        return jnp.concatenate([ref[first, lanes], ref[second, lanes]], 0)

    def store(ref, w, lanes, value):
        first, second = two(w)
        ref[first, lanes] = value[0:32]
        ref[second, lanes] = value[32:64]

    def lanes_of(g):
        return [slice(C * i + 128 * g, C * i + 128 * g + 128) for i in range(3)] + [
            slice(256 * g, 256 * g + 256)
        ]

    def forward(w, carry):
        whole = pl.ds(pl.multiple_of(w * 64, 64), 64)
        live = jnp.concatenate([load(mask_ref, w, slice(0, 128))] * 2, 1) > 0.5
        for g in range(HG):
            q_lanes, k_lanes, v_lanes, wide = lanes_of(g)
            q4 = spread(load(qkv_ref, w, q_lanes))
            s = dot_nt(load(qkv_ref, w, k_lanes), q4) * SCALE + bias_ref[:, wide]
            s = jnp.where(live, s, MASKED)
            weights = jnp.exp(s - jnp.max(s, 0, keepdims=True))
            p = weights * (1.0 / jnp.sum(weights, 0, keepdims=True))
            p_ref[whole, wide] = p
            store(o_ref, w, q_lanes, fold(dot_tn(p.astype(BF16), load(qkv_ref, w, v_lanes))).astype(BF16))
        return carry

    def backward(g):
        q_lanes, k_lanes, v_lanes, wide = lanes_of(g)

        def step(w, carry):
            whole = pl.ds(pl.multiple_of(w * 64, 64), 64)
            q4 = spread(load(qkv_ref, w, q_lanes))
            do4 = spread(load(do_ref, w, q_lanes))
            p = p_ref[whole, wide]
            dp = dot_nt(load(qkv_ref, w, v_lanes), do4)
            store(dqkv_ref, w, v_lanes, dot_nn(p.astype(BF16), do4).astype(BF16))
            ds = p * (dp - jnp.sum(p * dp, 0, keepdims=True))
            db_ref[:, wide] += ds
            dsc = (ds * SCALE).astype(BF16)
            store(dqkv_ref, w, k_lanes, dot_nn(dsc, q4).astype(BF16))
            dq = fold(dot_tn(dsc, load(qkv_ref, w, k_lanes)))
            store(dqkv_ref, w, q_lanes, dq.astype(BF16))
            return carry

        lax.fori_loop(0, WB, step, 0, unroll=6)
        for k in (g, 3 + g, 6 + g):
            grad_ref[k] = dot_nn(ht_ref[...], dqkv_ref[:, 128 * k : 128 * k + 128])

    lax.fori_loop(0, WB, forward, 0, unroll=2)

    halos[2].wait_recv()
    stage_rows([jnp.where(here_lower, hcot_ref[i].astype(F32), 0.0) for i in range(4)], 1, c_ref)
    pull(1)

    here = (band, grp, y, x, z, core)
    parts = []
    at = 0
    for rows, count, na in PARTS:
        parts.append(Part(rows, count, na, rest[at : at + 20], here, send, (grad_ref, bt_ref)))
        at += 20
    first, second, third = parts
    share = Share(f_ref, r3_ref, z_s, z_r, here)

    proj = dot_tn(o_ref[...], dz_ref[...])
    for k in range(3):
        grad_ref[9 + k] = proj[:, 128 * k : 128 * k + 128]
    backward(0)
    first.start()
    for i in range(8):
        f_ref[i, SLOTS:16, :] = jnp.zeros((16 - SLOTS, 128), F32)
    backward(1)
    second.start()
    first.spread()
    backward(2)
    for i in range(6):
        bt_ref[128 * i : 128 * i + 128, 0:64] = db_ref[:, 128 * i : 128 * i + 128].T
    third.start()
    second.spread()
    first.turn()

    wide_mask = jnp.concatenate([mask_ref[...]] * 3, 1)
    x_ref[...] = wide_mask * dot_nn(o_ref[...], wproj_ref[...])
    third.spread()
    for i in range(4):
        uu_ref[i] = grid_row(x_ref, 1, i).astype(BF16)
    halo_u = send(uu_ref, hu_ref, halo_s.at[3], halo_r.at[3], after_id)
    second.turn()
    c_ref[...] = dot_nt(dqkv_ref[...], wqkv_ref[...])

    def back(i, carry):
        rows = pl.ds(pl.multiple_of(i * 64, 64), 64)
        dh = c_ref[rows, :]
        n = n_ref[rows, :]
        inv = jnp.concatenate([inv_ref[rows, :]] * 3, 1)
        slope = jnp.mean(dh * n, -1, keepdims=True)
        c_ref[rows, :] = inv * (dh - jnp.mean(dh, -1, keepdims=True) - n * slope)
        return carry

    lax.fori_loop(0, WB, back, 0, unroll=3)
    for i in range(4):
        ug_ref[i] = grid_row(c_ref, 1, i).astype(BF16)
    halo_g = send(ug_ref, hg_ref, halo_s.at[4], halo_r.at[4], after_id)
    third.turn()
    first.collect(f_ref)
    for i in range(4):
        row = grid_row(x_ref, 0, i).astype(BF16).astype(F32)
        block_ref[4 + i] = (tok_ref[4 + i].astype(F32) + row).astype(BF16)
        row = grid_row(c_ref, 0, i).astype(BF16).astype(F32)
        grad_out_ref[4 + i] = (cot_ref[4 + i].astype(F32) + row).astype(BF16)
    upper, lower = pl.ds(4, 4), pl.ds(0, 4)
    keep(block_ref.at[upper], block_hbm.at[upper])
    keep(grad_out_ref.at[upper], grad_hbm.at[upper])
    second.collect(f_ref)
    third.collect(f_ref)
    share.start()
    inner = jnp.broadcast_to(linear, (4, 48, C)) > 0
    halo_u.wait_recv()
    low = jnp.where(inner, hu_ref[...].astype(F32), 0.0)
    block_ref[0:4] = (tok_ref[0:4].astype(F32) + low).astype(BF16)
    keep(block_ref.at[lower], block_hbm.at[lower])
    halo_g.wait_recv()
    low = jnp.where(inner, hg_ref[...].astype(F32), 0.0)
    grad_out_ref[0:4] = (cot_ref[0:4].astype(F32) + low).astype(BF16)
    keep(grad_out_ref.at[lower], grad_hbm.at[lower])
    for part in parts:
        part.drain()
    share.finish(red_ref)
    keep(red_ref, red_hbm)
    share.drain()
    for copy in halos + [halo_u, halo_g]:
        copy.wait_send()
    for copy in kept:
        copy.wait()


def place_kernel(
    block_hbm, grad_hbm, red_hbm, block_out, grad_out, qkv_out, proj_out, bias_out,
    block_ref, grad_ref, red_ref, in_sem, out_sem,
):
    load = pltpu.make_async_copy(red_hbm, red_ref, in_sem.at[4])
    load.start()
    moves = []
    for i, (src, via, dst) in enumerate(((block_hbm, block_ref, block_out), (grad_hbm, grad_ref, grad_out))):
        for j in range(2):
            part = pl.ds(4 * j, 4)
            into = pltpu.make_async_copy(src.at[part], via.at[part], in_sem.at[2 * i + j])
            into.start()
            moves.append((into, pltpu.make_async_copy(via.at[part], dst.at[part], out_sem.at[2 * i + j])))
    load.wait()
    for into, out in moves:
        into.wait()
        out.start()
    g = lax.rem(lax.axis_index("grp"), 4)
    lane = lax.broadcasted_iota(jnp.int32, (16, 128), 1)
    red = red_ref[...]
    following = jnp.concatenate([red[1:16], red[0:1]], 0)
    rolled = [red]
    for quarter in range(1, 4):
        shift = 128 - 32 * quarter
        value = jnp.where(lane < shift, pltpu.roll(red, shift, 1), pltpu.roll(following, shift, 1))
        rolled.append(value)

    def pick(step):
        which = jnp.broadcast_to(lax.rem(step * g, 4), (16, 128))
        value = rolled[0]
        for quarter in range(1, 4):
            value = jnp.where(which == quarter, rolled[quarter], value)
        return value

    for out, step, first, size in ((qkv_out, 27, 0, 864), (proj_out, 9, 8, 288), (bias_out, 3, 11, 96)):
        value = pick(step)
        for i in range(-(-size // 128)):
            n = min(128, size - 128 * i)
            out[pl.ds(128 * i, n)] = value[first + i, 0:n]
    for into, out in moves:
        out.wait()


def local(tokens, cotangent, ocean_mask, land_mask, w_qkv, w_proj, rel_bias):
    grid = jax.ShapeDtypeStruct((8, 48, C), BF16)
    dma = pltpu.SemaphoreType.DMA
    half = pltpu.VMEM((4, 48, C), BF16)
    scratch = [
        pltpu.VMEM((8, 48, C), BF16),
        pltpu.VMEM((8, 48, C), BF16),
        pltpu.VMEM((16, 128), F32),
        pltpu.VMEM((8, 48, C), BF16),
        pltpu.VMEM((8, 48, C), BF16),
        pltpu.VMEM((8, 48), jnp.int32),
        pltpu.VMEM((1, 6), jnp.int32),
        pltpu.VMEM((C, 3 * C), BF16),
        pltpu.VMEM((C, C), BF16),
        pltpu.VMEM((12, 64, 64), F32),
        half, half, pltpu.VMEM((8, 48), jnp.int32), half, half, half, half,
        pltpu.VMEM((C, C), F32),
        pltpu.VMEM((C, C), F32),
        pltpu.VMEM((C, C), F32),
        pltpu.VMEM((C, 128), F32),
        pltpu.VMEM((C, 128), F32),
        pltpu.VMEM((C, C), BF16),
        pltpu.VMEM((C, C), BF16),
        pltpu.VMEM((C, 3 * C), BF16),
        pltpu.VMEM((C, C), BF16),
        pltpu.VMEM((C, C), BF16),
        pltpu.VMEM((C, C), BF16),
        pltpu.VMEM((C, 3 * C), BF16),
        pltpu.VMEM((C, 768), F32),
        pltpu.VMEM((64, 768), F32),
        pltpu.VMEM((64, 768), F32),
        pltpu.VMEM((12, C, 128), F32),
        pltpu.VMEM((768, 128), F32),
        pltpu.VMEM((8, 16, 128), F32),
        pltpu.VMEM((NZ, 16, 128), F32),
        dma((7,)), dma((5,)), dma((5,)), dma((5,)), dma((8,)), dma((NZ,)),
    ]
    for rows, count, na in PARTS:
        scratch += part_scratch(count, na)
    block_out, token_grad, red = pl.pallas_call(
        kernel,
        out_shape=[grid, grid, jax.ShapeDtypeStruct((16, 128), F32)],
        in_specs=[pl.BlockSpec(memory_space=pltpu.HBM)] * 7,
        out_specs=[pl.BlockSpec(memory_space=pltpu.HBM)] * 3,
        scratch_shapes=scratch,
        compiler_params=pltpu.CompilerParams(
            collective_id=0, has_side_effects=True, vmem_limit_bytes=VMEM_BYTES
        ),
        cost_estimate=pl.CostEstimate(flops=15 * 10**8, bytes_accessed=5 * 10**6, transcendentals=300000),
        name="window_block",
    )(tokens, cotangent, ocean_mask, land_mask, w_qkv, w_proj, rel_bias)

    whole = pl.BlockSpec(memory_space=pltpu.VMEM)
    hbm = pl.BlockSpec(memory_space=pltpu.HBM)
    return tuple(
        pl.pallas_call(
            place_kernel,
            out_shape=[grid, grid] + [jax.ShapeDtypeStruct((n,), F32) for n in (864, 288, 96)],
            in_specs=[hbm] * 3,
            out_specs=[hbm, hbm, whole, whole, whole],
            scratch_shapes=[
                pltpu.VMEM((8, 48, C), BF16),
                pltpu.VMEM((8, 48, C), BF16),
                pltpu.VMEM((16, 128), F32),
                dma((5,)),
                dma((4,)),
            ],
            compiler_params=pltpu.CompilerParams(vmem_limit_bytes=VMEM_BYTES),
            cost_estimate=pl.CostEstimate(flops=10**4, bytes_accessed=12 * 10**5, transcendentals=0),
            name="outputs",
        )(block_out, token_grad, red)
    )


def solution(mesh):
    split = ("band", "grp")
    placed = (
        P(split, None, None),
        P(split, None, None),
        P(split, None),
        P(split, None),
        P(),
        P(),
        P(),
    )
    return jax.shard_map(
        local,
        mesh=mesh,
        in_specs=placed,
        out_specs=(P(split, None, None), P(split, None, None), P(split), P(split), P(split)),
        check_vma=False,
    )
```

```python
import math

import jax
import jax.numpy as jnp
from jax import lax
from jax.experimental import pallas as pl
from jax.experimental.pallas import tpu as pltpu
from jax.sharding import PartitionSpec as P

EPS = 1e-05
MASKED = -1e30
C = 384
WB = 6
HG = 3
SCALE = 1.0 / math.sqrt(32)
F32 = jnp.float32
BF16 = jnp.bfloat16
MESH = pl.DeviceIdType.MESH

NY, NX, NZ = 8, 4, 8
OWN = 192
VMEM_BYTES = 62 * 2**20


def qkv_rows(g):
    return [("qkv", j, k) for j in range(3) for k in (g, 3 + g, 6 + g)]


PROJ_ROWS = [("proj", j, k) for j in range(3) for k in range(3)]
BIAS_ROWS = [("bias", j, 0) for j in range(3)]
PARTS = [
    (qkv_rows(0) + PROJ_ROWS[:7], 16, 16),
    (qkv_rows(1) + qkv_rows(2) + PROJ_ROWS[7:] + BIAS_ROWS, 24, 16),
]
SLOTS = 13


def owned(g):
    qkv = [min(27 * g // 4 + i, 26) for i in range(8)]
    proj = [min(9 * g // 4 + i, 8) for i in range(3)]
    bias = [min(3 * g // 4 + i, 2) for i in range(2)]
    return (
        [("qkv", r // 9, r % 9) for r in qkv]
        + [("proj", r // 3, r % 3) for r in proj]
        + [("bias", r, 0) for r in bias]
    )


def dot_nt(a, b):
    return lax.dot_general(a, b, (((1,), (1,)), ((), ())), preferred_element_type=F32)


def dot_tn(a, b):
    return lax.dot_general(a, b, (((0,), (0,)), ((), ())), preferred_element_type=F32)


def dot_nn(a, b):
    return lax.dot_general(a, b, (((1,), (0,)), ((), ())), preferred_element_type=F32)


def stage_mask(ocean, land, half, mask_ref):
    place = lax.broadcasted_iota(jnp.int32, (8, 48), 0)
    column = lax.broadcasted_iota(jnp.int32, (8, 48), 1)
    for w in range(WB):
        live = 1.0 - land[:, w : w + 1]
        pick = (column == lax.rem(place + (8 * w + 4), 48)).astype(F32) * live
        for i in range(4):
            row = jnp.broadcast_to(ocean[i : i + 1, :], (8, 48))
            value = jnp.sum(row * pick, axis=1, keepdims=True)
            at = OWN * half + 32 * w + 8 * i
            mask_ref[at : at + 8, :] = jnp.broadcast_to(value, (8, 128))


def stage_rows(rows, half, out_ref):
    for i, row in enumerate(rows):
        rolled = pltpu.roll(row.astype(F32), 44, 0)
        for w in range(WB):
            at = OWN * half + 32 * w + 8 * i
            out_ref[at : at + 8, :] = rolled[8 * w : 8 * w + 8, :]


def grid_row(src_ref, half, i):
    ats = [OWN * half + 32 * w + 8 * i for w in range(WB)]
    return pltpu.roll(jnp.concatenate([src_ref[at : at + 8, :] for at in ats], 0), 4, 0)


class Part:
    def __init__(self, rows, count, along_y, refs, here, send, sources):
        (
            self.pk, self.pack, self.r0, self.s1, self.ra, self.ta, self.ra2, self.rb, self.tb, self.rb2,
            self.core_s, self.core_r, self.a1_s, self.a1_r, self.a2_s, self.a2_r,
            self.b1_s, self.b1_r, self.b2_s, self.b2_r,
        ) = refs
        self.rows, self.count, self.na = rows, count, along_y
        self.half = 2 * count
        self.nb = self.half - along_y
        self.here, self.send, self.sources = here, send, sources
        self.a1, self.a2, self.b1, self.b2 = [], [], [], []

    def start(self):
        band, grp, y, x, z, core = self.here
        n = self.count
        grad_ref, bt_ref = self.sources
        lane = lax.broadcasted_iota(jnp.int32, (128, 128), 1)
        for i, (kind, j, k) in enumerate(self.rows):
            if kind == "bias":
                even = bt_ref[pl.ds(2 * j, 128, stride=6), :]
                odd = bt_ref[pl.ds(2 * j + 1, 128, stride=6), :]
                value = jnp.where(lane < 64, even, pltpu.roll(odd, 64, 1))
            else:
                at = k if kind == "qkv" else 9 + k
                value = grad_ref.at[at][pl.ds(j, 128, stride=3), :]
            self.pk[pl.ds(i, 128, stride=n), :] = value
        for i in range(len(self.rows), n):
            self.pk[pl.ds(i, 128, stride=n), :] = jnp.zeros((128, 128), F32)
        theirs = (1 - core) * self.half

        def narrow(i, carry):
            for j in range(NX):
                at = pl.multiple_of((i * NX + j) * 4 * n + theirs, 16)
                self.pack[i, j] = self.pk[pl.ds(at, self.half), :].astype(BF16)
            return carry

        lax.fori_loop(0, NY, narrow, 0)
        self.core_copy = self.send(
            self.pack, self.r0, self.core_s.at[0], self.core_r.at[0], (band, z * 2 + 1 - core)
        )

    def spread(self):
        band, grp, y, x, z, core = self.here
        n, na = self.count, self.na
        mine = core * self.half
        self.core_copy.wait()

        def add(i, carry):
            for j in range(NX):
                at = pl.multiple_of((i * NX + j) * 4 * n + mine, 16)
                total = self.pk[pl.ds(at, self.half), :] + self.r0[i, j].astype(F32)
                self.s1[i, j] = total.astype(BF16)
            return carry

        lax.fori_loop(0, NY, add, 0)
        for d in range(1, NX):
            to = lax.rem(x + d, NX)
            self.b1.append(
                self.send(
                    self.s1.at[:, to, pl.ds(na, self.nb), :], self.rb.at[d - 1],
                    self.b1_s.at[d - 1], self.b1_r.at[d - 1], (y * NX + to, grp),
                )
            )
        for d in range(1, NY if na else 1):
            to = lax.rem(y + d, NY)
            self.a1.append(
                self.send(
                    self.s1.at[to, :, pl.ds(0, na), :], self.ra.at[d - 1],
                    self.a1_s.at[d - 1], self.a1_r.at[d - 1], (to * NX + x, grp),
                )
            )

    def turn(self):
        band, grp, y, x, z, core = self.here
        na = self.na
        total = self.s1[:, x, na : self.half, :].astype(F32)
        for d in range(1, NX):
            self.b1[d - 1].wait_recv()
            total = total + self.rb[d - 1].astype(F32)
        self.tb[...] = total.astype(BF16)
        for d in range(1, NY):
            to = lax.rem(y + d, NY)
            self.b2.append(
                self.send(
                    self.tb.at[to], self.rb2.at[d - 1],
                    self.b2_s.at[d - 1], self.b2_r.at[d - 1], (to * NX + x, grp),
                )
            )
        if not na:
            return
        total = self.s1[y, :, 0:na, :].astype(F32)
        for d in range(1, NY):
            self.a1[d - 1].wait_recv()
            total = total + self.ra[d - 1].astype(F32)
        self.ta[...] = total.astype(BF16)
        for d in range(1, NX):
            to = lax.rem(x + d, NX)
            self.a2.append(
                self.send(
                    self.ta.at[to], self.ra2.at[d - 1],
                    self.a2_s.at[d - 1], self.a2_r.at[d - 1], (y * NX + to, grp),
                )
            )

    def collect(self, f_ref):
        band, grp, y, x, z, core = self.here
        n, na = self.count, self.na
        total = self.tb[y].astype(F32)
        for d in range(1, NY):
            self.b2[d - 1].wait_recv()
            total = total + self.rb2[d - 1].astype(F32)
        if na:
            low = self.ta[x].astype(F32)
            for d in range(1, NX):
                self.a2[d - 1].wait_recv()
                low = low + self.ra2[d - 1].astype(F32)
            total = jnp.concatenate([low, total], 0)
        for i in range(8):
            for at, row in enumerate(owned(i % 4)):
                if row in self.rows:
                    first = n * (i // 4) + self.rows.index(row)
                    f_ref[i, at : at + 1, :] = total[first : first + 1, :]

    def drain(self):
        for copy in self.a1 + self.a2 + self.b1 + self.b2:
            copy.wait_send()


class Share:
    def __init__(self, f_ref, r3_ref, z_s, z_r, here):
        self.f, self.r3, self.z_s, self.z_r, self.here = f_ref, r3_ref, z_s, z_r, here

    def last(self, i):
        band, grp, y, x, z, core = self.here
        quarter, zi, to_core = i // 4, (i // 2) % 2, i % 2
        to_z = 2 * (2 * core + quarter) + zi
        copy = pltpu.make_async_remote_copy(
            src_ref=self.f.at[i],
            dst_ref=self.r3.at[z],
            send_sem=self.z_s.at[i],
            recv_sem=self.z_r.at[z],
            device_id=(band, to_z * 2 + to_core),
            device_id_type=MESH,
        )
        return copy, jnp.logical_or(to_z != z, core != to_core)

    def start(self):
        for i in range(8):
            copy, away = self.last(i)
            pl.when(away)(copy.start)

    def finish(self, red_ref):
        band, grp, y, x, z, core = self.here
        own_core = z // 4

        @pl.when(core == own_core)
        def _():
            self.r3[z] = self.f[4 * lax.rem(z // 2, 2) + lax.rem(grp, 4)]

        for s in range(NZ):
            come = pltpu.make_async_remote_copy(
                src_ref=self.f.at[0],
                dst_ref=self.r3.at[s],
                send_sem=self.z_s.at[0],
                recv_sem=self.z_r.at[s],
                device_id=(band, z * 2 + 1 - core),
                device_id_type=MESH,
            )
            pl.when(jnp.logical_or(z != s, core != own_core))(come.wait_recv)
        total = self.r3[0]
        for s in range(1, NZ):
            total = total + self.r3[s]
        red_ref[...] = total

    def drain(self):
        for i in range(8):
            copy, away = self.last(i)
            pl.when(away)(copy.wait_send)


def part_scratch(count, na):
    half = 2 * count
    nb = half - na
    dma = pltpu.SemaphoreType.DMA
    return [
        pltpu.VMEM((128 * count, 128), F32),
        pltpu.VMEM((NY, NX, half, 128), BF16),
        pltpu.VMEM((NY, NX, half, 128), BF16),
        pltpu.VMEM((NY, NX, half, 128), BF16),
        pltpu.VMEM((NY - 1, NX, max(na, 16), 128), BF16),
        pltpu.VMEM((NX, max(na, 16), 128), BF16),
        pltpu.VMEM((NX - 1, max(na, 16), 128), BF16),
        pltpu.VMEM((NX - 1, NY, nb, 128), BF16),
        pltpu.VMEM((NY, nb, 128), BF16),
        pltpu.VMEM((NY - 1, nb, 128), BF16),
        dma((1,)), dma((1,)),
        dma((NY - 1,)), dma((NY - 1,)),
        dma((NX - 1,)), dma((NX - 1,)),
        dma((NX - 1,)), dma((NX - 1,)),
        dma((NY - 1,)), dma((NY - 1,)),
    ]


def kernel(
    tok_hbm, cot_hbm, oce_hbm, land_hbm, wqkv_hbm, wproj_hbm, rb_hbm,
    block_hbm, grad_hbm, red_hbm,
    block_ref, grad_out_ref, red_ref,
    tok_ref, cot_ref, oce_ref, land_ref, wqkv_ref, wproj_ref, rb_ref,
    htok_ref, hcot_ref, hoce_ref, uu_ref, ug_ref, hu_ref, hg_ref,
    x_ref, c_ref, n_ref, inv_ref, mask_ref, h_ref, ht_ref, qkv_ref, dz_ref, do_ref, o_ref, dqkv_ref,
    p_ref, bias_ref, db_ref, grad_ref, bt_ref, f_ref, r3_ref, load_sem, store_sem, halo_s, halo_r, z_s, z_r, near_sem, *rest,
):
    band = lax.axis_index("band")
    grp = lax.axis_index("grp")
    y, x = band // NX, lax.rem(band, NX)
    z, core = grp // 2, lax.rem(grp, 2)
    linear = band * 16 + grp
    after = lax.rem(linear + 1, 512)
    before = lax.rem(linear + 511, 512)
    after_id = (after // 16, lax.rem(after, 16))
    before_id = (before // 16, lax.rem(before, 16))

    loads = []
    for i, (src, dst) in enumerate(
        (
            (tok_hbm, tok_ref), (oce_hbm, oce_ref), (land_hbm, land_ref), (wqkv_hbm, wqkv_ref),
            (cot_hbm, cot_ref), (wproj_hbm, wproj_ref), (rb_hbm, rb_ref),
        )
    ):
        loads.append(pltpu.make_async_copy(src, dst, load_sem.at[i]))
        loads[-1].start()

    barrier = pltpu.get_barrier_semaphore()


    def at_z(d):
        return (band, lax.rem(z + NZ + d, NZ) * 2 + core)

    def at_y(d):
        return (lax.rem(y + NY + d, NY) * NX + x, grp)

    def at_x(d):
        return (y * NX + lax.rem(x + NX + d, NX), grp)

    peers = [after_id, before_id, (band, z * 2 + 1 - core)]
    peers += [at(d) for at in (at_z, at_y, at_x) for d in (1, -1)]
    for peer in peers:
        pl.semaphore_signal(barrier, inc=1, device_id=peer, device_id_type=MESH)

    def tell(r, at, d):
        for to in (at(d), at(-d)):
            pl.semaphore_signal(near_sem.at[r], inc=1, device_id=to, device_id_type=MESH)

    def send(src, dst, s, r, to):
        copy = pltpu.make_async_remote_copy(
            src_ref=src, dst_ref=dst, send_sem=s, recv_sem=r, device_id=to, device_id_type=MESH
        )
        copy.start()
        return copy

    kept = []

    def keep(src, dst):
        kept.append(pltpu.make_async_copy(src, dst, store_sem.at[len(kept)]))
        kept[-1].start()

    loads[0].wait()
    stage_rows([tok_ref[4 + i] for i in range(4)], 0, x_ref)

    pl.semaphore_wait(barrier, len(peers))
    tell(0, at_z, 1)
    tell(1, at_y, 1)
    tell(2, at_x, 1)
    far = (2, 3, 4)
    halos = [
        send(tok_hbm.at[pl.ds(0, 4)], htok_ref, halo_s.at[0], halo_r.at[0], before_id),
        send(oce_hbm, hoce_ref, halo_s.at[1], halo_r.at[1], before_id),
        send(cot_hbm.at[pl.ds(0, 4)], hcot_ref, halo_s.at[2], halo_r.at[2], before_id),
    ]

    def norm(i, carry):
        rows = pl.ds(pl.multiple_of(i * 64, 64), 64)
        value = x_ref[rows, :]
        centered = value - jnp.mean(value, -1, keepdims=True)
        inv = lax.rsqrt(jnp.mean(centered * centered, -1, keepdims=True) + EPS)
        n = centered * inv
        n_ref[rows, :] = n
        inv_ref[rows, :] = jnp.broadcast_to(inv, (64, 128))
        h_ref[rows, :] = n.astype(BF16)
        return carry

    def project(half):
        rows = slice(OWN * half, OWN * half + OWN)
        qkv_ref[rows, :] = dot_nn(h_ref[rows, :], wqkv_ref[...]).astype(BF16)

    def pull(half):
        rows = slice(OWN * half, OWN * half + OWN)
        wide = jnp.concatenate([mask_ref[rows, :]] * 3, 1)
        dz_ref[rows, :] = (wide * c_ref[rows, :]).astype(BF16)
        do_ref[rows, :] = dot_nt(dz_ref[rows, :], wproj_ref[...]).astype(BF16)

    lax.fori_loop(0, 3, norm, 0, unroll=3)
    loads[1].wait()
    loads[2].wait()
    land = land_ref[...].astype(F32)
    stage_mask(oce_ref[4:8, :].astype(F32), land, 0, mask_ref)
    loads[3].wait()
    project(0)
    loads[4].wait()
    stage_rows([cot_ref[4 + i] for i in range(4)], 0, c_ref)
    loads[5].wait()
    pull(0)
    loads[6].wait()
    for i in range(6):
        pair = jnp.concatenate([rb_ref[2 * i], rb_ref[2 * i + 1]], 0)
        bias_ref[:, 128 * i : 128 * i + 128] = pair.T
    db_ref[...] = jnp.zeros_like(db_ref)

    here_lower = jnp.broadcast_to(linear, (48, C)) < 511
    halos[0].wait_recv()
    stage_rows([jnp.where(here_lower, htok_ref[i].astype(F32), 0.0) for i in range(4)], 1, x_ref)
    lax.fori_loop(3, 6, norm, 0, unroll=3)
    project(1)
    for r in (0, 1):
        pl.semaphore_wait(near_sem.at[r], 2)
    tell(3, at_z, 2)
    tell(4, at_y, 2)
    ht_ref[...] = h_ref[...].T
    halos[1].wait_recv()
    ocean = jnp.where(jnp.broadcast_to(linear, (4, 48)) < 511, hoce_ref[0:4, :].astype(F32), 0.0)
    stage_mask(ocean, land, 1, mask_ref)

    head = lax.broadcasted_iota(jnp.int32, (64, 128), 1) // 32
    picks = [(head == i).astype(F32) for i in range(4)]
    picks_low = [p.astype(BF16) for p in picks]

    def spread(a):
        return jnp.concatenate([a * p for p in picks_low], 0)

    def fold(value):
        total = value[0:64] * picks[0]
        for i in range(1, 4):
            total = total + value[64 * i : 64 * i + 64] * picks[i]
        return total

    def two(w):
        first = pl.ds(pl.multiple_of(w * 32, 32), 32)
        second = pl.ds(pl.multiple_of(OWN + w * 32, 32), 32)
        return first, second

    def load(ref, w, lanes):
        first, second = two(w)
        return jnp.concatenate([ref[first, lanes], ref[second, lanes]], 0)

    def store(ref, w, lanes, value):
        first, second = two(w)
        ref[first, lanes] = value[0:32]
        ref[second, lanes] = value[32:64]

    def lanes_of(g):
        return [slice(C * i + 128 * g, C * i + 128 * g + 128) for i in range(3)] + [
            slice(256 * g, 256 * g + 256)
        ]

    def forward(w, carry):
        whole = pl.ds(pl.multiple_of(w * 64, 64), 64)
        live = jnp.concatenate([load(mask_ref, w, slice(0, 128))] * 2, 1) > 0.5
        for g in range(HG):
            q_lanes, k_lanes, v_lanes, wide = lanes_of(g)
            q4 = spread(load(qkv_ref, w, q_lanes))
            s = dot_nt(load(qkv_ref, w, k_lanes), q4) * SCALE + bias_ref[:, wide]
            s = jnp.where(live, s, MASKED)
            weights = jnp.exp(s - jnp.max(s, 0, keepdims=True))
            p = weights * (1.0 / jnp.sum(weights, 0, keepdims=True))
            p_ref[whole, wide] = p
            store(o_ref, w, q_lanes, fold(dot_tn(p.astype(BF16), load(qkv_ref, w, v_lanes))).astype(BF16))
        return carry

    def backward(g):
        q_lanes, k_lanes, v_lanes, wide = lanes_of(g)

        def step(w, carry):
            whole = pl.ds(pl.multiple_of(w * 64, 64), 64)
            q4 = spread(load(qkv_ref, w, q_lanes))
            do4 = spread(load(do_ref, w, q_lanes))
            p = p_ref[whole, wide]
            dp = dot_nt(load(qkv_ref, w, v_lanes), do4)
            store(dqkv_ref, w, v_lanes, dot_nn(p.astype(BF16), do4).astype(BF16))
            ds = p * (dp - jnp.sum(p * dp, 0, keepdims=True))
            db_ref[:, wide] += ds
            dsc = (ds * SCALE).astype(BF16)
            store(dqkv_ref, w, k_lanes, dot_nn(dsc, q4).astype(BF16))
            dq = fold(dot_tn(dsc, load(qkv_ref, w, k_lanes)))
            store(dqkv_ref, w, q_lanes, dq.astype(BF16))
            return carry

        lax.fori_loop(0, WB, step, 0, unroll=6)
        for k in (g, 3 + g, 6 + g):
            grad_ref[k] = dot_nn(ht_ref[...], dqkv_ref[:, 128 * k : 128 * k + 128])

    lax.fori_loop(0, WB, forward, 0, unroll=2)

    halos[2].wait_recv()
    stage_rows([jnp.where(here_lower, hcot_ref[i].astype(F32), 0.0) for i in range(4)], 1, c_ref)
    pull(1)

    here = (band, grp, y, x, z, core)
    parts = []
    at = 0
    for rows, count, na in PARTS:
        parts.append(Part(rows, count, na, rest[at : at + 20], here, send, (grad_ref, bt_ref)))
        at += 20
    first, second = parts
    share = Share(f_ref, r3_ref, z_s, z_r, here)

    proj = dot_tn(o_ref[...], dz_ref[...])
    for k in range(3):
        grad_ref[9 + k] = proj[:, 128 * k : 128 * k + 128]
    backward(0)
    first.start()
    for i in range(8):
        f_ref[i, SLOTS:16, :] = jnp.zeros((16 - SLOTS, 128), F32)
    backward(1)
    for r in far:
        pl.semaphore_wait(near_sem.at[r], 2)
    first.spread()
    backward(2)
    for i in range(6):
        bt_ref[128 * i : 128 * i + 128, 0:64] = db_ref[:, 128 * i : 128 * i + 128].T
    second.start()
    first.turn()

    wide_mask = jnp.concatenate([mask_ref[...]] * 3, 1)
    x_ref[...] = wide_mask * dot_nn(o_ref[...], wproj_ref[...])
    second.spread()
    for i in range(4):
        uu_ref[i] = grid_row(x_ref, 1, i).astype(BF16)
    halo_u = send(uu_ref, hu_ref, halo_s.at[3], halo_r.at[3], after_id)
    c_ref[...] = dot_nt(dqkv_ref[...], wqkv_ref[...])

    def back(i, carry):
        rows = pl.ds(pl.multiple_of(i * 64, 64), 64)
        dh = c_ref[rows, :]
        n = n_ref[rows, :]
        inv = jnp.concatenate([inv_ref[rows, :]] * 3, 1)
        slope = jnp.mean(dh * n, -1, keepdims=True)
        c_ref[rows, :] = inv * (dh - jnp.mean(dh, -1, keepdims=True) - n * slope)
        return carry

    lax.fori_loop(0, WB, back, 0, unroll=3)
    for i in range(4):
        ug_ref[i] = grid_row(c_ref, 1, i).astype(BF16)
    halo_g = send(ug_ref, hg_ref, halo_s.at[4], halo_r.at[4], after_id)
    second.turn()
    first.collect(f_ref)
    for i in range(4):
        row = grid_row(x_ref, 0, i).astype(BF16).astype(F32)
        block_ref[4 + i] = (tok_ref[4 + i].astype(F32) + row).astype(BF16)
        row = grid_row(c_ref, 0, i).astype(BF16).astype(F32)
        grad_out_ref[4 + i] = (cot_ref[4 + i].astype(F32) + row).astype(BF16)
    upper, lower = pl.ds(4, 4), pl.ds(0, 4)
    keep(block_ref.at[upper], block_hbm.at[upper])
    keep(grad_out_ref.at[upper], grad_hbm.at[upper])
    second.collect(f_ref)
    share.start()
    inner = jnp.broadcast_to(linear, (4, 48, C)) > 0
    halo_u.wait_recv()
    low = jnp.where(inner, hu_ref[...].astype(F32), 0.0)
    block_ref[0:4] = (tok_ref[0:4].astype(F32) + low).astype(BF16)
    keep(block_ref.at[lower], block_hbm.at[lower])
    halo_g.wait_recv()
    low = jnp.where(inner, hg_ref[...].astype(F32), 0.0)
    grad_out_ref[0:4] = (cot_ref[0:4].astype(F32) + low).astype(BF16)
    keep(grad_out_ref.at[lower], grad_hbm.at[lower])
    for part in parts:
        part.drain()
    share.finish(red_ref)
    keep(red_ref, red_hbm)
    share.drain()
    for copy in halos + [halo_u, halo_g]:
        copy.wait_send()
    for copy in kept:
        copy.wait()


def place_kernel(
    block_hbm, grad_hbm, red_hbm, block_out, grad_out, qkv_out, proj_out, bias_out,
    block_ref, grad_ref, red_ref, in_sem, out_sem,
):
    load = pltpu.make_async_copy(red_hbm, red_ref, in_sem.at[4])
    load.start()
    moves = []
    for i, (src, via, dst) in enumerate(((block_hbm, block_ref, block_out), (grad_hbm, grad_ref, grad_out))):
        for j in range(2):
            part = pl.ds(4 * j, 4)
            into = pltpu.make_async_copy(src.at[part], via.at[part], in_sem.at[2 * i + j])
            into.start()
            moves.append((into, pltpu.make_async_copy(via.at[part], dst.at[part], out_sem.at[2 * i + j])))
    load.wait()
    for into, out in moves:
        into.wait()
        out.start()
    g = lax.rem(lax.axis_index("grp"), 4)
    lane = lax.broadcasted_iota(jnp.int32, (16, 128), 1)
    red = red_ref[...]
    following = jnp.concatenate([red[1:16], red[0:1]], 0)
    rolled = [red]
    for quarter in range(1, 4):
        shift = 128 - 32 * quarter
        value = jnp.where(lane < shift, pltpu.roll(red, shift, 1), pltpu.roll(following, shift, 1))
        rolled.append(value)

    def pick(step):
        which = jnp.broadcast_to(lax.rem(step * g, 4), (16, 128))
        value = rolled[0]
        for quarter in range(1, 4):
            value = jnp.where(which == quarter, rolled[quarter], value)
        return value

    for out, step, first, size in ((qkv_out, 27, 0, 864), (proj_out, 9, 8, 288), (bias_out, 3, 11, 96)):
        value = pick(step)
        for i in range(-(-size // 128)):
            n = min(128, size - 128 * i)
            out[pl.ds(128 * i, n)] = value[first + i, 0:n]
    for into, out in moves:
        out.wait()


def local(tokens, cotangent, ocean_mask, land_mask, w_qkv, w_proj, rel_bias):
    grid = jax.ShapeDtypeStruct((8, 48, C), BF16)
    dma = pltpu.SemaphoreType.DMA
    half = pltpu.VMEM((4, 48, C), BF16)
    scratch = [
        pltpu.VMEM((8, 48, C), BF16),
        pltpu.VMEM((8, 48, C), BF16),
        pltpu.VMEM((16, 128), F32),
        pltpu.VMEM((8, 48, C), BF16),
        pltpu.VMEM((8, 48, C), BF16),
        pltpu.VMEM((8, 48), jnp.int32),
        pltpu.VMEM((1, 6), jnp.int32),
        pltpu.VMEM((C, 3 * C), BF16),
        pltpu.VMEM((C, C), BF16),
        pltpu.VMEM((12, 64, 64), F32),
        half, half, pltpu.VMEM((8, 48), jnp.int32), half, half, half, half,
        pltpu.VMEM((C, C), F32),
        pltpu.VMEM((C, C), F32),
        pltpu.VMEM((C, C), F32),
        pltpu.VMEM((C, 128), F32),
        pltpu.VMEM((C, 128), F32),
        pltpu.VMEM((C, C), BF16),
        pltpu.VMEM((C, C), BF16),
        pltpu.VMEM((C, 3 * C), BF16),
        pltpu.VMEM((C, C), BF16),
        pltpu.VMEM((C, C), BF16),
        pltpu.VMEM((C, C), BF16),
        pltpu.VMEM((C, 3 * C), BF16),
        pltpu.VMEM((C, 768), F32),
        pltpu.VMEM((64, 768), F32),
        pltpu.VMEM((64, 768), F32),
        pltpu.VMEM((12, C, 128), F32),
        pltpu.VMEM((768, 128), F32),
        pltpu.VMEM((8, 16, 128), F32),
        pltpu.VMEM((NZ, 16, 128), F32),
        dma((7,)), dma((5,)), dma((5,)), dma((5,)), dma((8,)), dma((NZ,)),
        pltpu.SemaphoreType.REGULAR((5,)),
    ]
    for rows, count, na in PARTS:
        scratch += part_scratch(count, na)
    block_out, token_grad, red = pl.pallas_call(
        kernel,
        out_shape=[grid, grid, jax.ShapeDtypeStruct((16, 128), F32)],
        in_specs=[pl.BlockSpec(memory_space=pltpu.HBM)] * 7,
        out_specs=[pl.BlockSpec(memory_space=pltpu.HBM)] * 3,
        scratch_shapes=scratch,
        compiler_params=pltpu.CompilerParams(
            collective_id=0, has_side_effects=True, vmem_limit_bytes=VMEM_BYTES
        ),
        cost_estimate=pl.CostEstimate(flops=15 * 10**8, bytes_accessed=5 * 10**6, transcendentals=300000),
        name="window_block",
    )(tokens, cotangent, ocean_mask, land_mask, w_qkv, w_proj, rel_bias)

    whole = pl.BlockSpec(memory_space=pltpu.VMEM)
    hbm = pl.BlockSpec(memory_space=pltpu.HBM)
    return tuple(
        pl.pallas_call(
            place_kernel,
            out_shape=[grid, grid] + [jax.ShapeDtypeStruct((n,), F32) for n in (864, 288, 96)],
            in_specs=[hbm] * 3,
            out_specs=[hbm, hbm, whole, whole, whole],
            scratch_shapes=[
                pltpu.VMEM((8, 48, C), BF16),
                pltpu.VMEM((8, 48, C), BF16),
                pltpu.VMEM((16, 128), F32),
                dma((5,)),
                dma((4,)),
            ],
            compiler_params=pltpu.CompilerParams(vmem_limit_bytes=VMEM_BYTES),
            cost_estimate=pl.CostEstimate(flops=10**4, bytes_accessed=12 * 10**5, transcendentals=0),
            name="outputs",
        )(block_out, token_grad, red)
    )


def solution(mesh):
    split = ("band", "grp")
    placed = (
        P(split, None, None),
        P(split, None, None),
        P(split, None),
        P(split, None),
        P(),
        P(),
        P(),
    )
    return jax.shard_map(
        local,
        mesh=mesh,
        in_specs=placed,
        out_specs=(P(split, None, None), P(split, None, None), P(split), P(split), P(split)),
        check_vma=False,
    )
```

```python
import math

import jax
import jax.numpy as jnp
from jax import lax
from jax.experimental import pallas as pl
from jax.experimental.pallas import tpu as pltpu
from jax.sharding import PartitionSpec as P

EPS = 1e-05
MASKED = -1e30
C = 384
WB = 6
HG = 3
SCALE = 1.0 / math.sqrt(32)
F32 = jnp.float32
BF16 = jnp.bfloat16
MESH = pl.DeviceIdType.MESH

NY, NX, NZ = 8, 4, 8
OWN = 192
VMEM_BYTES = 62 * 2**20


def qkv_rows(g):
    return [("qkv", j, k) for k in (g, 3 + g, 6 + g) for j in range(3)]


PROJ_ROWS = [("proj", j, k) for k in range(3) for j in range(3)]
BIAS_ROWS = [("bias", j, 0) for j in range(3)]
GROUPS = [PROJ_ROWS + qkv_rows(0), qkv_rows(1), qkv_rows(2) + BIAS_ROWS]
TURNS = [[0], [1, 2]]
PADDED = 24
SLOTS = 13


def owned(g):
    qkv = [min(27 * g // 4 + i, 26) for i in range(8)]
    proj = [min(9 * g // 4 + i, 8) for i in range(3)]
    bias = [min(3 * g // 4 + i, 2) for i in range(2)]
    return (
        [("qkv", r // 9, r % 9) for r in qkv]
        + [("proj", r // 3, r % 3) for r in proj]
        + [("bias", r, 0) for r in bias]
    )


def dot_nt(a, b):
    return lax.dot_general(a, b, (((1,), (1,)), ((), ())), preferred_element_type=F32)


def dot_tn(a, b):
    return lax.dot_general(a, b, (((0,), (0,)), ((), ())), preferred_element_type=F32)


def dot_nn(a, b):
    return lax.dot_general(a, b, (((1,), (0,)), ((), ())), preferred_element_type=F32)


def stage_mask(ocean, land, half, mask_ref):
    place = lax.broadcasted_iota(jnp.int32, (8, 48), 0)
    column = lax.broadcasted_iota(jnp.int32, (8, 48), 1)
    for w in range(WB):
        live = 1.0 - land[:, w : w + 1]
        pick = (column == lax.rem(place + (8 * w + 4), 48)).astype(F32) * live
        for i in range(4):
            row = jnp.broadcast_to(ocean[i : i + 1, :], (8, 48))
            value = jnp.sum(row * pick, axis=1, keepdims=True)
            at = OWN * half + 32 * w + 8 * i
            mask_ref[at : at + 8, :] = jnp.broadcast_to(value, (8, 128))


def stage_rows(rows, half, out_ref):
    for i, row in enumerate(rows):
        rolled = pltpu.roll(row.astype(F32), 44, 0)
        for w in range(WB):
            at = OWN * half + 32 * w + 8 * i
            out_ref[at : at + 8, :] = rolled[8 * w : 8 * w + 8, :]


def grid_row(src_ref, half, i):
    ats = [OWN * half + 32 * w + 8 * i for w in range(WB)]
    return pltpu.roll(jnp.concatenate([src_ref[at : at + 8, :] for at in ats], 0), 4, 0)


class Group:
    def __init__(self, rows, refs, here, send):
        self.rows, self.n, self.here, self.send = rows, len(rows), here, send
        (
            self.pk, self.pack, self.r0, self.s1, self.rx,
            self.core_s, self.core_r, self.x_s, self.x_r,
        ) = refs

    def start(self):
        band, grp, y, x, z, core = self.here
        theirs = pl.ds(pl.multiple_of((1 - core) * 64, 64), 64)

        def narrow(i, carry):
            self.pack[i] = self.pk[i, theirs, :].astype(BF16)
            return carry

        lax.fori_loop(0, self.n, narrow, 0, unroll=3)
        self.core_copy = self.send(
            self.pack, self.r0, self.core_s.at[0], self.core_r.at[0], (band, z * 2 + 1 - core)
        )

    def spread(self):
        band, grp, y, x, z, core = self.here
        mine = pl.ds(pl.multiple_of(core * 64, 64), 64)
        self.core_copy.wait()

        def add(i, carry):
            self.s1[i] = (self.pk[i, mine, :] + self.r0[i].astype(F32)).astype(BF16)
            return carry

        lax.fori_loop(0, self.n, add, 0, unroll=3)
        self.sent = []
        for d in range(1, NX):
            to = lax.rem(x + d, NX)
            self.sent.append(
                self.send(
                    self.s1.at[:, pl.ds(pl.multiple_of(16 * to, 16), 16), :], self.rx.at[d - 1],
                    self.x_s.at[d - 1], self.x_r.at[d - 1], (y * NX + to, grp),
                )
            )

    def turn(self, tb_ref, base):
        band, grp, y, x, z, core = self.here
        total = self.s1[:, pl.ds(pl.multiple_of(16 * x, 16), 16), :].astype(F32)
        for d in range(1, NX):
            self.sent[d - 1].wait_recv()
            total = total + self.rx[d - 1].astype(F32)
        for i in range(self.n):
            for quarter in range(2):
                at = pl.ds(quarter * PADDED + base + i, NY, stride=2 * PADDED)
                tb_ref[at, :] = total[i, 8 * quarter : 8 * quarter + 8, :]


class Turn:
    def __init__(self, groups, refs, here, send):
        self.groups, self.here, self.send = groups, here, send
        self.rows = [row for group in groups for row in group.rows]
        self.wide, self.tb, self.ry, self.y_s, self.y_r = refs

    def clear(self):
        for i in range(len(self.rows), PADDED):
            for quarter in range(2):
                at = pl.ds(quarter * PADDED + i, NY, stride=2 * PADDED)
                self.wide[at, :] = jnp.zeros((NY, 128), F32)

    def start(self):
        band, grp, y, x, z, core = self.here
        base = 0
        for group in self.groups:
            group.turn(self.wide, base)
            base += group.n
        for i in range(NY):
            self.tb[i] = self.wide[2 * PADDED * i : 2 * PADDED * (i + 1), :].astype(BF16)
        self.sent = []
        for d in range(1, NY):
            to = lax.rem(y + d, NY)
            self.sent.append(
                self.send(
                    self.tb.at[to], self.ry.at[d - 1],
                    self.y_s.at[d - 1], self.y_r.at[d - 1], (to * NX + x, grp),
                )
            )

    def collect(self, f_ref):
        band, grp, y, x, z, core = self.here
        total = self.wide[pl.ds(pl.multiple_of(y * 2 * PADDED, 8), 2 * PADDED), :]
        for d in range(1, NY):
            self.sent[d - 1].wait_recv()
            total = total + self.ry[d - 1].astype(F32)
        for i in range(8):
            for at, row in enumerate(owned(i % 4)):
                if row in self.rows:
                    first = PADDED * (i // 4) + self.rows.index(row)
                    f_ref[i, at : at + 1, :] = total[first : first + 1, :]


class Share:
    def __init__(self, f_ref, r3_ref, z_s, z_r, here):
        self.f, self.r3, self.z_s, self.z_r, self.here = f_ref, r3_ref, z_s, z_r, here

    def last(self, i):
        band, grp, y, x, z, core = self.here
        quarter, zi, to_core = i // 4, (i // 2) % 2, i % 2
        to_z = 2 * (2 * core + quarter) + zi
        copy = pltpu.make_async_remote_copy(
            src_ref=self.f.at[i],
            dst_ref=self.r3.at[z],
            send_sem=self.z_s.at[i],
            recv_sem=self.z_r.at[z],
            device_id=(band, to_z * 2 + to_core),
            device_id_type=MESH,
        )
        return copy, jnp.logical_or(to_z != z, core != to_core)

    def start(self):
        for i in range(8):
            copy, away = self.last(i)
            pl.when(away)(copy.start)

    def finish(self, red_ref):
        band, grp, y, x, z, core = self.here
        own_core = z // 4

        @pl.when(core == own_core)
        def _():
            self.r3[z] = self.f[4 * lax.rem(z // 2, 2) + lax.rem(grp, 4)]

        for s in range(NZ):
            come = pltpu.make_async_remote_copy(
                src_ref=self.f.at[0],
                dst_ref=self.r3.at[s],
                send_sem=self.z_s.at[0],
                recv_sem=self.z_r.at[s],
                device_id=(band, z * 2 + 1 - core),
                device_id_type=MESH,
            )
            pl.when(jnp.logical_or(z != s, core != own_core))(come.wait_recv)
        total = self.r3[0]
        for s in range(1, NZ):
            total = total + self.r3[s]
        red_ref[...] = total

    def drain(self):
        for i in range(8):
            copy, away = self.last(i)
            pl.when(away)(copy.wait_send)


def group_scratch(n):
    dma = pltpu.SemaphoreType.DMA
    return [
        pltpu.VMEM((n, 128, 128), F32),
        pltpu.VMEM((n, 64, 128), BF16),
        pltpu.VMEM((n, 64, 128), BF16),
        pltpu.VMEM((n, 64, 128), BF16),
        pltpu.VMEM((NX - 1, n, 16, 128), BF16),
        dma((1,)), dma((1,)), dma((NX - 1,)), dma((NX - 1,)),
    ]


def turn_scratch():
    dma = pltpu.SemaphoreType.DMA
    return [
        pltpu.VMEM((NY * 2 * PADDED, 128), F32),
        pltpu.VMEM((NY, 2 * PADDED, 128), BF16),
        pltpu.VMEM((NY - 1, 2 * PADDED, 128), BF16),
        dma((NY - 1,)), dma((NY - 1,)),
    ]


def permutation():
    at = lax.broadcasted_iota(jnp.int32, (C, C), 0)
    feature = lax.broadcasted_iota(jnp.int32, (C, C), 1)

    def bits(low, count):
        return lax.bitwise_and(lax.shift_right_logical(at, jnp.full_like(at, low)), (1 << count) - 1)

    m = 16 * bits(0, 3) + bits(3, 1) + 4 * bits(4, 2) + 2 * bits(6, 1)
    return (feature == 3 * m + bits(7, 2)).astype(F32).astype(BF16)


def kernel(
    tok_hbm, cot_hbm, oce_hbm, land_hbm, wqkv_hbm, wproj_hbm, rb_hbm,
    block_hbm, grad_hbm, red_hbm,
    block_ref, grad_out_ref, red_ref,
    tok_ref, cot_ref, oce_ref, land_ref, wqkv_ref, wproj_ref, rb_ref,
    htok_ref, hcot_ref, hoce_ref, uu_ref, ug_ref, hu_ref, hg_ref,
    x_ref, c_ref, n_ref, inv_ref, mask_ref, h_ref, ht_ref, qkv_ref, dz_ref, do_ref, o_ref, dqkv_ref, ot_ref,
    p_ref, bias_ref, db_ref, perm_ref, bt_ref, f_ref, r3_ref, load_sem, store_sem, halo_s, halo_r, z_s, z_r, near_sem, *rest,
):
    band = lax.axis_index("band")
    grp = lax.axis_index("grp")
    y, x = band // NX, lax.rem(band, NX)
    z, core = grp // 2, lax.rem(grp, 2)
    linear = band * 16 + grp
    after = lax.rem(linear + 1, 512)
    before = lax.rem(linear + 511, 512)
    after_id = (after // 16, lax.rem(after, 16))
    before_id = (before // 16, lax.rem(before, 16))

    def blocks(ref, i, j):
        return ref.at[:, pl.ds(C * i + 128 * j, 128)]

    loads = []
    for i, (src, dst) in enumerate(
        [(tok_hbm, tok_ref), (oce_hbm, oce_ref), (land_hbm, land_ref), (cot_hbm, cot_ref)]
        + [(wproj_hbm, wproj_ref), (rb_hbm, rb_ref)]
        + [(blocks(wqkv_hbm, i, j), blocks(wqkv_ref, j, i)) for j in range(HG) for i in range(3)]
    ):
        loads.append(pltpu.make_async_copy(src, dst, load_sem.at[i]))
        loads[-1].start()

    barrier = pltpu.get_barrier_semaphore()


    def at_z(d):
        return (band, lax.rem(z + NZ + d, NZ) * 2 + core)

    def at_y(d):
        return (lax.rem(y + NY + d, NY) * NX + x, grp)

    def at_x(d):
        return (y * NX + lax.rem(x + NX + d, NX), grp)

    peers = [after_id, before_id, (band, z * 2 + 1 - core)]
    peers += [at(d) for at in (at_z, at_y, at_x) for d in (1, -1)]
    for peer in peers:
        pl.semaphore_signal(barrier, inc=1, device_id=peer, device_id_type=MESH)

    def tell(r, at, d):
        for to in (at(d), at(-d)):
            pl.semaphore_signal(near_sem.at[r], inc=1, device_id=to, device_id_type=MESH)

    def send(src, dst, s, r, to):
        copy = pltpu.make_async_remote_copy(
            src_ref=src, dst_ref=dst, send_sem=s, recv_sem=r, device_id=to, device_id_type=MESH
        )
        copy.start()
        return copy

    kept = []

    def keep(src, dst):
        kept.append(pltpu.make_async_copy(src, dst, store_sem.at[len(kept)]))
        kept[-1].start()

    loads[0].wait()
    stage_rows([tok_ref[4 + i] for i in range(4)], 0, x_ref)
    perm_ref[...] = permutation()

    pl.semaphore_wait(barrier, len(peers))
    tell(0, at_z, 1)
    tell(1, at_y, 1)
    tell(2, at_x, 1)
    far = (2, 3, 4)
    halos = [
        send(tok_hbm.at[pl.ds(0, 4)], htok_ref, halo_s.at[0], halo_r.at[0], before_id),
        send(oce_hbm, hoce_ref, halo_s.at[1], halo_r.at[1], before_id),
        send(cot_hbm.at[pl.ds(0, 4)], hcot_ref, halo_s.at[2], halo_r.at[2], before_id),
    ]

    def norm(i, carry):
        rows = pl.ds(pl.multiple_of(i * 64, 64), 64)
        value = x_ref[rows, :]
        centered = value - jnp.mean(value, -1, keepdims=True)
        inv = lax.rsqrt(jnp.mean(centered * centered, -1, keepdims=True) + EPS)
        n = centered * inv
        n_ref[rows, :] = n
        inv_ref[rows, :] = jnp.broadcast_to(inv, (64, 128))
        h_ref[rows, :] = n.astype(BF16)
        return carry

    def project(half):
        rows = slice(OWN * half, OWN * half + OWN)
        qkv_ref[rows, :] = dot_nn(h_ref[rows, :], wqkv_ref[...]).astype(BF16)

    def pull(half):
        rows = slice(OWN * half, OWN * half + OWN)
        wide = jnp.concatenate([mask_ref[rows, :]] * 3, 1)
        dz_ref[rows, :] = (wide * c_ref[rows, :]).astype(BF16)
        do_ref[rows, :] = dot_nt(dz_ref[rows, :], wproj_ref[...]).astype(BF16)

    lax.fori_loop(0, 3, norm, 0, unroll=3)
    loads[1].wait()
    loads[2].wait()
    land = land_ref[...].astype(F32)
    stage_mask(oce_ref[4:8, :].astype(F32), land, 0, mask_ref)
    for i in range(6, 15):
        loads[i].wait()
    project(0)
    loads[3].wait()
    stage_rows([cot_ref[4 + i] for i in range(4)], 0, c_ref)
    loads[4].wait()
    pull(0)
    loads[5].wait()
    for i in range(6):
        pair = jnp.concatenate([rb_ref[2 * i], rb_ref[2 * i + 1]], 0)
        bias_ref[:, 128 * i : 128 * i + 128] = pair.T
    db_ref[...] = jnp.zeros_like(db_ref)

    here_lower = jnp.broadcast_to(linear, (48, C)) < 511
    halos[0].wait_recv()
    stage_rows([jnp.where(here_lower, htok_ref[i].astype(F32), 0.0) for i in range(4)], 1, x_ref)
    lax.fori_loop(3, 6, norm, 0, unroll=3)
    project(1)
    for r in (0, 1):
        pl.semaphore_wait(near_sem.at[r], 2)
    tell(3, at_z, 2)
    tell(4, at_y, 2)
    ht_ref[...] = dot_nt(perm_ref[...], h_ref[...]).astype(BF16)
    halos[1].wait_recv()
    ocean = jnp.where(jnp.broadcast_to(linear, (4, 48)) < 511, hoce_ref[0:4, :].astype(F32), 0.0)
    stage_mask(ocean, land, 1, mask_ref)

    head = lax.broadcasted_iota(jnp.int32, (64, 128), 1) // 32
    picks = [(head == i).astype(F32) for i in range(4)]
    picks_low = [p.astype(BF16) for p in picks]

    def spread(a):
        return jnp.concatenate([a * p for p in picks_low], 0)

    def fold(value):
        total = value[0:64] * picks[0]
        for i in range(1, 4):
            total = total + value[64 * i : 64 * i + 64] * picks[i]
        return total

    def two(w):
        first = pl.ds(pl.multiple_of(w * 32, 32), 32)
        second = pl.ds(pl.multiple_of(OWN + w * 32, 32), 32)
        return first, second

    def load(ref, w, lanes):
        first, second = two(w)
        return jnp.concatenate([ref[first, lanes], ref[second, lanes]], 0)

    def store(ref, w, lanes, value):
        first, second = two(w)
        ref[first, lanes] = value[0:32]
        ref[second, lanes] = value[32:64]

    def lanes_of(g):
        return [slice(C * g + 128 * i, C * g + 128 * i + 128) for i in range(3)] + [
            slice(256 * g, 256 * g + 256)
        ]

    def forward(w, carry):
        whole = pl.ds(pl.multiple_of(w * 64, 64), 64)
        live = jnp.concatenate([load(mask_ref, w, slice(0, 128))] * 2, 1) > 0.5
        for g in range(HG):
            q_lanes, k_lanes, v_lanes, wide = lanes_of(g)
            q4 = spread(load(qkv_ref, w, q_lanes))
            s = dot_nt(load(qkv_ref, w, k_lanes), q4) * SCALE + bias_ref[:, wide]
            s = jnp.where(live, s, MASKED)
            weights = jnp.exp(s - jnp.max(s, 0, keepdims=True))
            p = weights * (1.0 / jnp.sum(weights, 0, keepdims=True))
            p_ref[whole, wide] = p
            store(o_ref, w, slice(128 * g, 128 * g + 128), fold(dot_tn(p.astype(BF16), load(qkv_ref, w, v_lanes))).astype(BF16))
        return carry

    def backward(g):
        q_lanes, k_lanes, v_lanes, wide = lanes_of(g)

        def step(w, carry):
            whole = pl.ds(pl.multiple_of(w * 64, 64), 64)
            q4 = spread(load(qkv_ref, w, q_lanes))
            do4 = spread(load(do_ref, w, slice(128 * g, 128 * g + 128)))
            p = p_ref[whole, wide]
            dp = dot_nt(load(qkv_ref, w, v_lanes), do4)
            store(dqkv_ref, w, v_lanes, dot_nn(p.astype(BF16), do4).astype(BF16))
            ds = p * (dp - jnp.sum(p * dp, 0, keepdims=True))
            db_ref[:, wide] += ds
            dsc = (ds * SCALE).astype(BF16)
            store(dqkv_ref, w, k_lanes, dot_nn(dsc, q4).astype(BF16))
            dq = fold(dot_tn(dsc, load(qkv_ref, w, k_lanes)))
            store(dqkv_ref, w, q_lanes, dq.astype(BF16))
            return carry

        lax.fori_loop(0, WB, step, 0, unroll=6)
        fill(groups[g], dot_nn(ht_ref[...], dqkv_ref[:, C * g : C * g + C]), 9 if g == 0 else 0)

    lax.fori_loop(0, WB, forward, 0, unroll=2)

    halos[2].wait_recv()
    stage_rows([jnp.where(here_lower, hcot_ref[i].astype(F32), 0.0) for i in range(4)], 1, c_ref)
    pull(1)

    here = (band, grp, y, x, z, core)
    groups, turns = [], []
    at = 0
    for rows in GROUPS:
        groups.append(Group(rows, rest[at : at + 9], here, send))
        at += 9
    for members in TURNS:
        turns.append(Turn([groups[i] for i in members], rest[at : at + 5], here, send))
        at += 5
    share = Share(f_ref, r3_ref, z_s, z_r, here)

    def fill(group, value, base):
        for k in range(3):
            for j in range(3):
                group.pk[base + 3 * k + j] = value[128 * j : 128 * j + 128, 128 * k : 128 * k + 128]

    ot_ref[...] = dot_nt(perm_ref[...], o_ref[...]).astype(BF16)
    fill(groups[0], dot_nn(ot_ref[...], dz_ref[...]), 0)
    backward(0)
    groups[0].start()
    for i in range(8):
        f_ref[i, SLOTS:16, :] = jnp.zeros((16 - SLOTS, 128), F32)
    for turn in turns:
        turn.clear()
    backward(1)
    groups[1].start()
    for r in far:
        pl.semaphore_wait(near_sem.at[r], 2)
    groups[0].spread()
    backward(2)
    for i in range(6):
        bt_ref[128 * i : 128 * i + 128, 0:64] = db_ref[:, 128 * i : 128 * i + 128].T
    lane = lax.broadcasted_iota(jnp.int32, (8, 128), 1)
    for j in range(3):
        for i in range(16):
            first = 2 * j + 24 * ((i // 2) % 4) + 12 * (i // 8) + 6 * (i % 2)
            even = bt_ref[pl.ds(first, 8, stride=96), :]
            odd = bt_ref[pl.ds(first + 1, 8, stride=96), :]
            groups[2].pk[9 + j, 8 * i : 8 * i + 8, :] = jnp.where(lane < 64, even, pltpu.roll(odd, 64, 1))
    groups[2].start()
    groups[1].spread()

    wide_mask = jnp.concatenate([mask_ref[...]] * 3, 1)
    x_ref[...] = wide_mask * dot_nn(o_ref[...], wproj_ref[...])
    groups[2].spread()
    turns[0].start()
    for i in range(4):
        uu_ref[i] = grid_row(x_ref, 1, i).astype(BF16)
    c_ref[...] = dot_nt(dqkv_ref[...], wqkv_ref[...])

    def back(i, carry):
        rows = pl.ds(pl.multiple_of(i * 64, 64), 64)
        dh = c_ref[rows, :]
        n = n_ref[rows, :]
        inv = jnp.concatenate([inv_ref[rows, :]] * 3, 1)
        slope = jnp.mean(dh * n, -1, keepdims=True)
        c_ref[rows, :] = inv * (dh - jnp.mean(dh, -1, keepdims=True) - n * slope)
        return carry

    lax.fori_loop(0, WB, back, 0, unroll=3)
    for i in range(4):
        ug_ref[i] = grid_row(c_ref, 1, i).astype(BF16)
    turns[1].start()
    halo_u = send(uu_ref, hu_ref, halo_s.at[3], halo_r.at[3], after_id)
    halo_g = send(ug_ref, hg_ref, halo_s.at[4], halo_r.at[4], after_id)
    turns[0].collect(f_ref)
    for i in range(4):
        row = grid_row(x_ref, 0, i).astype(BF16).astype(F32)
        block_ref[4 + i] = (tok_ref[4 + i].astype(F32) + row).astype(BF16)
        row = grid_row(c_ref, 0, i).astype(BF16).astype(F32)
        grad_out_ref[4 + i] = (cot_ref[4 + i].astype(F32) + row).astype(BF16)
    upper, lower = pl.ds(4, 4), pl.ds(0, 4)
    keep(block_ref.at[upper], block_hbm.at[upper])
    keep(grad_out_ref.at[upper], grad_hbm.at[upper])
    turns[1].collect(f_ref)
    share.start()
    inner = jnp.broadcast_to(linear, (4, 48, C)) > 0
    halo_u.wait_recv()
    low = jnp.where(inner, hu_ref[...].astype(F32), 0.0)
    block_ref[0:4] = (tok_ref[0:4].astype(F32) + low).astype(BF16)
    keep(block_ref.at[lower], block_hbm.at[lower])
    halo_g.wait_recv()
    low = jnp.where(inner, hg_ref[...].astype(F32), 0.0)
    grad_out_ref[0:4] = (cot_ref[0:4].astype(F32) + low).astype(BF16)
    keep(grad_out_ref.at[lower], grad_hbm.at[lower])
    for one in groups + turns:
        for copy in one.sent:
            copy.wait_send()
    share.finish(red_ref)
    keep(red_ref, red_hbm)
    share.drain()
    for copy in halos + [halo_u, halo_g]:
        copy.wait_send()
    for copy in kept:
        copy.wait()


def place_kernel(
    block_hbm, grad_hbm, red_hbm, block_out, grad_out, qkv_out, proj_out, bias_out,
    block_ref, grad_ref, red_ref, in_sem, out_sem,
):
    load = pltpu.make_async_copy(red_hbm, red_ref, in_sem.at[4])
    load.start()
    moves = []
    for i, (src, via, dst) in enumerate(((block_hbm, block_ref, block_out), (grad_hbm, grad_ref, grad_out))):
        for j in range(2):
            part = pl.ds(4 * j, 4)
            into = pltpu.make_async_copy(src.at[part], via.at[part], in_sem.at[2 * i + j])
            into.start()
            moves.append((into, pltpu.make_async_copy(via.at[part], dst.at[part], out_sem.at[2 * i + j])))
    load.wait()
    for into, out in moves:
        into.wait()
        out.start()
    g = lax.rem(lax.axis_index("grp"), 4)
    lane = lax.broadcasted_iota(jnp.int32, (16, 128), 1)
    red = red_ref[...]
    following = jnp.concatenate([red[1:16], red[0:1]], 0)
    rolled = [red]
    for quarter in range(1, 4):
        shift = 128 - 32 * quarter
        value = jnp.where(lane < shift, pltpu.roll(red, shift, 1), pltpu.roll(following, shift, 1))
        rolled.append(value)

    def pick(step):
        which = jnp.broadcast_to(lax.rem(step * g, 4), (16, 128))
        value = rolled[0]
        for quarter in range(1, 4):
            value = jnp.where(which == quarter, rolled[quarter], value)
        return value

    for out, step, first, size in ((qkv_out, 27, 0, 864), (proj_out, 9, 8, 288), (bias_out, 3, 11, 96)):
        value = pick(step)
        for i in range(-(-size // 128)):
            n = min(128, size - 128 * i)
            out[pl.ds(128 * i, n)] = value[first + i, 0:n]
    for into, out in moves:
        out.wait()


def local(tokens, cotangent, ocean_mask, land_mask, w_qkv, w_proj, rel_bias):
    grid = jax.ShapeDtypeStruct((8, 48, C), BF16)
    dma = pltpu.SemaphoreType.DMA
    half = pltpu.VMEM((4, 48, C), BF16)
    scratch = [
        pltpu.VMEM((8, 48, C), BF16),
        pltpu.VMEM((8, 48, C), BF16),
        pltpu.VMEM((16, 128), F32),
        pltpu.VMEM((8, 48, C), BF16),
        pltpu.VMEM((8, 48, C), BF16),
        pltpu.VMEM((8, 48), jnp.int32),
        pltpu.VMEM((1, 6), jnp.int32),
        pltpu.VMEM((C, 3 * C), BF16),
        pltpu.VMEM((C, C), BF16),
        pltpu.VMEM((12, 64, 64), F32),
        half, half, pltpu.VMEM((8, 48), jnp.int32), half, half, half, half,
        pltpu.VMEM((C, C), F32),
        pltpu.VMEM((C, C), F32),
        pltpu.VMEM((C, C), F32),
        pltpu.VMEM((C, 128), F32),
        pltpu.VMEM((C, 128), F32),
        pltpu.VMEM((C, C), BF16),
        pltpu.VMEM((C, C), BF16),
        pltpu.VMEM((C, 3 * C), BF16),
        pltpu.VMEM((C, C), BF16),
        pltpu.VMEM((C, C), BF16),
        pltpu.VMEM((C, C), BF16),
        pltpu.VMEM((C, 3 * C), BF16),
        pltpu.VMEM((C, C), BF16),
        pltpu.VMEM((C, 768), F32),
        pltpu.VMEM((64, 768), F32),
        pltpu.VMEM((64, 768), F32),
        pltpu.VMEM((C, C), BF16),
        pltpu.VMEM((768, 128), F32),
        pltpu.VMEM((8, 16, 128), F32),
        pltpu.VMEM((NZ, 16, 128), F32),
        dma((15,)), dma((5,)), dma((5,)), dma((5,)), dma((8,)), dma((NZ,)),
        pltpu.SemaphoreType.REGULAR((5,)),
    ]
    for rows in GROUPS:
        scratch += group_scratch(len(rows))
    for members in TURNS:
        scratch += turn_scratch()
    block_out, token_grad, red = pl.pallas_call(
        kernel,
        out_shape=[grid, grid, jax.ShapeDtypeStruct((16, 128), F32)],
        in_specs=[pl.BlockSpec(memory_space=pltpu.HBM)] * 7,
        out_specs=[pl.BlockSpec(memory_space=pltpu.HBM)] * 3,
        scratch_shapes=scratch,
        compiler_params=pltpu.CompilerParams(
            collective_id=0, has_side_effects=True, vmem_limit_bytes=VMEM_BYTES
        ),
        cost_estimate=pl.CostEstimate(flops=15 * 10**8, bytes_accessed=5 * 10**6, transcendentals=300000),
        name="window_block",
    )(tokens, cotangent, ocean_mask, land_mask, w_qkv, w_proj, rel_bias)

    whole = pl.BlockSpec(memory_space=pltpu.VMEM)
    hbm = pl.BlockSpec(memory_space=pltpu.HBM)
    return tuple(
        pl.pallas_call(
            place_kernel,
            out_shape=[grid, grid] + [jax.ShapeDtypeStruct((n,), F32) for n in (864, 288, 96)],
            in_specs=[hbm] * 3,
            out_specs=[hbm, hbm, whole, whole, whole],
            scratch_shapes=[
                pltpu.VMEM((8, 48, C), BF16),
                pltpu.VMEM((8, 48, C), BF16),
                pltpu.VMEM((16, 128), F32),
                dma((5,)),
                dma((4,)),
            ],
            compiler_params=pltpu.CompilerParams(vmem_limit_bytes=VMEM_BYTES),
            cost_estimate=pl.CostEstimate(flops=10**4, bytes_accessed=12 * 10**5, transcendentals=0),
            name="outputs",
        )(block_out, token_grad, red)
    )


def solution(mesh):
    split = ("band", "grp")
    placed = (
        P(split, None, None),
        P(split, None, None),
        P(split, None),
        P(split, None),
        P(),
        P(),
        P(),
    )
    return jax.shard_map(
        local,
        mesh=mesh,
        in_specs=placed,
        out_specs=(P(split, None, None), P(split, None, None), P(split), P(split), P(split)),
        check_vma=False,
    )
```

```python
import math

import jax
import jax.numpy as jnp
from jax import lax
from jax.experimental import pallas as pl
from jax.experimental.pallas import tpu as pltpu
from jax.sharding import PartitionSpec as P

EPS = 1e-05
MASKED = -1e30
C = 384
WB = 6
HG = 3
SCALE = 1.0 / math.sqrt(32)
F32 = jnp.float32
BF16 = jnp.bfloat16
MESH = pl.DeviceIdType.MESH

NY, NX, NZ = 8, 4, 8
OWN = 192
VMEM_BYTES = 62 * 2**20


def qkv_rows(g):
    return [("qkv", j, k) for k in (g, 3 + g, 6 + g) for j in range(3)]


PROJ_ROWS = [("proj", j, k) for k in range(3) for j in range(3)]
BIAS_ROWS = [("bias", j, 0) for j in range(3)]
GROUPS = [PROJ_ROWS + qkv_rows(0), qkv_rows(1)[:8], qkv_rows(1)[8:] + qkv_rows(2) + BIAS_ROWS]
SLOTS = 13


def owned(g):
    qkv = [min(27 * g // 4 + i, 26) for i in range(8)]
    proj = [min(9 * g // 4 + i, 8) for i in range(3)]
    bias = [min(3 * g // 4 + i, 2) for i in range(2)]
    return (
        [("qkv", r // 9, r % 9) for r in qkv]
        + [("proj", r // 3, r % 3) for r in proj]
        + [("bias", r, 0) for r in bias]
    )


def dot_nt(a, b):
    return lax.dot_general(a, b, (((1,), (1,)), ((), ())), preferred_element_type=F32)


def dot_tn(a, b):
    return lax.dot_general(a, b, (((0,), (0,)), ((), ())), preferred_element_type=F32)


def dot_nn(a, b):
    return lax.dot_general(a, b, (((1,), (0,)), ((), ())), preferred_element_type=F32)


def stage_mask(ocean, land, half, mask_ref):
    place = lax.broadcasted_iota(jnp.int32, (8, 48), 0)
    column = lax.broadcasted_iota(jnp.int32, (8, 48), 1)
    for w in range(WB):
        live = 1.0 - land[:, w : w + 1]
        pick = (column == lax.rem(place + (8 * w + 4), 48)).astype(F32) * live
        for i in range(4):
            row = jnp.broadcast_to(ocean[i : i + 1, :], (8, 48))
            value = jnp.sum(row * pick, axis=1, keepdims=True)
            at = OWN * half + 32 * w + 8 * i
            mask_ref[at : at + 8, :] = jnp.broadcast_to(value, (8, 128))


def stage_rows(rows, half, out_ref):
    for i, row in enumerate(rows):
        rolled = pltpu.roll(row.astype(F32), 44, 0)
        for w in range(WB):
            at = OWN * half + 32 * w + 8 * i
            out_ref[at : at + 8, :] = rolled[8 * w : 8 * w + 8, :]


def grid_row(src_ref, half, i):
    ats = [OWN * half + 32 * w + 8 * i for w in range(WB)]
    return pltpu.roll(jnp.concatenate([src_ref[at : at + 8, :] for at in ats], 0), 4, 0)


class Group:
    def __init__(self, rows, refs, here, send):
        self.rows, self.n, self.here, self.send = rows, len(rows), here, send
        (
            self.pk, self.pack, self.r0, self.s1, self.rx,
            self.core_s, self.core_r, self.x_s, self.x_r,
        ) = refs

    def start(self):
        band, grp, y, x, z, core = self.here
        theirs = pl.ds(pl.multiple_of((1 - core) * 64, 64), 64)

        def narrow(i, carry):
            self.pack[i] = self.pk[i, theirs, :].astype(BF16)
            return carry

        lax.fori_loop(0, self.n, narrow, 0, unroll=3)
        self.core_copy = self.send(
            self.pack, self.r0, self.core_s.at[0], self.core_r.at[0], (band, z * 2 + 1 - core)
        )

    def spread(self):
        band, grp, y, x, z, core = self.here
        mine = pl.ds(pl.multiple_of(core * 64, 64), 64)
        self.core_copy.wait()

        def add(i, carry):
            self.s1[i] = (self.pk[i, mine, :] + self.r0[i].astype(F32)).astype(BF16)
            return carry

        lax.fori_loop(0, self.n, add, 0, unroll=3)
        self.sent = []
        for d in range(1, NX):
            to = lax.rem(x + d, NX)
            self.sent.append(
                self.send(
                    self.s1.at[:, pl.ds(pl.multiple_of(16 * to, 16), 16), :], self.rx.at[d - 1],
                    self.x_s.at[d - 1], self.x_r.at[d - 1], (y * NX + to, grp),
                )
            )

    def take(self, wide_ref, padded):
        band, grp, y, x, z, core = self.here
        total = self.s1[:, pl.ds(pl.multiple_of(16 * x, 16), 16), :].astype(F32)
        for d in range(1, NX):
            self.sent[d - 1].wait_recv()
            total = total + self.rx[d - 1].astype(F32)
        for i in range(self.n):
            for quarter in range(2):
                at = pl.ds(quarter * padded + i, NY, stride=2 * padded)
                wide_ref[at, :] = total[i, 8 * quarter : 8 * quarter + 8, :]


def padded_of(n):
    return -(-n // 8) * 8


class Turn:
    def __init__(self, group, refs, here, send):
        self.group, self.here, self.send = group, here, send
        self.rows, self.padded = group.rows, padded_of(group.n)
        self.wide, self.tb, self.ry, self.y_s, self.y_r = refs

    def clear(self):
        for i in range(len(self.rows), self.padded):
            for quarter in range(2):
                at = pl.ds(quarter * self.padded + i, NY, stride=2 * self.padded)
                self.wide[at, :] = jnp.zeros((NY, 128), F32)

    def start(self):
        band, grp, y, x, z, core = self.here
        n = 2 * self.padded
        self.group.take(self.wide, self.padded)
        for i in range(NY):
            self.tb[i] = self.wide[n * i : n * (i + 1), :].astype(BF16)
        self.sent = []
        for d in range(1, NY):
            to = lax.rem(y + d, NY)
            self.sent.append(
                self.send(
                    self.tb.at[to], self.ry.at[d - 1],
                    self.y_s.at[d - 1], self.y_r.at[d - 1], (to * NX + x, grp),
                )
            )

    def collect(self, f_ref):
        band, grp, y, x, z, core = self.here
        n = 2 * self.padded
        total = self.wide[pl.ds(pl.multiple_of(y * n, 8), n), :]
        for d in range(1, NY):
            self.sent[d - 1].wait_recv()
            total = total + self.ry[d - 1].astype(F32)
        for i in range(8):
            for at, row in enumerate(owned(i % 4)):
                if row in self.rows:
                    first = self.padded * (i // 4) + self.rows.index(row)
                    f_ref[i, at : at + 1, :] = total[first : first + 1, :]


class Share:
    def __init__(self, wide_ref, f_ref, r3_ref, z_s, z_r, here):
        self.wide, self.f, self.r3, self.z_s, self.z_r, self.here = wide_ref, f_ref, r3_ref, z_s, z_r, here

    def last(self, i):
        band, grp, y, x, z, core = self.here
        quarter, zi, to_core = i // 4, (i // 2) % 2, i % 2
        to_z = 2 * (2 * core + quarter) + zi
        copy = pltpu.make_async_remote_copy(
            src_ref=self.f.at[i],
            dst_ref=self.r3.at[z],
            send_sem=self.z_s.at[i],
            recv_sem=self.z_r.at[z],
            device_id=(band, to_z * 2 + to_core),
            device_id_type=MESH,
        )
        return copy, jnp.logical_or(to_z != z, core != to_core)

    def start(self):
        self.f[...] = self.wide[...].astype(BF16)
        for i in range(8):
            copy, away = self.last(i)
            pl.when(away)(copy.start)

    def finish(self, red_ref):
        band, grp, y, x, z, core = self.here
        own_core = z // 4

        @pl.when(core == own_core)
        def _():
            self.r3[z] = self.f[4 * lax.rem(z // 2, 2) + lax.rem(grp, 4)]

        for s in range(NZ):
            come = pltpu.make_async_remote_copy(
                src_ref=self.f.at[0],
                dst_ref=self.r3.at[s],
                send_sem=self.z_s.at[0],
                recv_sem=self.z_r.at[s],
                device_id=(band, z * 2 + 1 - core),
                device_id_type=MESH,
            )
            pl.when(jnp.logical_or(z != s, core != own_core))(come.wait_recv)
        total = self.r3[0].astype(F32)
        for s in range(1, NZ):
            total = total + self.r3[s].astype(F32)
        red_ref[...] = total

    def drain(self):
        for i in range(8):
            copy, away = self.last(i)
            pl.when(away)(copy.wait_send)


def group_scratch(n):
    dma = pltpu.SemaphoreType.DMA
    return [
        pltpu.VMEM((n, 128, 128), F32),
        pltpu.VMEM((n, 64, 128), BF16),
        pltpu.VMEM((n, 64, 128), BF16),
        pltpu.VMEM((n, 64, 128), BF16),
        pltpu.VMEM((NX - 1, n, 16, 128), BF16),
        dma((1,)), dma((1,)), dma((NX - 1,)), dma((NX - 1,)),
    ]


def turn_scratch(n):
    dma = pltpu.SemaphoreType.DMA
    wide = 2 * padded_of(n)
    return [
        pltpu.VMEM((NY * wide, 128), F32),
        pltpu.VMEM((NY, wide, 128), BF16),
        pltpu.VMEM((NY - 1, wide, 128), BF16),
        dma((NY - 1,)), dma((NY - 1,)),
    ]


def permutation():
    at = lax.broadcasted_iota(jnp.int32, (C, C), 0)
    feature = lax.broadcasted_iota(jnp.int32, (C, C), 1)

    def bits(low, count):
        return lax.bitwise_and(lax.shift_right_logical(at, jnp.full_like(at, low)), (1 << count) - 1)

    m = 16 * bits(0, 3) + bits(3, 1) + 4 * bits(4, 2) + 2 * bits(6, 1)
    return (feature == 3 * m + bits(7, 2)).astype(F32).astype(BF16)


def kernel(
    tok_hbm, cot_hbm, oce_hbm, land_hbm, wqkv_hbm, wproj_hbm, rb_hbm,
    block_hbm, grad_hbm, red_hbm,
    block_ref, grad_out_ref, red_ref,
    tok_ref, cot_ref, oce_ref, land_ref, wqkv_ref, wproj_ref, rb_ref,
    htok_ref, hcot_ref, hoce_ref, uu_ref, ug_ref, hu_ref, hg_ref,
    x_ref, c_ref, n_ref, inv_ref, mask_ref, h_ref, ht_ref, qkv_ref, dz_ref, do_ref, o_ref, dqkv_ref, ot_ref,
    p_ref, bias_ref, db_ref, perm_ref, bt_ref, f_ref, low_ref, r3_ref, load_sem, store_sem, halo_s, halo_r, z_s, z_r, near_sem, *rest,
):
    band = lax.axis_index("band")
    grp = lax.axis_index("grp")
    y, x = band // NX, lax.rem(band, NX)
    z, core = grp // 2, lax.rem(grp, 2)
    linear = band * 16 + grp
    after = lax.rem(linear + 1, 512)
    before = lax.rem(linear + 511, 512)
    after_id = (after // 16, lax.rem(after, 16))
    before_id = (before // 16, lax.rem(before, 16))

    barrier = pltpu.get_barrier_semaphore()


    def at_z(d):
        return (band, lax.rem(z + NZ + d, NZ) * 2 + core)

    def at_y(d):
        return (lax.rem(y + NY + d, NY) * NX + x, grp)

    def at_x(d):
        return (y * NX + lax.rem(x + NX + d, NX), grp)

    peers = [after_id, before_id, (band, z * 2 + 1 - core)]
    peers += [at(d) for at in (at_z, at_y, at_x) for d in (1, -1)]
    for peer in peers:
        pl.semaphore_signal(barrier, inc=1, device_id=peer, device_id_type=MESH)

    def blocks(ref, i, j):
        return ref.at[:, pl.ds(C * i + 128 * j, 128)]

    loads = []
    for i, (src, dst) in enumerate(
        [(tok_hbm, tok_ref), (oce_hbm, oce_ref), (land_hbm, land_ref), (cot_hbm, cot_ref)]
        + [(wproj_hbm, wproj_ref), (rb_hbm, rb_ref)]
        + [(blocks(wqkv_hbm, i, j), blocks(wqkv_ref, j, i)) for j in range(HG) for i in range(3)]
    ):
        loads.append(pltpu.make_async_copy(src, dst, load_sem.at[i]))
        loads[-1].start()

    def tell(r, at, d):
        for to in (at(d), at(-d)):
            pl.semaphore_signal(near_sem.at[r], inc=1, device_id=to, device_id_type=MESH)

    def send(src, dst, s, r, to):
        copy = pltpu.make_async_remote_copy(
            src_ref=src, dst_ref=dst, send_sem=s, recv_sem=r, device_id=to, device_id_type=MESH
        )
        copy.start()
        return copy

    kept = []

    def keep(src, dst):
        kept.append(pltpu.make_async_copy(src, dst, store_sem.at[len(kept)]))
        kept[-1].start()

    pl.semaphore_wait(barrier, len(peers))
    tell(0, at_z, 1)
    tell(1, at_y, 1)
    tell(2, at_x, 1)
    far = (2, 3, 4)
    halos = [
        send(tok_hbm.at[pl.ds(0, 4)], htok_ref, halo_s.at[0], halo_r.at[0], before_id),
        send(oce_hbm, hoce_ref, halo_s.at[1], halo_r.at[1], before_id),
        send(cot_hbm.at[pl.ds(0, 4)], hcot_ref, halo_s.at[2], halo_r.at[2], before_id),
    ]

    loads[0].wait()
    stage_rows([tok_ref[4 + i] for i in range(4)], 0, x_ref)
    perm_ref[...] = permutation()

    def norm(i, carry):
        rows = pl.ds(pl.multiple_of(i * 64, 64), 64)
        value = x_ref[rows, :]
        centered = value - jnp.mean(value, -1, keepdims=True)
        inv = lax.rsqrt(jnp.mean(centered * centered, -1, keepdims=True) + EPS)
        n = centered * inv
        n_ref[rows, :] = n
        inv_ref[rows, :] = jnp.broadcast_to(inv, (64, 128))
        h_ref[rows, :] = n.astype(BF16)
        return carry

    def project(half):
        rows = slice(OWN * half, OWN * half + OWN)
        qkv_ref[rows, :] = dot_nn(h_ref[rows, :], wqkv_ref[...]).astype(BF16)

    def pull(half):
        rows = slice(OWN * half, OWN * half + OWN)
        wide = jnp.concatenate([mask_ref[rows, :]] * 3, 1)
        dz_ref[rows, :] = (wide * c_ref[rows, :]).astype(BF16)
        do_ref[rows, :] = dot_nt(dz_ref[rows, :], wproj_ref[...]).astype(BF16)

    lax.fori_loop(0, 3, norm, 0, unroll=3)
    loads[1].wait()
    loads[2].wait()
    land = land_ref[...].astype(F32)
    stage_mask(oce_ref[4:8, :].astype(F32), land, 0, mask_ref)
    for i in range(6, 15):
        loads[i].wait()
    project(0)
    loads[3].wait()
    stage_rows([cot_ref[4 + i] for i in range(4)], 0, c_ref)
    loads[4].wait()
    pull(0)
    loads[5].wait()
    for i in range(6):
        pair = jnp.concatenate([rb_ref[2 * i], rb_ref[2 * i + 1]], 0)
        bias_ref[:, 128 * i : 128 * i + 128] = pair.T
    db_ref[...] = jnp.zeros_like(db_ref)

    here_lower = jnp.broadcast_to(linear, (48, C)) < 511
    halos[0].wait_recv()
    stage_rows([jnp.where(here_lower, htok_ref[i].astype(F32), 0.0) for i in range(4)], 1, x_ref)
    lax.fori_loop(3, 6, norm, 0, unroll=3)
    project(1)
    for r in (0, 1):
        pl.semaphore_wait(near_sem.at[r], 2)
    tell(3, at_z, 2)
    tell(4, at_y, 2)
    ht_ref[...] = dot_nt(perm_ref[...], h_ref[...]).astype(BF16)
    halos[1].wait_recv()
    ocean = jnp.where(jnp.broadcast_to(linear, (4, 48)) < 511, hoce_ref[0:4, :].astype(F32), 0.0)
    stage_mask(ocean, land, 1, mask_ref)

    head = lax.broadcasted_iota(jnp.int32, (64, 128), 1) // 32
    picks = [(head == i).astype(F32) for i in range(4)]
    picks_low = [p.astype(BF16) for p in picks]

    def spread(a):
        return jnp.concatenate([a * p for p in picks_low], 0)

    def fold(value):
        total = value[0:64] * picks[0]
        for i in range(1, 4):
            total = total + value[64 * i : 64 * i + 64] * picks[i]
        return total

    def two(w):
        first = pl.ds(pl.multiple_of(w * 32, 32), 32)
        second = pl.ds(pl.multiple_of(OWN + w * 32, 32), 32)
        return first, second

    def load(ref, w, lanes):
        first, second = two(w)
        return jnp.concatenate([ref[first, lanes], ref[second, lanes]], 0)

    def store(ref, w, lanes, value):
        first, second = two(w)
        ref[first, lanes] = value[0:32]
        ref[second, lanes] = value[32:64]

    def lanes_of(g):
        return [slice(C * g + 128 * i, C * g + 128 * i + 128) for i in range(3)] + [
            slice(256 * g, 256 * g + 256)
        ]

    def forward(w, carry):
        whole = pl.ds(pl.multiple_of(w * 64, 64), 64)
        live = jnp.concatenate([load(mask_ref, w, slice(0, 128))] * 2, 1) > 0.5
        for g in range(HG):
            q_lanes, k_lanes, v_lanes, wide = lanes_of(g)
            q4 = spread(load(qkv_ref, w, q_lanes))
            s = dot_nt(load(qkv_ref, w, k_lanes), q4) * SCALE + bias_ref[:, wide]
            s = jnp.where(live, s, MASKED)
            weights = jnp.exp(s - jnp.max(s, 0, keepdims=True))
            p = weights * (1.0 / jnp.sum(weights, 0, keepdims=True))
            p_ref[whole, wide] = p
            store(o_ref, w, slice(128 * g, 128 * g + 128), fold(dot_tn(p.astype(BF16), load(qkv_ref, w, v_lanes))).astype(BF16))
        return carry

    def backward(g):
        q_lanes, k_lanes, v_lanes, wide = lanes_of(g)

        def step(w, carry):
            whole = pl.ds(pl.multiple_of(w * 64, 64), 64)
            q4 = spread(load(qkv_ref, w, q_lanes))
            do4 = spread(load(do_ref, w, slice(128 * g, 128 * g + 128)))
            p = p_ref[whole, wide]
            dp = dot_nt(load(qkv_ref, w, v_lanes), do4)
            store(dqkv_ref, w, v_lanes, dot_nn(p.astype(BF16), do4).astype(BF16))
            ds = p * (dp - jnp.sum(p * dp, 0, keepdims=True))
            db_ref[:, wide] += ds
            dsc = (ds * SCALE).astype(BF16)
            store(dqkv_ref, w, k_lanes, dot_nn(dsc, q4).astype(BF16))
            dq = fold(dot_tn(dsc, load(qkv_ref, w, k_lanes)))
            store(dqkv_ref, w, q_lanes, dq.astype(BF16))
            return carry

        lax.fori_loop(0, WB, step, 0, unroll=6)
        fill(qkv_rows(g), dot_nn(ht_ref[...], dqkv_ref[:, C * g : C * g + C]))

    lax.fori_loop(0, WB, forward, 0, unroll=2)

    halos[2].wait_recv()
    stage_rows([jnp.where(here_lower, hcot_ref[i].astype(F32), 0.0) for i in range(4)], 1, c_ref)
    pull(1)

    here = (band, grp, y, x, z, core)
    groups, turns = [], []
    at = 0
    for rows in GROUPS:
        groups.append(Group(rows, rest[at : at + 9], here, send))
        at += 9
    for group in groups:
        turns.append(Turn(group, rest[at : at + 5], here, send))
        at += 5
    share = Share(f_ref, low_ref, r3_ref, z_s, z_r, here)

    def fill(rows, value):
        for i, row in enumerate(rows):
            j, k = i % 3, i // 3
            for group in groups:
                if row in group.rows:
                    at = group.rows.index(row)
                    group.pk[at] = value[128 * j : 128 * j + 128, 128 * k : 128 * k + 128]

    ot_ref[...] = dot_nt(perm_ref[...], o_ref[...]).astype(BF16)
    fill(PROJ_ROWS, dot_nn(ot_ref[...], dz_ref[...]))
    backward(0)
    groups[0].start()
    for i in range(8):
        f_ref[i, SLOTS:16, :] = jnp.zeros((16 - SLOTS, 128), F32)
    for turn in turns:
        turn.clear()
    backward(1)
    groups[1].start()
    for r in far:
        pl.semaphore_wait(near_sem.at[r], 2)
    groups[0].spread()
    backward(2)
    for i in range(6):
        bt_ref[128 * i : 128 * i + 128, 0:64] = db_ref[:, 128 * i : 128 * i + 128].T
    lane = lax.broadcasted_iota(jnp.int32, (8, 128), 1)
    for j in range(3):
        for i in range(16):
            first = 2 * j + 24 * ((i // 2) % 4) + 12 * (i // 8) + 6 * (i % 2)
            even = bt_ref[pl.ds(first, 8, stride=96), :]
            odd = bt_ref[pl.ds(first + 1, 8, stride=96), :]
            groups[2].pk[groups[2].n - 3 + j, 8 * i : 8 * i + 8, :] = jnp.where(lane < 64, even, pltpu.roll(odd, 64, 1))
    groups[2].start()
    groups[1].spread()

    wide_mask = jnp.concatenate([mask_ref[...]] * 3, 1)
    x_ref[...] = wide_mask * dot_nn(o_ref[...], wproj_ref[...])
    groups[2].spread()
    turns[0].start()
    for i in range(4):
        uu_ref[i] = grid_row(x_ref, 1, i).astype(BF16)
    c_ref[...] = dot_nt(dqkv_ref[...], wqkv_ref[...])

    def back(i, carry):
        rows = pl.ds(pl.multiple_of(i * 64, 64), 64)
        dh = c_ref[rows, :]
        n = n_ref[rows, :]
        inv = jnp.concatenate([inv_ref[rows, :]] * 3, 1)
        slope = jnp.mean(dh * n, -1, keepdims=True)
        c_ref[rows, :] = inv * (dh - jnp.mean(dh, -1, keepdims=True) - n * slope)
        return carry

    lax.fori_loop(0, WB, back, 0, unroll=3)
    for i in range(4):
        ug_ref[i] = grid_row(c_ref, 1, i).astype(BF16)
    turns[1].start()
    turns[2].start()
    halo_u = send(uu_ref, hu_ref, halo_s.at[3], halo_r.at[3], after_id)
    halo_g = send(ug_ref, hg_ref, halo_s.at[4], halo_r.at[4], after_id)
    turns[0].collect(f_ref)
    for i in range(4):
        row = grid_row(x_ref, 0, i).astype(BF16).astype(F32)
        block_ref[4 + i] = (tok_ref[4 + i].astype(F32) + row).astype(BF16)
        row = grid_row(c_ref, 0, i).astype(BF16).astype(F32)
        grad_out_ref[4 + i] = (cot_ref[4 + i].astype(F32) + row).astype(BF16)
    upper, lower = pl.ds(4, 4), pl.ds(0, 4)
    keep(block_ref.at[upper], block_hbm.at[upper])
    keep(grad_out_ref.at[upper], grad_hbm.at[upper])
    turns[1].collect(f_ref)
    turns[2].collect(f_ref)
    share.start()
    inner = jnp.broadcast_to(linear, (4, 48, C)) > 0
    halo_u.wait_recv()
    low = jnp.where(inner, hu_ref[...].astype(F32), 0.0)
    block_ref[0:4] = (tok_ref[0:4].astype(F32) + low).astype(BF16)
    keep(block_ref.at[lower], block_hbm.at[lower])
    halo_g.wait_recv()
    low = jnp.where(inner, hg_ref[...].astype(F32), 0.0)
    grad_out_ref[0:4] = (cot_ref[0:4].astype(F32) + low).astype(BF16)
    keep(grad_out_ref.at[lower], grad_hbm.at[lower])
    for one in groups + turns:
        for copy in one.sent:
            copy.wait_send()
    share.finish(red_ref)
    keep(red_ref, red_hbm)
    share.drain()
    for copy in halos + [halo_u, halo_g]:
        copy.wait_send()
    for copy in kept:
        copy.wait()


def place_kernel(
    block_hbm, grad_hbm, red_hbm, block_out, grad_out, qkv_out, proj_out, bias_out,
    block_ref, grad_ref, red_ref, in_sem, out_sem,
):
    load = pltpu.make_async_copy(red_hbm, red_ref, in_sem.at[4])
    load.start()
    moves = []
    for i, (src, via, dst) in enumerate(((block_hbm, block_ref, block_out), (grad_hbm, grad_ref, grad_out))):
        for j in range(2):
            part = pl.ds(4 * j, 4)
            into = pltpu.make_async_copy(src.at[part], via.at[part], in_sem.at[2 * i + j])
            into.start()
            moves.append((into, pltpu.make_async_copy(via.at[part], dst.at[part], out_sem.at[2 * i + j])))
    load.wait()
    for into, out in moves:
        into.wait()
        out.start()
    g = lax.rem(lax.axis_index("grp"), 4)
    lane = lax.broadcasted_iota(jnp.int32, (16, 128), 1)
    red = red_ref[...]
    following = jnp.concatenate([red[1:16], red[0:1]], 0)
    rolled = [red]
    for quarter in range(1, 4):
        shift = 128 - 32 * quarter
        value = jnp.where(lane < shift, pltpu.roll(red, shift, 1), pltpu.roll(following, shift, 1))
        rolled.append(value)

    def pick(step):
        which = jnp.broadcast_to(lax.rem(step * g, 4), (16, 128))
        value = rolled[0]
        for quarter in range(1, 4):
            value = jnp.where(which == quarter, rolled[quarter], value)
        return value

    for out, step, first, size in ((qkv_out, 27, 0, 864), (proj_out, 9, 8, 288), (bias_out, 3, 11, 96)):
        value = pick(step)
        for i in range(-(-size // 128)):
            n = min(128, size - 128 * i)
            out[pl.ds(128 * i, n)] = value[first + i, 0:n]
    for into, out in moves:
        out.wait()


def local(tokens, cotangent, ocean_mask, land_mask, w_qkv, w_proj, rel_bias):
    grid = jax.ShapeDtypeStruct((8, 48, C), BF16)
    dma = pltpu.SemaphoreType.DMA
    half = pltpu.VMEM((4, 48, C), BF16)
    scratch = [
        pltpu.VMEM((8, 48, C), BF16),
        pltpu.VMEM((8, 48, C), BF16),
        pltpu.VMEM((16, 128), F32),
        pltpu.VMEM((8, 48, C), BF16),
        pltpu.VMEM((8, 48, C), BF16),
        pltpu.VMEM((8, 48), jnp.int32),
        pltpu.VMEM((1, 6), jnp.int32),
        pltpu.VMEM((C, 3 * C), BF16),
        pltpu.VMEM((C, C), BF16),
        pltpu.VMEM((12, 64, 64), F32),
        half, half, pltpu.VMEM((8, 48), jnp.int32), half, half, half, half,
        pltpu.VMEM((C, C), F32),
        pltpu.VMEM((C, C), F32),
        pltpu.VMEM((C, C), F32),
        pltpu.VMEM((C, 128), F32),
        pltpu.VMEM((C, 128), F32),
        pltpu.VMEM((C, C), BF16),
        pltpu.VMEM((C, C), BF16),
        pltpu.VMEM((C, 3 * C), BF16),
        pltpu.VMEM((C, C), BF16),
        pltpu.VMEM((C, C), BF16),
        pltpu.VMEM((C, C), BF16),
        pltpu.VMEM((C, 3 * C), BF16),
        pltpu.VMEM((C, C), BF16),
        pltpu.VMEM((C, 768), F32),
        pltpu.VMEM((64, 768), F32),
        pltpu.VMEM((64, 768), F32),
        pltpu.VMEM((C, C), BF16),
        pltpu.VMEM((768, 128), F32),
        pltpu.VMEM((8, 16, 128), F32),
        pltpu.VMEM((8, 16, 128), BF16),
        pltpu.VMEM((NZ, 16, 128), BF16),
        dma((15,)), dma((5,)), dma((5,)), dma((5,)), dma((8,)), dma((NZ,)),
        pltpu.SemaphoreType.REGULAR((5,)),
    ]
    for rows in GROUPS:
        scratch += group_scratch(len(rows))
    for rows in GROUPS:
        scratch += turn_scratch(len(rows))
    block_out, token_grad, red = pl.pallas_call(
        kernel,
        out_shape=[grid, grid, jax.ShapeDtypeStruct((16, 128), F32)],
        in_specs=[pl.BlockSpec(memory_space=pltpu.HBM)] * 7,
        out_specs=[pl.BlockSpec(memory_space=pltpu.HBM)] * 3,
        scratch_shapes=scratch,
        compiler_params=pltpu.CompilerParams(
            collective_id=0, has_side_effects=True, vmem_limit_bytes=VMEM_BYTES
        ),
        cost_estimate=pl.CostEstimate(flops=15 * 10**8, bytes_accessed=5 * 10**6, transcendentals=300000),
        name="window_block",
    )(tokens, cotangent, ocean_mask, land_mask, w_qkv, w_proj, rel_bias)

    whole = pl.BlockSpec(memory_space=pltpu.VMEM)
    hbm = pl.BlockSpec(memory_space=pltpu.HBM)
    return tuple(
        pl.pallas_call(
            place_kernel,
            out_shape=[grid, grid] + [jax.ShapeDtypeStruct((n,), F32) for n in (864, 288, 96)],
            in_specs=[hbm] * 3,
            out_specs=[hbm, hbm, whole, whole, whole],
            scratch_shapes=[
                pltpu.VMEM((8, 48, C), BF16),
                pltpu.VMEM((8, 48, C), BF16),
                pltpu.VMEM((16, 128), F32),
                dma((5,)),
                dma((4,)),
            ],
            compiler_params=pltpu.CompilerParams(vmem_limit_bytes=VMEM_BYTES),
            cost_estimate=pl.CostEstimate(flops=10**4, bytes_accessed=12 * 10**5, transcendentals=0),
            name="outputs",
        )(block_out, token_grad, red)
    )


def solution(mesh):
    split = ("band", "grp")
    placed = (
        P(split, None, None),
        P(split, None, None),
        P(split, None),
        P(split, None),
        P(),
        P(),
        P(),
    )
    return jax.shard_map(
        local,
        mesh=mesh,
        in_specs=placed,
        out_specs=(P(split, None, None), P(split, None, None), P(split), P(split), P(split)),
        check_vma=False,
    )
```

```python
import math

import jax
import jax.numpy as jnp
from jax import lax
from jax.experimental import pallas as pl
from jax.experimental.pallas import tpu as pltpu
from jax.sharding import PartitionSpec as P

EPS = 1e-05
MASKED = -1e30
C = 384
WB = 6
HG = 3
SCALE = 1.0 / math.sqrt(32)
F32 = jnp.float32
BF16 = jnp.bfloat16
MESH = pl.DeviceIdType.MESH

NY, NX, NZ = 8, 4, 8
OWN = 192
VMEM_BYTES = 62 * 2**20


def qkv_rows(g):
    return [("qkv", j, k) for k in (g, 3 + g, 6 + g) for j in range(3)]


PROJ_ROWS = [("proj", j, k) for k in range(3) for j in range(3)]
BIAS_ROWS = [("bias", j, 0) for j in range(3)]
GROUPS = [PROJ_ROWS + qkv_rows(0), qkv_rows(1)[:8], qkv_rows(1)[8:] + qkv_rows(2) + BIAS_ROWS]
SLOTS = 13
X_ORDER = (2, 1, 3)
Y_ORDER = (4, 3, 5, 2, 6, 1, 7)


def owned(g):
    qkv = [min(27 * g // 4 + i, 26) for i in range(8)]
    proj = [min(9 * g // 4 + i, 8) for i in range(3)]
    bias = [min(3 * g // 4 + i, 2) for i in range(2)]
    return (
        [("qkv", r // 9, r % 9) for r in qkv]
        + [("proj", r // 3, r % 3) for r in proj]
        + [("bias", r, 0) for r in bias]
    )


def dot_nt(a, b):
    return lax.dot_general(a, b, (((1,), (1,)), ((), ())), preferred_element_type=F32)


def dot_tn(a, b):
    return lax.dot_general(a, b, (((0,), (0,)), ((), ())), preferred_element_type=F32)


def dot_nn(a, b):
    return lax.dot_general(a, b, (((1,), (0,)), ((), ())), preferred_element_type=F32)


def stage_mask(ocean, land, half, mask_ref):
    place = lax.broadcasted_iota(jnp.int32, (8, 48), 0)
    column = lax.broadcasted_iota(jnp.int32, (8, 48), 1)
    for w in range(WB):
        live = 1.0 - land[:, w : w + 1]
        pick = (column == lax.rem(place + (8 * w + 4), 48)).astype(F32) * live
        for i in range(4):
            row = jnp.broadcast_to(ocean[i : i + 1, :], (8, 48))
            value = jnp.sum(row * pick, axis=1, keepdims=True)
            at = OWN * half + 32 * w + 8 * i
            mask_ref[at : at + 8, :] = jnp.broadcast_to(value, (8, 128))


def stage_rows(rows, half, out_ref):
    for i, row in enumerate(rows):
        rolled = pltpu.roll(row.astype(F32), 44, 0)
        for w in range(WB):
            at = OWN * half + 32 * w + 8 * i
            out_ref[at : at + 8, :] = rolled[8 * w : 8 * w + 8, :]


def grid_row(src_ref, half, i):
    ats = [OWN * half + 32 * w + 8 * i for w in range(WB)]
    return pltpu.roll(jnp.concatenate([src_ref[at : at + 8, :] for at in ats], 0), 4, 0)


class Group:
    def __init__(self, rows, base, pk_ref, refs, here, plan):
        self.rows, self.n, self.base, self.pk = rows, len(rows), base, pk_ref
        self.pack, self.r0, self.s1, self.rx, core_s, core_r, x_s, x_r = refs
        band, grp, y, x, z, core = here
        self.theirs = pl.ds(pl.multiple_of((1 - core) * 64, 64), 64)
        self.mine = pl.ds(pl.multiple_of(core * 64, 64), 64)
        self.own = pl.ds(pl.multiple_of(16 * x, 16), 16)
        self.core_copy = plan(self.pack, self.r0, core_s.at[0], core_r.at[0], (band, z * 2 + 1 - core))
        self.sent = []
        for d in X_ORDER:
            to = lax.rem(x + d, NX)
            part = self.s1.at[:, pl.ds(pl.multiple_of(16 * to, 16), 16), :]
            self.sent.append(plan(part, self.rx.at[d - 1], x_s.at[d - 1], x_r.at[d - 1], (y * NX + to, grp)))

    def start(self):
        def narrow(i, carry):
            self.pack[i] = self.pk[self.base + i, self.theirs, :].astype(BF16)
            return carry

        lax.fori_loop(0, self.n, narrow, 0, unroll=2)
        self.core_copy.start()

    def spread(self):
        self.core_copy.wait()

        def add(i, carry):
            total = self.pk[self.base + i, self.mine, :] + self.r0[i].astype(F32)
            self.s1[i] = total.astype(BF16)
            return carry

        lax.fori_loop(0, self.n, add, 0, unroll=2)
        for copy in self.sent:
            copy.start()

    def take(self, wide_ref, padded):
        total = self.s1[:, self.own, :].astype(F32)
        for copy, d in zip(self.sent, X_ORDER):
            copy.wait_recv()
            total = total + self.rx[d - 1].astype(F32)
        for i in range(self.n):
            for quarter in range(2):
                at = pl.ds(quarter * padded + i, NY, stride=2 * padded)
                wide_ref[at, :] = total[i, 8 * quarter : 8 * quarter + 8, :]


def padded_of(n):
    return -(-n // 8) * 8


class Turn:
    def __init__(self, group, refs, here, plan):
        self.group, self.rows, self.padded = group, group.rows, padded_of(group.n)
        self.wide, self.tb, self.ry, y_s, y_r = refs
        band, grp, y, x, z, core = here
        n = 2 * self.padded
        self.own = pl.ds(pl.multiple_of(y * n, 8), n)
        self.sent = []
        for d in Y_ORDER:
            to = lax.rem(y + d, NY)
            self.sent.append(
                plan(self.tb.at[to], self.ry.at[d - 1], y_s.at[d - 1], y_r.at[d - 1], (to * NX + x, grp))
            )

    def clear(self):
        for i in range(len(self.rows), self.padded):
            for quarter in range(2):
                at = pl.ds(quarter * self.padded + i, NY, stride=2 * self.padded)
                self.wide[at, :] = jnp.zeros((NY, 128), F32)

    def start(self):
        n = 2 * self.padded
        self.group.take(self.wide, self.padded)
        for i in range(NY):
            self.tb[i] = self.wide[n * i : n * (i + 1), :].astype(BF16)
        for copy in self.sent:
            copy.start()

    def collect(self, f_ref):
        total = self.wide[self.own, :]
        for copy, d in zip(self.sent, Y_ORDER):
            copy.wait_recv()
            total = total + self.ry[d - 1].astype(F32)
        for i in range(8):
            for at, row in enumerate(owned(i % 4)):
                if row in self.rows:
                    first = self.padded * (i // 4) + self.rows.index(row)
                    f_ref[i, at : at + 1, :] = total[first : first + 1, :]


class Share:
    def __init__(self, wide_ref, f_ref, r3_ref, z_s, z_r, here):
        self.wide, self.f, self.r3, self.z_s, self.z_r, self.here = wide_ref, f_ref, r3_ref, z_s, z_r, here

    def last(self, i):
        band, grp, y, x, z, core = self.here
        quarter, zi, to_core = i // 4, (i // 2) % 2, i % 2
        to_z = 2 * (2 * core + quarter) + zi
        copy = pltpu.make_async_remote_copy(
            src_ref=self.f.at[i],
            dst_ref=self.r3.at[z],
            send_sem=self.z_s.at[i],
            recv_sem=self.z_r.at[z],
            device_id=(band, to_z * 2 + to_core),
            device_id_type=MESH,
        )
        return copy, jnp.logical_or(to_z != z, core != to_core)

    def start(self):
        self.f[...] = self.wide[...].astype(BF16)
        for i in range(8):
            copy, away = self.last(i)
            pl.when(away)(copy.start)

    def finish(self, red_ref):
        band, grp, y, x, z, core = self.here
        own_core = z // 4

        @pl.when(core == own_core)
        def _():
            self.r3[z] = self.f[4 * lax.rem(z // 2, 2) + lax.rem(grp, 4)]

        for s in range(NZ):
            come = pltpu.make_async_remote_copy(
                src_ref=self.f.at[0],
                dst_ref=self.r3.at[s],
                send_sem=self.z_s.at[0],
                recv_sem=self.z_r.at[s],
                device_id=(band, z * 2 + 1 - core),
                device_id_type=MESH,
            )
            pl.when(jnp.logical_or(z != s, core != own_core))(come.wait_recv)
        total = self.r3[0].astype(F32)
        for s in range(1, NZ):
            total = total + self.r3[s].astype(F32)
        red_ref[...] = total

    def drain(self):
        for i in range(8):
            copy, away = self.last(i)
            pl.when(away)(copy.wait_send)


def group_scratch(n):
    dma = pltpu.SemaphoreType.DMA
    return [
        pltpu.VMEM((n, 64, 128), BF16),
        pltpu.VMEM((n, 64, 128), BF16),
        pltpu.VMEM((n, 64, 128), BF16),
        pltpu.VMEM((NX - 1, n, 16, 128), BF16),
        dma((1,)), dma((1,)), dma((NX - 1,)), dma((NX - 1,)),
    ]


def turn_scratch(n):
    dma = pltpu.SemaphoreType.DMA
    wide = 2 * padded_of(n)
    return [
        pltpu.VMEM((NY * wide, 128), F32),
        pltpu.VMEM((NY, wide, 128), BF16),
        pltpu.VMEM((NY - 1, wide, 128), BF16),
        dma((NY - 1,)), dma((NY - 1,)),
    ]


def permutation():
    at = lax.broadcasted_iota(jnp.int32, (C, C), 0)
    feature = lax.broadcasted_iota(jnp.int32, (C, C), 1)

    def bits(low, count):
        return lax.bitwise_and(lax.shift_right_logical(at, jnp.full_like(at, low)), (1 << count) - 1)

    m = 16 * bits(0, 3) + bits(3, 1) + 4 * bits(4, 2) + 2 * bits(6, 1)
    return (feature == 3 * m + bits(7, 2)).astype(F32).astype(BF16)


def kernel(
    tok_hbm, cot_hbm, oce_hbm, land_hbm, wqkv_hbm, wproj_hbm, rb_hbm,
    block_hbm, grad_hbm, red_hbm,
    block_ref, grad_out_ref, red_ref,
    tok_ref, cot_ref, oce_ref, land_ref, wqkv_ref, wproj_ref, rb_ref,
    htok_ref, hcot_ref, hoce_ref, uu_ref, ug_ref, hu_ref, hg_ref,
    x_ref, c_ref, n_ref, inv_ref, mask_ref, h_ref, ht_ref, qkv_ref, dz_ref, do_ref, o_ref, dqkv_ref, ot_ref,
    p_ref, bias_ref, db_ref, perm_ref, pk_ref, bt_ref, f_ref, low_ref, r3_ref, load_sem, store_sem, halo_s, halo_r, z_s, z_r, near_sem, *rest,
):
    band = lax.axis_index("band")
    grp = lax.axis_index("grp")
    y, x = band // NX, lax.rem(band, NX)
    z, core = grp // 2, lax.rem(grp, 2)
    linear = band * 16 + grp
    after = lax.rem(linear + 1, 512)
    before = lax.rem(linear + 511, 512)
    after_id = (after // 16, lax.rem(after, 16))
    before_id = (before // 16, lax.rem(before, 16))

    barrier = pltpu.get_barrier_semaphore()


    def at_z(d):
        return (band, lax.rem(z + NZ + d, NZ) * 2 + core)

    def at_y(d):
        return (lax.rem(y + NY + d, NY) * NX + x, grp)

    def at_x(d):
        return (y * NX + lax.rem(x + NX + d, NX), grp)

    peers = [after_id, before_id, (band, z * 2 + 1 - core)]
    peers += [at(d) for at in (at_z, at_y, at_x) for d in (1, -1)]
    for peer in peers:
        pl.semaphore_signal(barrier, inc=1, device_id=peer, device_id_type=MESH)

    def blocks(ref, i, j):
        return ref.at[:, pl.ds(C * i + 128 * j, 128)]

    loads = []
    for i, (src, dst) in enumerate(
        [(tok_hbm, tok_ref), (oce_hbm, oce_ref), (land_hbm, land_ref), (cot_hbm, cot_ref)]
        + [(wproj_hbm, wproj_ref), (rb_hbm, rb_ref)]
        + [(blocks(wqkv_hbm, i, j), blocks(wqkv_ref, j, i)) for j in range(HG) for i in range(3)]
    ):
        loads.append(pltpu.make_async_copy(src, dst, load_sem.at[i]))
        loads[-1].start()

    def tell(r, at, d):
        for to in (at(d), at(-d)):
            pl.semaphore_signal(near_sem.at[r], inc=1, device_id=to, device_id_type=MESH)

    def plan(src, dst, s, r, to):
        return pltpu.make_async_remote_copy(
            src_ref=src, dst_ref=dst, send_sem=s, recv_sem=r, device_id=to, device_id_type=MESH
        )

    def send(*args):
        copy = plan(*args)
        copy.start()
        return copy

    kept = []

    def keep(src, dst):
        kept.append(pltpu.make_async_copy(src, dst, store_sem.at[len(kept)]))
        kept[-1].start()

    pl.semaphore_wait(barrier, len(peers))
    tell(0, at_z, 1)
    tell(1, at_y, 1)
    tell(2, at_x, 1)
    far = (2, 3, 4)
    halos = [
        send(tok_hbm.at[pl.ds(0, 4)], htok_ref, halo_s.at[0], halo_r.at[0], before_id),
        send(oce_hbm, hoce_ref, halo_s.at[1], halo_r.at[1], before_id),
        send(cot_hbm.at[pl.ds(0, 4)], hcot_ref, halo_s.at[2], halo_r.at[2], before_id),
    ]

    loads[0].wait()
    stage_rows([tok_ref[4 + i] for i in range(4)], 0, x_ref)
    perm_ref[...] = permutation()

    def norm(i, carry):
        rows = pl.ds(pl.multiple_of(i * 64, 64), 64)
        value = x_ref[rows, :]
        centered = value - jnp.mean(value, -1, keepdims=True)
        inv = lax.rsqrt(jnp.mean(centered * centered, -1, keepdims=True) + EPS)
        n = centered * inv
        n_ref[rows, :] = n
        inv_ref[rows, :] = jnp.broadcast_to(inv, (64, 128))
        h_ref[rows, :] = n.astype(BF16)
        return carry

    def project(half):
        rows = slice(OWN * half, OWN * half + OWN)

        def part(g, carry):
            lanes = pl.ds(pl.multiple_of(C * g, 128), C)
            qkv_ref[rows, lanes] = dot_nn(h_ref[rows, :], wqkv_ref[:, lanes]).astype(BF16)
            return carry

        lax.fori_loop(0, HG, part, 0)

    def pull(half):
        rows = slice(OWN * half, OWN * half + OWN)
        wide = jnp.concatenate([mask_ref[rows, :]] * 3, 1)
        dz_ref[rows, :] = (wide * c_ref[rows, :]).astype(BF16)
        do_ref[rows, :] = dot_nt(dz_ref[rows, :], wproj_ref[...]).astype(BF16)

    lax.fori_loop(0, 3, norm, 0, unroll=3)
    loads[1].wait()
    loads[2].wait()
    land = land_ref[...].astype(F32)
    stage_mask(oce_ref[4:8, :].astype(F32), land, 0, mask_ref)
    for i in range(6, 15):
        loads[i].wait()
    project(0)
    loads[3].wait()
    stage_rows([cot_ref[4 + i] for i in range(4)], 0, c_ref)
    loads[4].wait()
    pull(0)
    loads[5].wait()
    for i in range(6):
        pair = jnp.concatenate([rb_ref[2 * i], rb_ref[2 * i + 1]], 0)
        bias_ref[:, 128 * i : 128 * i + 128] = pair.T
    db_ref[...] = jnp.zeros_like(db_ref)

    here_lower = jnp.broadcast_to(linear, (48, C)) < 511
    halos[0].wait_recv()
    stage_rows([jnp.where(here_lower, htok_ref[i].astype(F32), 0.0) for i in range(4)], 1, x_ref)
    lax.fori_loop(3, 6, norm, 0, unroll=3)
    project(1)
    for r in (0, 1):
        pl.semaphore_wait(near_sem.at[r], 2)
    tell(3, at_z, 2)
    tell(4, at_y, 2)
    ht_ref[...] = dot_nt(perm_ref[...], h_ref[...]).astype(BF16)
    halos[1].wait_recv()
    ocean = jnp.where(jnp.broadcast_to(linear, (4, 48)) < 511, hoce_ref[0:4, :].astype(F32), 0.0)
    stage_mask(ocean, land, 1, mask_ref)

    head = lax.broadcasted_iota(jnp.int32, (64, 128), 1) // 32
    picks = [(head == i).astype(F32) for i in range(4)]
    picks_low = [p.astype(BF16) for p in picks]

    def spread(a):
        return jnp.concatenate([a * p for p in picks_low], 0)

    def fold(value):
        total = value[0:64] * picks[0]
        for i in range(1, 4):
            total = total + value[64 * i : 64 * i + 64] * picks[i]
        return total

    def two(w):
        first = pl.ds(pl.multiple_of(w * 32, 32), 32)
        second = pl.ds(pl.multiple_of(OWN + w * 32, 32), 32)
        return first, second

    def load(ref, w, lanes):
        first, second = two(w)
        return jnp.concatenate([ref[first, lanes], ref[second, lanes]], 0)

    def store(ref, w, lanes, value):
        first, second = two(w)
        ref[first, lanes] = value[0:32]
        ref[second, lanes] = value[32:64]

    def lanes_of(g):
        return [pl.ds(pl.multiple_of(C * g + 128 * i, 128), 128) for i in range(3)] + [
            pl.ds(pl.multiple_of(256 * g, 256), 256),
            pl.ds(pl.multiple_of(128 * g, 128), 128),
        ]

    def forward(w, carry):
        whole = pl.ds(pl.multiple_of(w * 64, 64), 64)
        live = jnp.concatenate([load(mask_ref, w, slice(0, 128))] * 2, 1) > 0.5
        for g in range(HG):
            q_lanes, k_lanes, v_lanes, wide, head_lanes = lanes_of(g)
            q4 = spread(load(qkv_ref, w, q_lanes))
            s = dot_nt(load(qkv_ref, w, k_lanes), q4) * SCALE + bias_ref[:, wide]
            s = jnp.where(live, s, MASKED)
            weights = jnp.exp(s - jnp.max(s, 0, keepdims=True))
            p = weights * (1.0 / jnp.sum(weights, 0, keepdims=True))
            p_ref[whole, wide] = p
            store(o_ref, w, head_lanes, fold(dot_tn(p.astype(BF16), load(qkv_ref, w, v_lanes))).astype(BF16))
        return carry

    def backward(g):
        q_lanes, k_lanes, v_lanes, wide, head_lanes = lanes_of(g)

        def step(w, carry):
            whole = pl.ds(pl.multiple_of(w * 64, 64), 64)
            q4 = spread(load(qkv_ref, w, q_lanes))
            do4 = spread(load(do_ref, w, head_lanes))
            p = p_ref[whole, wide]
            dp = dot_nt(load(qkv_ref, w, v_lanes), do4)
            store(dqkv_ref, w, v_lanes, dot_nn(p.astype(BF16), do4).astype(BF16))
            ds = p * (dp - jnp.sum(p * dp, 0, keepdims=True))
            db_ref[:, wide] += ds
            dsc = (ds * SCALE).astype(BF16)
            store(dqkv_ref, w, k_lanes, dot_nn(dsc, q4).astype(BF16))
            dq = fold(dot_tn(dsc, load(qkv_ref, w, k_lanes)))
            store(dqkv_ref, w, q_lanes, dq.astype(BF16))
            return carry

        lax.fori_loop(0, WB, step, 0, unroll=6)
        fill(9 + 9 * g, dot_nn(ht_ref[...], dqkv_ref[:, pl.ds(pl.multiple_of(C * g, 128), C)]))

    lax.fori_loop(0, WB, forward, 0, unroll=2)

    halos[2].wait_recv()
    stage_rows([jnp.where(here_lower, hcot_ref[i].astype(F32), 0.0) for i in range(4)], 1, c_ref)
    pull(1)

    here = (band, grp, y, x, z, core)
    groups, turns = [], []
    at = base = 0
    for rows in GROUPS:
        groups.append(Group(rows, base, pk_ref, rest[at : at + 8], here, plan))
        at += 8
        base += len(rows)
    for group in groups:
        turns.append(Turn(group, rest[at : at + 5], here, plan))
        at += 5
    share = Share(f_ref, low_ref, r3_ref, z_s, z_r, here)

    def fill(base, value):
        for k in range(3):
            for j in range(3):
                pk_ref[base + 3 * k + j] = value[128 * j : 128 * j + 128, 128 * k : 128 * k + 128]

    ot_ref[...] = dot_nt(perm_ref[...], o_ref[...]).astype(BF16)
    fill(0, dot_nn(ot_ref[...], dz_ref[...]))
    for turn in turns:
        turn.clear()
    for i in range(8):
        f_ref[i, SLOTS:16, :] = jnp.zeros((16 - SLOTS, 128), F32)

    def heads(g, carry):
        backward(g)

        @pl.when(g == 0)
        def _():
            groups[0].start()

        @pl.when(g == 1)
        def _():
            groups[1].start()
            for r in far:
                pl.semaphore_wait(near_sem.at[r], 2)
            groups[0].spread()

        return carry

    lax.fori_loop(0, HG, heads, 0)
    for i in range(6):
        bt_ref[128 * i : 128 * i + 128, 0:64] = db_ref[:, 128 * i : 128 * i + 128].T
    lane = lax.broadcasted_iota(jnp.int32, (8, 128), 1)
    for j in range(3):
        for i in range(16):
            first = 2 * j + 24 * ((i // 2) % 4) + 12 * (i // 8) + 6 * (i % 2)
            even = bt_ref[pl.ds(first, 8, stride=96), :]
            odd = bt_ref[pl.ds(first + 1, 8, stride=96), :]
            pk_ref[36 + j, 8 * i : 8 * i + 8, :] = jnp.where(lane < 64, even, pltpu.roll(odd, 64, 1))
    groups[2].start()
    groups[1].spread()

    wide_mask = jnp.concatenate([mask_ref[...]] * 3, 1)
    x_ref[...] = wide_mask * dot_nn(o_ref[...], wproj_ref[...])
    groups[2].spread()
    turns[0].start()
    for i in range(4):
        uu_ref[i] = grid_row(x_ref, 1, i).astype(BF16)
    c_ref[...] = dot_nt(dqkv_ref[...], wqkv_ref[...])

    def back(i, carry):
        rows = pl.ds(pl.multiple_of(i * 64, 64), 64)
        dh = c_ref[rows, :]
        n = n_ref[rows, :]
        inv = jnp.concatenate([inv_ref[rows, :]] * 3, 1)
        slope = jnp.mean(dh * n, -1, keepdims=True)
        c_ref[rows, :] = inv * (dh - jnp.mean(dh, -1, keepdims=True) - n * slope)
        return carry

    lax.fori_loop(0, WB, back, 0, unroll=3)
    for i in range(4):
        ug_ref[i] = grid_row(c_ref, 1, i).astype(BF16)
    turns[1].start()
    turns[2].start()
    halo_u = send(uu_ref, hu_ref, halo_s.at[3], halo_r.at[3], after_id)
    halo_g = send(ug_ref, hg_ref, halo_s.at[4], halo_r.at[4], after_id)
    turns[0].collect(f_ref)
    for i in range(4):
        row = grid_row(x_ref, 0, i).astype(BF16).astype(F32)
        block_ref[4 + i] = (tok_ref[4 + i].astype(F32) + row).astype(BF16)
        row = grid_row(c_ref, 0, i).astype(BF16).astype(F32)
        grad_out_ref[4 + i] = (cot_ref[4 + i].astype(F32) + row).astype(BF16)
    upper, lower = pl.ds(4, 4), pl.ds(0, 4)
    keep(block_ref.at[upper], block_hbm.at[upper])
    keep(grad_out_ref.at[upper], grad_hbm.at[upper])
    turns[1].collect(f_ref)
    turns[2].collect(f_ref)
    share.start()
    inner = jnp.broadcast_to(linear, (4, 48, C)) > 0
    halo_u.wait_recv()
    low = jnp.where(inner, hu_ref[...].astype(F32), 0.0)
    block_ref[0:4] = (tok_ref[0:4].astype(F32) + low).astype(BF16)
    keep(block_ref.at[lower], block_hbm.at[lower])
    halo_g.wait_recv()
    low = jnp.where(inner, hg_ref[...].astype(F32), 0.0)
    grad_out_ref[0:4] = (cot_ref[0:4].astype(F32) + low).astype(BF16)
    keep(grad_out_ref.at[lower], grad_hbm.at[lower])
    for one in groups + turns:
        for copy in one.sent:
            copy.wait_send()
    share.finish(red_ref)
    keep(red_ref, red_hbm)
    share.drain()
    for copy in halos + [halo_u, halo_g]:
        copy.wait_send()
    for copy in kept:
        copy.wait()


def place_kernel(
    block_hbm, grad_hbm, red_hbm, block_out, grad_out, qkv_out, proj_out, bias_out,
    block_ref, grad_ref, red_ref, in_sem, out_sem,
):
    load = pltpu.make_async_copy(red_hbm, red_ref, in_sem.at[4])
    load.start()
    moves = []
    for i, (src, via, dst) in enumerate(((block_hbm, block_ref, block_out), (grad_hbm, grad_ref, grad_out))):
        for j in range(2):
            part = pl.ds(4 * j, 4)
            into = pltpu.make_async_copy(src.at[part], via.at[part], in_sem.at[2 * i + j])
            into.start()
            moves.append((into, pltpu.make_async_copy(via.at[part], dst.at[part], out_sem.at[2 * i + j])))
    load.wait()
    for into, out in moves:
        into.wait()
        out.start()
    g = lax.rem(lax.axis_index("grp"), 4)
    lane = lax.broadcasted_iota(jnp.int32, (16, 128), 1)
    red = red_ref[...]
    following = jnp.concatenate([red[1:16], red[0:1]], 0)
    rolled = [red]
    for quarter in range(1, 4):
        shift = 128 - 32 * quarter
        value = jnp.where(lane < shift, pltpu.roll(red, shift, 1), pltpu.roll(following, shift, 1))
        rolled.append(value)

    def pick(step):
        which = jnp.broadcast_to(lax.rem(step * g, 4), (16, 128))
        value = rolled[0]
        for quarter in range(1, 4):
            value = jnp.where(which == quarter, rolled[quarter], value)
        return value

    for out, step, first, size in ((qkv_out, 27, 0, 864), (proj_out, 9, 8, 288), (bias_out, 3, 11, 96)):
        value = pick(step)
        for i in range(-(-size // 128)):
            n = min(128, size - 128 * i)
            out[pl.ds(128 * i, n)] = value[first + i, 0:n]
    for into, out in moves:
        out.wait()


def local(tokens, cotangent, ocean_mask, land_mask, w_qkv, w_proj, rel_bias):
    grid = jax.ShapeDtypeStruct((8, 48, C), BF16)
    dma = pltpu.SemaphoreType.DMA
    half = pltpu.VMEM((4, 48, C), BF16)
    scratch = [
        pltpu.VMEM((8, 48, C), BF16),
        pltpu.VMEM((8, 48, C), BF16),
        pltpu.VMEM((16, 128), F32),
        pltpu.VMEM((8, 48, C), BF16),
        pltpu.VMEM((8, 48, C), BF16),
        pltpu.VMEM((8, 48), jnp.int32),
        pltpu.VMEM((1, 6), jnp.int32),
        pltpu.VMEM((C, 3 * C), BF16),
        pltpu.VMEM((C, C), BF16),
        pltpu.VMEM((12, 64, 64), F32),
        half, half, pltpu.VMEM((8, 48), jnp.int32), half, half, half, half,
        pltpu.VMEM((C, C), F32),
        pltpu.VMEM((C, C), F32),
        pltpu.VMEM((C, C), F32),
        pltpu.VMEM((C, 128), F32),
        pltpu.VMEM((C, 128), F32),
        pltpu.VMEM((C, C), BF16),
        pltpu.VMEM((C, C), BF16),
        pltpu.VMEM((C, 3 * C), BF16),
        pltpu.VMEM((C, C), BF16),
        pltpu.VMEM((C, C), BF16),
        pltpu.VMEM((C, C), BF16),
        pltpu.VMEM((C, 3 * C), BF16),
        pltpu.VMEM((C, C), BF16),
        pltpu.VMEM((C, 768), F32),
        pltpu.VMEM((64, 768), F32),
        pltpu.VMEM((64, 768), F32),
        pltpu.VMEM((C, C), BF16),
        pltpu.VMEM((39, 128, 128), F32),
        pltpu.VMEM((768, 128), F32),
        pltpu.VMEM((8, 16, 128), F32),
        pltpu.VMEM((8, 16, 128), BF16),
        pltpu.VMEM((NZ, 16, 128), BF16),
        dma((15,)), dma((5,)), dma((5,)), dma((5,)), dma((8,)), dma((NZ,)),
        pltpu.SemaphoreType.REGULAR((5,)),
    ]
    for rows in GROUPS:
        scratch += group_scratch(len(rows))
    for rows in GROUPS:
        scratch += turn_scratch(len(rows))
    block_out, token_grad, red = pl.pallas_call(
        kernel,
        out_shape=[grid, grid, jax.ShapeDtypeStruct((16, 128), F32)],
        in_specs=[pl.BlockSpec(memory_space=pltpu.HBM)] * 7,
        out_specs=[pl.BlockSpec(memory_space=pltpu.HBM)] * 3,
        scratch_shapes=scratch,
        compiler_params=pltpu.CompilerParams(
            collective_id=0, has_side_effects=True, vmem_limit_bytes=VMEM_BYTES
        ),
        cost_estimate=pl.CostEstimate(flops=15 * 10**8, bytes_accessed=5 * 10**6, transcendentals=300000),
        name="window_block",
    )(tokens, cotangent, ocean_mask, land_mask, w_qkv, w_proj, rel_bias)

    whole = pl.BlockSpec(memory_space=pltpu.VMEM)
    hbm = pl.BlockSpec(memory_space=pltpu.HBM)
    return tuple(
        pl.pallas_call(
            place_kernel,
            out_shape=[grid, grid] + [jax.ShapeDtypeStruct((n,), F32) for n in (864, 288, 96)],
            in_specs=[hbm] * 3,
            out_specs=[hbm, hbm, whole, whole, whole],
            scratch_shapes=[
                pltpu.VMEM((8, 48, C), BF16),
                pltpu.VMEM((8, 48, C), BF16),
                pltpu.VMEM((16, 128), F32),
                dma((5,)),
                dma((4,)),
            ],
            compiler_params=pltpu.CompilerParams(vmem_limit_bytes=VMEM_BYTES),
            cost_estimate=pl.CostEstimate(flops=10**4, bytes_accessed=12 * 10**5, transcendentals=0),
            name="outputs",
        )(block_out, token_grad, red)
    )


def solution(mesh):
    split = ("band", "grp")
    placed = (
        P(split, None, None),
        P(split, None, None),
        P(split, None),
        P(split, None),
        P(),
        P(),
        P(),
    )
    return jax.shard_map(
        local,
        mesh=mesh,
        in_specs=placed,
        out_specs=(P(split, None, None), P(split, None, None), P(split), P(split), P(split)),
        check_vma=False,
    )
```

```python
import math

import jax
import jax.numpy as jnp
from jax import lax
from jax.experimental import pallas as pl
from jax.experimental.pallas import tpu as pltpu
from jax.sharding import PartitionSpec as P

EPS = 1e-05
MASKED = -1e30
C = 384
WB = 6
HG = 3
SCALE = 1.0 / math.sqrt(32)
F32 = jnp.float32
BF16 = jnp.bfloat16
MESH = pl.DeviceIdType.MESH

NY, NX, NZ = 8, 4, 8
OWN = 192
VMEM_BYTES = 62 * 2**20


def qkv_rows(g):
    return [("qkv", j, k) for k in (g, 3 + g, 6 + g) for j in range(3)]


PROJ_ROWS = [("proj", j, k) for k in range(3) for j in range(3)]
BIAS_ROWS = [("bias", j, 0) for j in range(3)]
GROUPS = [PROJ_ROWS + qkv_rows(0), qkv_rows(1)[:8], qkv_rows(1)[8:] + qkv_rows(2) + BIAS_ROWS]
SLOTS = 13
X_ORDER = (2, 1, 3)
Y_ORDER = (4, 3, 5, 2, 6, 1, 7)
Z_ORDER = (4, 3, 5, 2, 6, 1, 7, 0)


def owned(g):
    qkv = [min(27 * g // 4 + i, 26) for i in range(8)]
    proj = [min(9 * g // 4 + i, 8) for i in range(3)]
    bias = [min(3 * g // 4 + i, 2) for i in range(2)]
    return (
        [("qkv", r // 9, r % 9) for r in qkv]
        + [("proj", r // 3, r % 3) for r in proj]
        + [("bias", r, 0) for r in bias]
    )


def dot_nt(a, b):
    return lax.dot_general(a, b, (((1,), (1,)), ((), ())), preferred_element_type=F32)


def dot_tn(a, b):
    return lax.dot_general(a, b, (((0,), (0,)), ((), ())), preferred_element_type=F32)


def dot_nn(a, b):
    return lax.dot_general(a, b, (((1,), (0,)), ((), ())), preferred_element_type=F32)


def stage_mask(ocean, land, half, mask_ref):
    place = lax.broadcasted_iota(jnp.int32, (8, 48), 0)
    column = lax.broadcasted_iota(jnp.int32, (8, 48), 1)
    for w in range(WB):
        live = 1.0 - land[:, w : w + 1]
        pick = (column == lax.rem(place + (8 * w + 4), 48)).astype(F32) * live
        for i in range(4):
            row = jnp.broadcast_to(ocean[i : i + 1, :], (8, 48))
            value = jnp.sum(row * pick, axis=1, keepdims=True)
            at = OWN * half + 32 * w + 8 * i
            mask_ref[at : at + 8, :] = jnp.broadcast_to(value, (8, 128))


def stage_rows(rows, half, out_ref):
    for i, row in enumerate(rows):
        rolled = pltpu.roll(row.astype(F32), 44, 0)
        for w in range(WB):
            at = OWN * half + 32 * w + 8 * i
            out_ref[at : at + 8, :] = rolled[8 * w : 8 * w + 8, :]


def grid_row(src_ref, half, i):
    ats = [OWN * half + 32 * w + 8 * i for w in range(WB)]
    return pltpu.roll(jnp.concatenate([src_ref[at : at + 8, :] for at in ats], 0), 4, 0)


class Group:
    def __init__(self, rows, base, pk_ref, refs, here, plan):
        self.rows, self.n, self.base, self.pk = rows, len(rows), base, pk_ref
        self.pack, self.r0, self.s1, self.rx, core_s, core_r, x_s, x_r = refs
        band, grp, y, x, z, core = here
        self.theirs = pl.ds(pl.multiple_of((1 - core) * 64, 64), 64)
        self.mine = pl.ds(pl.multiple_of(core * 64, 64), 64)
        self.own = pl.ds(pl.multiple_of(16 * x, 16), 16)
        self.core_copy = plan(self.pack, self.r0, core_s.at[0], core_r.at[0], (band, z * 2 + 1 - core))
        self.sent = []
        for d in X_ORDER:
            to = lax.rem(x + d, NX)
            part = self.s1.at[:, pl.ds(pl.multiple_of(16 * to, 16), 16), :]
            self.sent.append(plan(part, self.rx.at[d - 1], x_s.at[d - 1], x_r.at[d - 1], (y * NX + to, grp)))

    def start(self):
        def narrow(i, carry):
            self.pack[i] = self.pk[self.base + i, self.theirs, :].astype(BF16)
            return carry

        lax.fori_loop(0, self.n, narrow, 0, unroll=2)
        self.core_copy.start()

    def spread(self):
        self.core_copy.wait()

        def add(i, carry):
            total = self.pk[self.base + i, self.mine, :] + self.r0[i].astype(F32)
            self.s1[i] = total.astype(BF16)
            return carry

        lax.fori_loop(0, self.n, add, 0, unroll=2)
        for copy in self.sent:
            copy.start()

    def take(self, wide_ref, padded):
        total = self.s1[:, self.own, :].astype(F32)
        for copy, d in zip(self.sent, X_ORDER):
            copy.wait_recv()
            total = total + self.rx[d - 1].astype(F32)
        for i in range(self.n):
            for quarter in range(2):
                at = pl.ds(quarter * padded + i, NY, stride=2 * padded)
                wide_ref[at, :] = total[i, 8 * quarter : 8 * quarter + 8, :]


def padded_of(n):
    return -(-n // 8) * 8


class Turn:
    def __init__(self, group, refs, here, plan):
        self.group, self.rows, self.padded = group, group.rows, padded_of(group.n)
        self.wide, self.tb, self.ry, y_s, y_r = refs
        band, grp, y, x, z, core = here
        n = 2 * self.padded
        self.own = pl.ds(pl.multiple_of(y * n, 8), n)
        self.sent = []
        for d in Y_ORDER:
            to = lax.rem(y + d, NY)
            self.sent.append(
                plan(self.tb.at[to], self.ry.at[d - 1], y_s.at[d - 1], y_r.at[d - 1], (to * NX + x, grp))
            )

    def clear(self):
        for i in range(len(self.rows), self.padded):
            for quarter in range(2):
                at = pl.ds(quarter * self.padded + i, NY, stride=2 * self.padded)
                self.wide[at, :] = jnp.zeros((NY, 128), F32)

    def start(self):
        n = 2 * self.padded
        self.group.take(self.wide, self.padded)
        for i in range(NY):
            self.tb[i] = self.wide[n * i : n * (i + 1), :].astype(BF16)
        for copy in self.sent:
            copy.start()

    def collect(self, f_ref):
        total = self.wide[self.own, :]
        for copy, d in zip(self.sent, Y_ORDER):
            copy.wait_recv()
            total = total + self.ry[d - 1].astype(F32)
        for i in range(8):
            for at, row in enumerate(owned(i % 4)):
                if row in self.rows:
                    first = self.padded * (i // 4) + self.rows.index(row)
                    f_ref[i, at : at + 1, :] = total[first : first + 1, :]


class Share:
    def __init__(self, wide_ref, f_ref, r3_ref, z_s, z_r, here):
        self.wide, self.f, self.r3, self.z_s, self.z_r, self.here = wide_ref, f_ref, r3_ref, z_s, z_r, here

    def copies(self):
        band, grp, y, x, z, core = self.here
        for d in Z_ORDER:
            to_z = lax.rem(z + d, NZ)
            for to_core in range(2):
                i = 2 * lax.rem(to_z, 4) + to_core
                copy = pltpu.make_async_remote_copy(
                    src_ref=self.f.at[i],
                    dst_ref=self.r3.at[z],
                    send_sem=self.z_s.at[i],
                    recv_sem=self.z_r.at[z],
                    device_id=(band, to_z * 2 + to_core),
                    device_id_type=MESH,
                )
                away = to_z // 4 == core
                if d == 0:
                    away = jnp.logical_and(away, core != to_core)
                yield copy, away

    def start(self):
        self.f[...] = self.wide[...].astype(BF16)
        for copy, away in self.copies():
            pl.when(away)(copy.start)

    def finish(self, red_ref):
        band, grp, y, x, z, core = self.here
        own_core = z // 4

        @pl.when(core == own_core)
        def _():
            self.r3[z] = self.f[4 * lax.rem(z // 2, 2) + lax.rem(grp, 4)]

        for s in range(NZ):
            come = pltpu.make_async_remote_copy(
                src_ref=self.f.at[0],
                dst_ref=self.r3.at[s],
                send_sem=self.z_s.at[0],
                recv_sem=self.z_r.at[s],
                device_id=(band, z * 2 + 1 - core),
                device_id_type=MESH,
            )
            pl.when(jnp.logical_or(z != s, core != own_core))(come.wait_recv)
        total = self.r3[0].astype(F32)
        for s in range(1, NZ):
            total = total + self.r3[s].astype(F32)
        red_ref[...] = total

    def drain(self):
        for copy, away in self.copies():
            pl.when(away)(copy.wait_send)


def group_scratch(n):
    dma = pltpu.SemaphoreType.DMA
    return [
        pltpu.VMEM((n, 64, 128), BF16),
        pltpu.VMEM((n, 64, 128), BF16),
        pltpu.VMEM((n, 64, 128), BF16),
        pltpu.VMEM((NX - 1, n, 16, 128), BF16),
        dma((1,)), dma((1,)), dma((NX - 1,)), dma((NX - 1,)),
    ]


def turn_scratch(n):
    dma = pltpu.SemaphoreType.DMA
    wide = 2 * padded_of(n)
    return [
        pltpu.VMEM((NY * wide, 128), F32),
        pltpu.VMEM((NY, wide, 128), BF16),
        pltpu.VMEM((NY - 1, wide, 128), BF16),
        dma((NY - 1,)), dma((NY - 1,)),
    ]


def permutation():
    at = lax.broadcasted_iota(jnp.int32, (C, C), 0)
    feature = lax.broadcasted_iota(jnp.int32, (C, C), 1)

    def bits(low, count):
        return lax.bitwise_and(lax.shift_right_logical(at, jnp.full_like(at, low)), (1 << count) - 1)

    m = 16 * bits(0, 3) + bits(3, 1) + 4 * bits(4, 2) + 2 * bits(6, 1)
    return (feature == 3 * m + bits(7, 2)).astype(F32).astype(BF16)


def kernel(
    tok_hbm, cot_hbm, oce_hbm, land_hbm, wqkv_hbm, wproj_hbm, rb_hbm,
    block_hbm, grad_hbm, red_hbm,
    block_ref, grad_out_ref, red_ref,
    tok_ref, cot_ref, oce_ref, land_ref, wqkv_ref, wproj_ref, rb_ref,
    htok_ref, hcot_ref, hoce_ref, uu_ref, ug_ref, hu_ref, hg_ref,
    x_ref, c_ref, n_ref, inv_ref, mask_ref, h_ref, ht_ref, qkv_ref, dz_ref, do_ref, o_ref, dqkv_ref, ot_ref,
    p_ref, bias_ref, db_ref, perm_ref, pk_ref, bt_ref, f_ref, low_ref, r3_ref, load_sem, store_sem, halo_s, halo_r, z_s, z_r, near_sem, *rest,
):
    band = lax.axis_index("band")
    grp = lax.axis_index("grp")
    y, x = band // NX, lax.rem(band, NX)
    z, core = grp // 2, lax.rem(grp, 2)
    linear = band * 16 + grp
    after = lax.rem(linear + 1, 512)
    before = lax.rem(linear + 511, 512)
    after_id = (after // 16, lax.rem(after, 16))
    before_id = (before // 16, lax.rem(before, 16))

    barrier = pltpu.get_barrier_semaphore()


    def at_z(d):
        return (band, lax.rem(z + NZ + d, NZ) * 2 + core)

    def at_y(d):
        return (lax.rem(y + NY + d, NY) * NX + x, grp)

    def at_x(d):
        return (y * NX + lax.rem(x + NX + d, NX), grp)

    peers = [after_id, before_id, (band, z * 2 + 1 - core)]
    peers += [at(d) for at in (at_z, at_y, at_x) for d in (1, -1)]
    for peer in peers:
        pl.semaphore_signal(barrier, inc=1, device_id=peer, device_id_type=MESH)

    def blocks(ref, i, j):
        return ref.at[:, pl.ds(C * i + 128 * j, 128)]

    loads = []
    for i, (src, dst) in enumerate(
        [(tok_hbm, tok_ref), (oce_hbm, oce_ref), (land_hbm, land_ref), (cot_hbm, cot_ref)]
        + [(wproj_hbm, wproj_ref), (rb_hbm, rb_ref)]
        + [(blocks(wqkv_hbm, i, j), blocks(wqkv_ref, j, i)) for j in range(HG) for i in range(3)]
    ):
        loads.append(pltpu.make_async_copy(src, dst, load_sem.at[i]))
        loads[-1].start()

    def tell(r, at, d):
        for to in (at(d), at(-d)):
            pl.semaphore_signal(near_sem.at[r], inc=1, device_id=to, device_id_type=MESH)

    def plan(src, dst, s, r, to):
        return pltpu.make_async_remote_copy(
            src_ref=src, dst_ref=dst, send_sem=s, recv_sem=r, device_id=to, device_id_type=MESH
        )

    def send(*args):
        copy = plan(*args)
        copy.start()
        return copy

    kept = []

    def keep(src, dst):
        kept.append(pltpu.make_async_copy(src, dst, store_sem.at[len(kept)]))
        kept[-1].start()

    pl.semaphore_wait(barrier, len(peers))
    tell(0, at_z, 1)
    tell(1, at_y, 1)
    tell(2, at_x, 1)
    far = (2, 3, 4)
    halos = [
        send(tok_hbm.at[pl.ds(0, 4)], htok_ref, halo_s.at[0], halo_r.at[0], before_id),
        send(oce_hbm, hoce_ref, halo_s.at[1], halo_r.at[1], before_id),
        send(cot_hbm.at[pl.ds(0, 4)], hcot_ref, halo_s.at[2], halo_r.at[2], before_id),
    ]

    loads[0].wait()
    stage_rows([tok_ref[4 + i] for i in range(4)], 0, x_ref)
    perm_ref[...] = permutation()

    def norm(i, carry):
        rows = pl.ds(pl.multiple_of(i * 64, 64), 64)
        value = x_ref[rows, :]
        centered = value - jnp.mean(value, -1, keepdims=True)
        inv = lax.rsqrt(jnp.mean(centered * centered, -1, keepdims=True) + EPS)
        n = centered * inv
        n_ref[rows, :] = n
        inv_ref[rows, :] = jnp.broadcast_to(inv, (64, 128))
        h_ref[rows, :] = n.astype(BF16)
        return carry

    def project(half):
        rows = slice(OWN * half, OWN * half + OWN)
        qkv_ref[rows, :] = dot_nn(h_ref[rows, :], wqkv_ref[...]).astype(BF16)

    def pull(half):
        rows = slice(OWN * half, OWN * half + OWN)
        wide = jnp.concatenate([mask_ref[rows, :]] * 3, 1)
        dz_ref[rows, :] = (wide * c_ref[rows, :]).astype(BF16)
        do_ref[rows, :] = dot_nt(dz_ref[rows, :], wproj_ref[...]).astype(BF16)

    lax.fori_loop(0, 3, norm, 0, unroll=3)
    loads[1].wait()
    loads[2].wait()
    land = land_ref[...].astype(F32)
    stage_mask(oce_ref[4:8, :].astype(F32), land, 0, mask_ref)
    for i in range(6, 15):
        loads[i].wait()
    project(0)
    loads[3].wait()
    stage_rows([cot_ref[4 + i] for i in range(4)], 0, c_ref)
    loads[4].wait()
    pull(0)
    loads[5].wait()
    for i in range(6):
        pair = jnp.concatenate([rb_ref[2 * i], rb_ref[2 * i + 1]], 0)
        bias_ref[:, 128 * i : 128 * i + 128] = pair.T
    db_ref[...] = jnp.zeros_like(db_ref)

    here_lower = jnp.broadcast_to(linear, (48, C)) < 511
    halos[0].wait_recv()
    stage_rows([jnp.where(here_lower, htok_ref[i].astype(F32), 0.0) for i in range(4)], 1, x_ref)
    lax.fori_loop(3, 6, norm, 0, unroll=3)
    project(1)
    for r in (0, 1):
        pl.semaphore_wait(near_sem.at[r], 2)
    tell(3, at_z, 2)
    tell(4, at_y, 2)
    ht_ref[...] = dot_nt(perm_ref[...], h_ref[...]).astype(BF16)
    halos[1].wait_recv()
    ocean = jnp.where(jnp.broadcast_to(linear, (4, 48)) < 511, hoce_ref[0:4, :].astype(F32), 0.0)
    stage_mask(ocean, land, 1, mask_ref)

    head = lax.broadcasted_iota(jnp.int32, (64, 128), 1) // 32
    picks = [(head == i).astype(F32) for i in range(4)]
    picks_low = [p.astype(BF16) for p in picks]

    def spread(a):
        return jnp.concatenate([a * p for p in picks_low], 0)

    def fold(value):
        total = value[0:64] * picks[0]
        for i in range(1, 4):
            total = total + value[64 * i : 64 * i + 64] * picks[i]
        return total

    def two(w):
        first = pl.ds(pl.multiple_of(w * 32, 32), 32)
        second = pl.ds(pl.multiple_of(OWN + w * 32, 32), 32)
        return first, second

    def load(ref, w, lanes):
        first, second = two(w)
        return jnp.concatenate([ref[first, lanes], ref[second, lanes]], 0)

    def store(ref, w, lanes, value):
        first, second = two(w)
        ref[first, lanes] = value[0:32]
        ref[second, lanes] = value[32:64]

    def lanes_of(g):
        return [slice(C * g + 128 * i, C * g + 128 * i + 128) for i in range(3)] + [
            slice(256 * g, 256 * g + 256),
            slice(128 * g, 128 * g + 128),
        ]

    def forward(w, carry):
        whole = pl.ds(pl.multiple_of(w * 64, 64), 64)
        live = jnp.concatenate([load(mask_ref, w, slice(0, 128))] * 2, 1) > 0.5
        for g in range(HG):
            q_lanes, k_lanes, v_lanes, wide, head_lanes = lanes_of(g)
            q4 = spread(load(qkv_ref, w, q_lanes))
            s = dot_nt(load(qkv_ref, w, k_lanes), q4) * SCALE + bias_ref[:, wide]
            s = jnp.where(live, s, MASKED)
            weights = jnp.exp(s - jnp.max(s, 0, keepdims=True))
            p = weights * (1.0 / jnp.sum(weights, 0, keepdims=True))
            p_ref[whole, wide] = p
            store(o_ref, w, head_lanes, fold(dot_tn(p.astype(BF16), load(qkv_ref, w, v_lanes))).astype(BF16))
        return carry

    def backward(g):
        q_lanes, k_lanes, v_lanes, wide, head_lanes = lanes_of(g)

        def step(w, carry):
            whole = pl.ds(pl.multiple_of(w * 64, 64), 64)
            q4 = spread(load(qkv_ref, w, q_lanes))
            do4 = spread(load(do_ref, w, head_lanes))
            p = p_ref[whole, wide]
            dp = dot_nt(load(qkv_ref, w, v_lanes), do4)
            store(dqkv_ref, w, v_lanes, dot_nn(p.astype(BF16), do4).astype(BF16))
            ds = p * (dp - jnp.sum(p * dp, 0, keepdims=True))
            db_ref[:, wide] += ds
            dsc = (ds * SCALE).astype(BF16)
            store(dqkv_ref, w, k_lanes, dot_nn(dsc, q4).astype(BF16))
            dq = fold(dot_tn(dsc, load(qkv_ref, w, k_lanes)))
            store(dqkv_ref, w, q_lanes, dq.astype(BF16))
            return carry

        lax.fori_loop(0, WB, step, 0, unroll=6)
        fill(9 + 9 * g, dot_nn(ht_ref[...], dqkv_ref[:, C * g : C * g + C]))

    lax.fori_loop(0, WB, forward, 0, unroll=2)

    halos[2].wait_recv()
    stage_rows([jnp.where(here_lower, hcot_ref[i].astype(F32), 0.0) for i in range(4)], 1, c_ref)
    pull(1)

    here = (band, grp, y, x, z, core)
    groups, turns = [], []
    at = base = 0
    for rows in GROUPS:
        groups.append(Group(rows, base, pk_ref, rest[at : at + 8], here, plan))
        at += 8
        base += len(rows)
    for group in groups:
        turns.append(Turn(group, rest[at : at + 5], here, plan))
        at += 5
    share = Share(f_ref, low_ref, r3_ref, z_s, z_r, here)

    def fill(base, value):
        for k in range(3):
            for j in range(3):
                pk_ref[base + 3 * k + j] = value[128 * j : 128 * j + 128, 128 * k : 128 * k + 128]

    ot_ref[...] = dot_nt(perm_ref[...], o_ref[...]).astype(BF16)
    fill(0, dot_nn(ot_ref[...], dz_ref[...]))
    for turn in turns:
        turn.clear()
    for i in range(8):
        f_ref[i, SLOTS:16, :] = jnp.zeros((16 - SLOTS, 128), F32)

    backward(0)
    groups[0].start()
    backward(1)
    groups[1].start()
    for r in far:
        pl.semaphore_wait(near_sem.at[r], 2)
    groups[0].spread()
    backward(2)
    for i in range(6):
        bt_ref[128 * i : 128 * i + 128, 0:64] = db_ref[:, 128 * i : 128 * i + 128].T
    lane = lax.broadcasted_iota(jnp.int32, (8, 128), 1)
    for j in range(3):
        for i in range(16):
            first = 2 * j + 24 * ((i // 2) % 4) + 12 * (i // 8) + 6 * (i % 2)
            even = bt_ref[pl.ds(first, 8, stride=96), :]
            odd = bt_ref[pl.ds(first + 1, 8, stride=96), :]
            pk_ref[36 + j, 8 * i : 8 * i + 8, :] = jnp.where(lane < 64, even, pltpu.roll(odd, 64, 1))
    groups[2].start()
    groups[1].spread()

    wide_mask = jnp.concatenate([mask_ref[...]] * 3, 1)
    x_ref[...] = wide_mask * dot_nn(o_ref[...], wproj_ref[...])
    groups[2].spread()
    turns[0].start()
    for i in range(4):
        uu_ref[i] = grid_row(x_ref, 1, i).astype(BF16)
    c_ref[...] = dot_nt(dqkv_ref[...], wqkv_ref[...])

    def back(i, carry):
        rows = pl.ds(pl.multiple_of(i * 64, 64), 64)
        dh = c_ref[rows, :]
        n = n_ref[rows, :]
        inv = jnp.concatenate([inv_ref[rows, :]] * 3, 1)
        slope = jnp.mean(dh * n, -1, keepdims=True)
        c_ref[rows, :] = inv * (dh - jnp.mean(dh, -1, keepdims=True) - n * slope)
        return carry

    lax.fori_loop(0, WB, back, 0, unroll=3)
    for i in range(4):
        ug_ref[i] = grid_row(c_ref, 1, i).astype(BF16)
    turns[1].start()
    turns[2].start()
    halo_u = send(uu_ref, hu_ref, halo_s.at[3], halo_r.at[3], after_id)
    halo_g = send(ug_ref, hg_ref, halo_s.at[4], halo_r.at[4], after_id)
    turns[0].collect(f_ref)
    for i in range(4):
        row = grid_row(x_ref, 0, i).astype(BF16).astype(F32)
        block_ref[4 + i] = (tok_ref[4 + i].astype(F32) + row).astype(BF16)
        row = grid_row(c_ref, 0, i).astype(BF16).astype(F32)
        grad_out_ref[4 + i] = (cot_ref[4 + i].astype(F32) + row).astype(BF16)
    upper, lower = pl.ds(4, 4), pl.ds(0, 4)
    keep(block_ref.at[upper], block_hbm.at[upper])
    keep(grad_out_ref.at[upper], grad_hbm.at[upper])
    turns[1].collect(f_ref)
    turns[2].collect(f_ref)
    share.start()
    inner = jnp.broadcast_to(linear, (4, 48, C)) > 0
    halo_u.wait_recv()
    low = jnp.where(inner, hu_ref[...].astype(F32), 0.0)
    block_ref[0:4] = (tok_ref[0:4].astype(F32) + low).astype(BF16)
    keep(block_ref.at[lower], block_hbm.at[lower])
    halo_g.wait_recv()
    low = jnp.where(inner, hg_ref[...].astype(F32), 0.0)
    grad_out_ref[0:4] = (cot_ref[0:4].astype(F32) + low).astype(BF16)
    keep(grad_out_ref.at[lower], grad_hbm.at[lower])
    for one in groups + turns:
        for copy in one.sent:
            copy.wait_send()
    share.finish(red_ref)
    keep(red_ref, red_hbm)
    share.drain()
    for copy in halos + [halo_u, halo_g]:
        copy.wait_send()
    for copy in kept:
        copy.wait()


def place_kernel(
    block_hbm, grad_hbm, red_hbm, block_out, grad_out, qkv_out, proj_out, bias_out,
    block_ref, grad_ref, red_ref, qkv_ref, proj_ref, bias_ref, in_sem, out_sem,
):
    load = pltpu.make_async_copy(red_hbm, red_ref, in_sem.at[4])
    load.start()
    moves = []
    for i, (src, via, dst) in enumerate(((block_hbm, block_ref, block_out), (grad_hbm, grad_ref, grad_out))):
        for j in range(2):
            part = pl.ds(4 * j, 4)
            into = pltpu.make_async_copy(src.at[part], via.at[part], in_sem.at[2 * i + j])
            into.start()
            moves.append((into, pltpu.make_async_copy(via.at[part], dst.at[part], out_sem.at[2 * i + j])))
    load.wait()
    g = lax.rem(lax.axis_index("grp"), 4)
    lane = lax.broadcasted_iota(jnp.int32, (16, 128), 1)
    red = red_ref[...]
    following = jnp.concatenate([red[1:16], red[0:1]], 0)
    rolled = [red]
    for quarter in range(1, 4):
        shift = 128 - 32 * quarter
        value = jnp.where(lane < shift, pltpu.roll(red, shift, 1), pltpu.roll(following, shift, 1))
        rolled.append(value)

    def pick(step):
        which = jnp.broadcast_to(lax.rem(step * g, 4), (16, 128))
        value = rolled[0]
        for quarter in range(1, 4):
            value = jnp.where(which == quarter, rolled[quarter], value)
        return value

    for into, out in moves:
        into.wait()
        out.start()
    small = []
    for i, (ref, out, step, first, size) in enumerate(
        (
            (qkv_ref, qkv_out, 27, 0, 864),
            (proj_ref, proj_out, 9, 8, 288),
            (bias_ref, bias_out, 3, 11, 96),
        )
    ):
        value = pick(step)
        for j in range(-(-size // 128)):
            n = min(128, size - 128 * j)
            ref[pl.ds(128 * j, n)] = value[first + j, 0:n]
        small.append(pltpu.make_async_copy(ref, out, out_sem.at[4 + i]))
        small[-1].start()
    for out in [out for into, out in moves] + small:
        out.wait()


def local(tokens, cotangent, ocean_mask, land_mask, w_qkv, w_proj, rel_bias):
    grid = jax.ShapeDtypeStruct((8, 48, C), BF16)
    dma = pltpu.SemaphoreType.DMA
    half = pltpu.VMEM((4, 48, C), BF16)
    scratch = [
        pltpu.VMEM((8, 48, C), BF16),
        pltpu.VMEM((8, 48, C), BF16),
        pltpu.VMEM((16, 128), F32),
        pltpu.VMEM((8, 48, C), BF16),
        pltpu.VMEM((8, 48, C), BF16),
        pltpu.VMEM((8, 48), jnp.int32),
        pltpu.VMEM((1, 6), jnp.int32),
        pltpu.VMEM((C, 3 * C), BF16),
        pltpu.VMEM((C, C), BF16),
        pltpu.VMEM((12, 64, 64), F32),
        half, half, pltpu.VMEM((8, 48), jnp.int32), half, half, half, half,
        pltpu.VMEM((C, C), F32),
        pltpu.VMEM((C, C), F32),
        pltpu.VMEM((C, C), F32),
        pltpu.VMEM((C, 128), F32),
        pltpu.VMEM((C, 128), F32),
        pltpu.VMEM((C, C), BF16),
        pltpu.VMEM((C, C), BF16),
        pltpu.VMEM((C, 3 * C), BF16),
        pltpu.VMEM((C, C), BF16),
        pltpu.VMEM((C, C), BF16),
        pltpu.VMEM((C, C), BF16),
        pltpu.VMEM((C, 3 * C), BF16),
        pltpu.VMEM((C, C), BF16),
        pltpu.VMEM((C, 768), F32),
        pltpu.VMEM((64, 768), F32),
        pltpu.VMEM((64, 768), F32),
        pltpu.VMEM((C, C), BF16),
        pltpu.VMEM((39, 128, 128), F32),
        pltpu.VMEM((768, 128), F32),
        pltpu.VMEM((8, 16, 128), F32),
        pltpu.VMEM((8, 16, 128), BF16),
        pltpu.VMEM((NZ, 16, 128), BF16),
        dma((15,)), dma((5,)), dma((5,)), dma((5,)), dma((8,)), dma((NZ,)),
        pltpu.SemaphoreType.REGULAR((5,)),
    ]
    for rows in GROUPS:
        scratch += group_scratch(len(rows))
    for rows in GROUPS:
        scratch += turn_scratch(len(rows))
    block_out, token_grad, red = pl.pallas_call(
        kernel,
        out_shape=[grid, grid, jax.ShapeDtypeStruct((16, 128), F32)],
        in_specs=[pl.BlockSpec(memory_space=pltpu.HBM)] * 7,
        out_specs=[pl.BlockSpec(memory_space=pltpu.HBM)] * 3,
        scratch_shapes=scratch,
        compiler_params=pltpu.CompilerParams(
            collective_id=0, has_side_effects=True, vmem_limit_bytes=VMEM_BYTES
        ),
        cost_estimate=pl.CostEstimate(flops=15 * 10**8, bytes_accessed=5 * 10**6, transcendentals=300000),
        name="window_block",
    )(tokens, cotangent, ocean_mask, land_mask, w_qkv, w_proj, rel_bias)

    hbm = pl.BlockSpec(memory_space=pltpu.HBM)
    return tuple(
        pl.pallas_call(
            place_kernel,
            out_shape=[grid, grid] + [jax.ShapeDtypeStruct((n,), F32) for n in (864, 288, 96)],
            in_specs=[hbm] * 3,
            out_specs=[hbm] * 5,
            scratch_shapes=[
                pltpu.VMEM((8, 48, C), BF16),
                pltpu.VMEM((8, 48, C), BF16),
                pltpu.VMEM((16, 128), F32),
                pltpu.VMEM((864,), F32),
                pltpu.VMEM((288,), F32),
                pltpu.VMEM((96,), F32),
                dma((5,)),
                dma((7,)),
            ],
            compiler_params=pltpu.CompilerParams(vmem_limit_bytes=VMEM_BYTES),
            cost_estimate=pl.CostEstimate(flops=10**4, bytes_accessed=12 * 10**5, transcendentals=0),
            name="outputs",
        )(block_out, token_grad, red)
    )


def solution(mesh):
    split = ("band", "grp")
    placed = (
        P(split, None, None),
        P(split, None, None),
        P(split, None),
        P(split, None),
        P(),
        P(),
        P(),
    )
    return jax.shard_map(
        local,
        mesh=mesh,
        in_specs=placed,
        out_specs=(P(split, None, None), P(split, None, None), P(split), P(split), P(split)),
        check_vma=False,
    )
```

```python
import math

import jax
import jax.numpy as jnp
from jax import lax
from jax.experimental import pallas as pl
from jax.experimental.pallas import tpu as pltpu
from jax.sharding import PartitionSpec as P

EPS = 1e-05
MASKED = -1e30
C = 384
WB = 6
HG = 3
SCALE = 1.0 / math.sqrt(32)
F32 = jnp.float32
BF16 = jnp.bfloat16
MESH = pl.DeviceIdType.MESH

NY, NX, NZ = 8, 4, 8
OWN = 192
VMEM_BYTES = 62 * 2**20


def qkv_rows(g):
    return [("qkv", j, k) for k in (g, 3 + g) for j in range(3)]


PROJ_ROWS = [("proj", j, k) for k in range(3) for j in range(3)]
BIAS_ROWS = [("bias", j, 0) for j in range(3)]
V_ROWS = [("qkv", j, 6 + g) for g in range(3) for j in range(3)]
GROUPS = [PROJ_ROWS + V_ROWS, qkv_rows(0) + qkv_rows(1), qkv_rows(2) + BIAS_ROWS]
SLOTS = 13
X_ORDER = (2, 1, 3)
Y_ORDER = (4, 3, 5, 2, 6, 1, 7)
Z_ORDER = (4, 3, 5, 2, 6, 1, 7, 0)


def owned(g):
    qkv = [min(27 * g // 4 + i, 26) for i in range(8)]
    proj = [min(9 * g // 4 + i, 8) for i in range(3)]
    bias = [min(3 * g // 4 + i, 2) for i in range(2)]
    return (
        [("qkv", r // 9, r % 9) for r in qkv]
        + [("proj", r // 3, r % 3) for r in proj]
        + [("bias", r, 0) for r in bias]
    )


def dot_nt(a, b):
    return lax.dot_general(a, b, (((1,), (1,)), ((), ())), preferred_element_type=F32)


def dot_tn(a, b):
    return lax.dot_general(a, b, (((0,), (0,)), ((), ())), preferred_element_type=F32)


def dot_nn(a, b):
    return lax.dot_general(a, b, (((1,), (0,)), ((), ())), preferred_element_type=F32)


def stage_mask(ocean, land, half, mask_ref):
    place = lax.broadcasted_iota(jnp.int32, (8, 48), 0)
    column = lax.broadcasted_iota(jnp.int32, (8, 48), 1)
    for w in range(WB):
        live = 1.0 - land[:, w : w + 1]
        pick = (column == lax.rem(place + (8 * w + 4), 48)).astype(F32) * live
        for i in range(4):
            row = jnp.broadcast_to(ocean[i : i + 1, :], (8, 48))
            value = jnp.sum(row * pick, axis=1, keepdims=True)
            at = OWN * half + 32 * w + 8 * i
            mask_ref[at : at + 8, :] = jnp.broadcast_to(value, (8, 128))


def stage_rows(rows, half, out_ref):
    for i, row in enumerate(rows):
        rolled = pltpu.roll(row.astype(F32), 44, 0)
        for w in range(WB):
            at = OWN * half + 32 * w + 8 * i
            out_ref[at : at + 8, :] = rolled[8 * w : 8 * w + 8, :]


def grid_row(src_ref, half, i):
    ats = [OWN * half + 32 * w + 8 * i for w in range(WB)]
    return pltpu.roll(jnp.concatenate([src_ref[at : at + 8, :] for at in ats], 0), 4, 0)


class Group:
    def __init__(self, rows, base, pk_ref, refs, here, plan):
        self.rows, self.n, self.base, self.pk = rows, len(rows), base, pk_ref
        self.pack, self.r0, self.s1, self.rx, core_s, core_r, x_s, x_r = refs
        band, grp, y, x, z, core = here
        self.theirs = pl.ds(pl.multiple_of((1 - core) * 64, 64), 64)
        self.mine = pl.ds(pl.multiple_of(core * 64, 64), 64)
        self.own = pl.ds(pl.multiple_of(16 * x, 16), 16)
        self.core_copy = plan(self.pack, self.r0, core_s.at[0], core_r.at[0], (band, z * 2 + 1 - core))
        self.sent = []
        for d in X_ORDER:
            to = lax.rem(x + d, NX)
            part = self.s1.at[:, pl.ds(pl.multiple_of(16 * to, 16), 16), :]
            self.sent.append(plan(part, self.rx.at[d - 1], x_s.at[d - 1], x_r.at[d - 1], (y * NX + to, grp)))

    def start(self):
        def narrow(i, carry):
            self.pack[i] = self.pk[self.base + i, self.theirs, :].astype(BF16)
            return carry

        lax.fori_loop(0, self.n, narrow, 0, unroll=2)
        self.core_copy.start()

    def spread(self):
        self.core_copy.wait()

        def add(i, carry):
            total = self.pk[self.base + i, self.mine, :] + self.r0[i].astype(F32)
            self.s1[i] = total.astype(BF16)
            return carry

        lax.fori_loop(0, self.n, add, 0, unroll=2)
        for copy in self.sent:
            copy.start()

    def take(self, wide_ref, padded):
        total = self.s1[:, self.own, :].astype(F32)
        for copy, d in zip(self.sent, X_ORDER):
            copy.wait_recv()
            total = total + self.rx[d - 1].astype(F32)
        for i in range(self.n):
            for quarter in range(2):
                at = pl.ds(quarter * padded + i, NY, stride=2 * padded)
                wide_ref[at, :] = total[i, 8 * quarter : 8 * quarter + 8, :]


def padded_of(n):
    return -(-n // 8) * 8


class Turn:
    def __init__(self, group, refs, here, plan):
        self.group, self.rows, self.padded = group, group.rows, padded_of(group.n)
        self.wide, self.tb, self.ry, y_s, y_r = refs
        band, grp, y, x, z, core = here
        n = 2 * self.padded
        self.own = pl.ds(pl.multiple_of(y * n, 8), n)
        self.sent = []
        for d in Y_ORDER:
            to = lax.rem(y + d, NY)
            self.sent.append(
                plan(self.tb.at[to], self.ry.at[d - 1], y_s.at[d - 1], y_r.at[d - 1], (to * NX + x, grp))
            )

    def clear(self):
        for i in range(len(self.rows), self.padded):
            for quarter in range(2):
                at = pl.ds(quarter * self.padded + i, NY, stride=2 * self.padded)
                self.wide[at, :] = jnp.zeros((NY, 128), F32)

    def start(self):
        n = 2 * self.padded
        self.group.take(self.wide, self.padded)
        for i in range(NY):
            self.tb[i] = self.wide[n * i : n * (i + 1), :].astype(BF16)
        for copy in self.sent:
            copy.start()

    def collect(self, f_ref):
        total = self.wide[self.own, :]
        for copy, d in zip(self.sent, Y_ORDER):
            copy.wait_recv()
            total = total + self.ry[d - 1].astype(F32)
        for i in range(8):
            for at, row in enumerate(owned(i % 4)):
                if row in self.rows:
                    first = self.padded * (i // 4) + self.rows.index(row)
                    f_ref[i, at : at + 1, :] = total[first : first + 1, :]


class Share:
    def __init__(self, wide_ref, f_ref, r3_ref, z_s, z_r, here):
        self.wide, self.f, self.r3, self.z_s, self.z_r, self.here = wide_ref, f_ref, r3_ref, z_s, z_r, here

    def copies(self):
        band, grp, y, x, z, core = self.here
        for d in Z_ORDER:
            to_z = lax.rem(z + d, NZ)
            for to_core in range(2):
                i = 2 * lax.rem(to_z, 4) + to_core
                copy = pltpu.make_async_remote_copy(
                    src_ref=self.f.at[i],
                    dst_ref=self.r3.at[z],
                    send_sem=self.z_s.at[i],
                    recv_sem=self.z_r.at[z],
                    device_id=(band, to_z * 2 + to_core),
                    device_id_type=MESH,
                )
                away = to_z // 4 == core
                if d == 0:
                    away = jnp.logical_and(away, core != to_core)
                yield copy, away

    def start(self):
        self.f[...] = self.wide[...].astype(BF16)
        for copy, away in self.copies():
            pl.when(away)(copy.start)

    def finish(self, red_ref):
        band, grp, y, x, z, core = self.here
        own_core = z // 4

        @pl.when(core == own_core)
        def _():
            self.r3[z] = self.f[4 * lax.rem(z // 2, 2) + lax.rem(grp, 4)]

        for s in range(NZ):
            come = pltpu.make_async_remote_copy(
                src_ref=self.f.at[0],
                dst_ref=self.r3.at[s],
                send_sem=self.z_s.at[0],
                recv_sem=self.z_r.at[s],
                device_id=(band, z * 2 + 1 - core),
                device_id_type=MESH,
            )
            pl.when(jnp.logical_or(z != s, core != own_core))(come.wait_recv)
        total = self.r3[0].astype(F32)
        for s in range(1, NZ):
            total = total + self.r3[s].astype(F32)
        red_ref[...] = total

    def drain(self):
        for copy, away in self.copies():
            pl.when(away)(copy.wait_send)


def group_scratch(n):
    dma = pltpu.SemaphoreType.DMA
    return [
        pltpu.VMEM((n, 64, 128), BF16),
        pltpu.VMEM((n, 64, 128), BF16),
        pltpu.VMEM((n, 64, 128), BF16),
        pltpu.VMEM((NX - 1, n, 16, 128), BF16),
        dma((1,)), dma((1,)), dma((NX - 1,)), dma((NX - 1,)),
    ]


def turn_scratch(n):
    dma = pltpu.SemaphoreType.DMA
    wide = 2 * padded_of(n)
    return [
        pltpu.VMEM((NY * wide, 128), F32),
        pltpu.VMEM((NY, wide, 128), BF16),
        pltpu.VMEM((NY - 1, wide, 128), BF16),
        dma((NY - 1,)), dma((NY - 1,)),
    ]


def permutation():
    at = lax.broadcasted_iota(jnp.int32, (C, C), 0)
    feature = lax.broadcasted_iota(jnp.int32, (C, C), 1)

    def bits(low, count):
        return lax.bitwise_and(lax.shift_right_logical(at, jnp.full_like(at, low)), (1 << count) - 1)

    m = 16 * bits(0, 3) + bits(3, 1) + 4 * bits(4, 2) + 2 * bits(6, 1)
    return (feature == 3 * m + bits(7, 2)).astype(F32).astype(BF16)


def kernel(
    tok_hbm, cot_hbm, oce_hbm, land_hbm, wqkv_hbm, wproj_hbm, rb_hbm,
    block_hbm, grad_hbm, red_hbm,
    block_ref, grad_out_ref, red_ref,
    tok_ref, cot_ref, oce_ref, land_ref, wqkv_ref, wproj_ref, rb_ref,
    htok_ref, hcot_ref, hoce_ref, uu_ref, ug_ref, hu_ref, hg_ref,
    x_ref, c_ref, n_ref, inv_ref, mask_ref, h_ref, ht_ref, qkv_ref, dz_ref, do_ref, o_ref, dqkv_ref, ot_ref,
    p_ref, bias_ref, db_ref, perm_ref, pk_ref, bt_ref, f_ref, low_ref, r3_ref, load_sem, store_sem, halo_s, halo_r, z_s, z_r, near_sem, *rest,
):
    band = lax.axis_index("band")
    grp = lax.axis_index("grp")
    y, x = band // NX, lax.rem(band, NX)
    z, core = grp // 2, lax.rem(grp, 2)
    linear = band * 16 + grp
    after = lax.rem(linear + 1, 512)
    before = lax.rem(linear + 511, 512)
    after_id = (after // 16, lax.rem(after, 16))
    before_id = (before // 16, lax.rem(before, 16))

    barrier = pltpu.get_barrier_semaphore()


    def at_z(d):
        return (band, lax.rem(z + NZ + d, NZ) * 2 + core)

    def at_y(d):
        return (lax.rem(y + NY + d, NY) * NX + x, grp)

    def at_x(d):
        return (y * NX + lax.rem(x + NX + d, NX), grp)

    peers = [after_id, before_id, (band, z * 2 + 1 - core)]
    peers += [at(d) for at in (at_z, at_y, at_x) for d in (1, -1)]
    for peer in peers:
        pl.semaphore_signal(barrier, inc=1, device_id=peer, device_id_type=MESH)

    def blocks(i, j):
        to = 256 * j + 128 * i if i < 2 else 768 + 128 * j
        return wqkv_hbm.at[:, pl.ds(C * i + 128 * j, 128)], wqkv_ref.at[:, pl.ds(to, 128)]

    loads = []
    for i, (src, dst) in enumerate(
        [(tok_hbm, tok_ref), (oce_hbm, oce_ref), (land_hbm, land_ref), (cot_hbm, cot_ref)]
        + [(wproj_hbm, wproj_ref), (rb_hbm, rb_ref)]
        + [blocks(i, j) for j in range(HG) for i in range(3)]
    ):
        loads.append(pltpu.make_async_copy(src, dst, load_sem.at[i]))
        loads[-1].start()

    def tell(r, at, d):
        for to in (at(d), at(-d)):
            pl.semaphore_signal(near_sem.at[r], inc=1, device_id=to, device_id_type=MESH)

    def plan(src, dst, s, r, to):
        return pltpu.make_async_remote_copy(
            src_ref=src, dst_ref=dst, send_sem=s, recv_sem=r, device_id=to, device_id_type=MESH
        )

    def send(*args):
        copy = plan(*args)
        copy.start()
        return copy

    kept = []

    def keep(src, dst):
        kept.append(pltpu.make_async_copy(src, dst, store_sem.at[len(kept)]))
        kept[-1].start()

    pl.semaphore_wait(barrier, len(peers))
    tell(0, at_z, 1)
    tell(1, at_y, 1)
    tell(2, at_x, 1)
    far = (2, 3, 4)
    halos = [
        send(tok_hbm.at[pl.ds(0, 4)], htok_ref, halo_s.at[0], halo_r.at[0], before_id),
        send(oce_hbm, hoce_ref, halo_s.at[1], halo_r.at[1], before_id),
        send(cot_hbm.at[pl.ds(0, 4)], hcot_ref, halo_s.at[2], halo_r.at[2], before_id),
    ]

    loads[0].wait()
    stage_rows([tok_ref[4 + i] for i in range(4)], 0, x_ref)
    perm_ref[...] = permutation()

    def norm(i, carry):
        rows = pl.ds(pl.multiple_of(i * 64, 64), 64)
        value = x_ref[rows, :]
        centered = value - jnp.mean(value, -1, keepdims=True)
        inv = lax.rsqrt(jnp.mean(centered * centered, -1, keepdims=True) + EPS)
        n = centered * inv
        n_ref[rows, :] = n
        inv_ref[rows, :] = jnp.broadcast_to(inv, (64, 128))
        h_ref[rows, :] = n.astype(BF16)
        return carry

    def project(half):
        rows = slice(OWN * half, OWN * half + OWN)
        qkv_ref[rows, :] = dot_nn(h_ref[rows, :], wqkv_ref[...]).astype(BF16)

    def pull(half):
        rows = slice(OWN * half, OWN * half + OWN)
        wide = jnp.concatenate([mask_ref[rows, :]] * 3, 1)
        dz_ref[rows, :] = (wide * c_ref[rows, :]).astype(BF16)
        do_ref[rows, :] = dot_nt(dz_ref[rows, :], wproj_ref[...]).astype(BF16)

    lax.fori_loop(0, 3, norm, 0, unroll=3)
    loads[1].wait()
    loads[2].wait()
    land = land_ref[...].astype(F32)
    stage_mask(oce_ref[4:8, :].astype(F32), land, 0, mask_ref)
    for i in range(6, 15):
        loads[i].wait()
    project(0)
    loads[3].wait()
    stage_rows([cot_ref[4 + i] for i in range(4)], 0, c_ref)
    loads[4].wait()
    pull(0)
    loads[5].wait()
    for i in range(6):
        pair = jnp.concatenate([rb_ref[2 * i], rb_ref[2 * i + 1]], 0)
        bias_ref[:, 128 * i : 128 * i + 128] = pair.T
    db_ref[...] = jnp.zeros_like(db_ref)

    here_lower = jnp.broadcast_to(linear, (48, C)) < 511
    halos[0].wait_recv()
    stage_rows([jnp.where(here_lower, htok_ref[i].astype(F32), 0.0) for i in range(4)], 1, x_ref)
    lax.fori_loop(3, 6, norm, 0, unroll=3)
    project(1)
    for r in (0, 1):
        pl.semaphore_wait(near_sem.at[r], 2)
    tell(3, at_z, 2)
    tell(4, at_y, 2)
    ht_ref[...] = dot_nt(perm_ref[...], h_ref[...]).astype(BF16)
    halos[1].wait_recv()
    ocean = jnp.where(jnp.broadcast_to(linear, (4, 48)) < 511, hoce_ref[0:4, :].astype(F32), 0.0)
    stage_mask(ocean, land, 1, mask_ref)

    head = lax.broadcasted_iota(jnp.int32, (64, 128), 1) // 32
    picks = [(head == i).astype(F32) for i in range(4)]
    picks_low = [p.astype(BF16) for p in picks]

    def spread(a):
        return jnp.concatenate([a * p for p in picks_low], 0)

    def fold(value):
        total = value[0:64] * picks[0]
        for i in range(1, 4):
            total = total + value[64 * i : 64 * i + 64] * picks[i]
        return total

    def two(w):
        first = pl.ds(pl.multiple_of(w * 32, 32), 32)
        second = pl.ds(pl.multiple_of(OWN + w * 32, 32), 32)
        return first, second

    def load(ref, w, lanes):
        first, second = two(w)
        return jnp.concatenate([ref[first, lanes], ref[second, lanes]], 0)

    def store(ref, w, lanes, value):
        first, second = two(w)
        ref[first, lanes] = value[0:32]
        ref[second, lanes] = value[32:64]

    def lanes_of(g):
        firsts = (256 * g, 256 * g + 128, 768 + 128 * g)
        return [slice(first, first + 128) for first in firsts] + [
            slice(256 * g, 256 * g + 256),
            slice(128 * g, 128 * g + 128),
        ]

    def forward(w, carry):
        whole = pl.ds(pl.multiple_of(w * 64, 64), 64)
        live = jnp.concatenate([load(mask_ref, w, slice(0, 128))] * 2, 1) > 0.5
        for g in range(HG):
            q_lanes, k_lanes, v_lanes, wide, head_lanes = lanes_of(g)
            q4 = spread(load(qkv_ref, w, q_lanes))
            s = dot_nt(load(qkv_ref, w, k_lanes), q4) * SCALE + bias_ref[:, wide]
            s = jnp.where(live, s, MASKED)
            weights = jnp.exp(s - jnp.max(s, 0, keepdims=True))
            p = weights * (1.0 / jnp.sum(weights, 0, keepdims=True))
            p_ref[whole, wide] = p
            do4 = spread(load(do_ref, w, head_lanes))
            store(dqkv_ref, w, v_lanes, dot_nn(p.astype(BF16), do4).astype(BF16))
            store(o_ref, w, head_lanes, fold(dot_tn(p.astype(BF16), load(qkv_ref, w, v_lanes))).astype(BF16))
        return carry

    def backward(g):
        q_lanes, k_lanes, v_lanes, wide, head_lanes = lanes_of(g)

        def step(w, carry):
            whole = pl.ds(pl.multiple_of(w * 64, 64), 64)
            q4 = spread(load(qkv_ref, w, q_lanes))
            do4 = spread(load(do_ref, w, head_lanes))
            p = p_ref[whole, wide]
            dp = dot_nt(load(qkv_ref, w, v_lanes), do4)
            ds = p * (dp - jnp.sum(p * dp, 0, keepdims=True))
            db_ref[:, wide] += ds
            dsc = (ds * SCALE).astype(BF16)
            store(dqkv_ref, w, k_lanes, dot_nn(dsc, q4).astype(BF16))
            dq = fold(dot_tn(dsc, load(qkv_ref, w, k_lanes)))
            store(dqkv_ref, w, q_lanes, dq.astype(BF16))
            return carry

        lax.fori_loop(0, WB, step, 0, unroll=6)
        fill(18 + 6 * g, dot_nn(ht_ref[...], dqkv_ref[:, 256 * g : 256 * g + 256]))

    halos[2].wait_recv()
    stage_rows([jnp.where(here_lower, hcot_ref[i].astype(F32), 0.0) for i in range(4)], 1, c_ref)
    pull(1)
    lax.fori_loop(0, WB, forward, 0, unroll=2)


    here = (band, grp, y, x, z, core)
    groups, turns = [], []
    at = base = 0
    for rows in GROUPS:
        groups.append(Group(rows, base, pk_ref, rest[at : at + 8], here, plan))
        at += 8
        base += len(rows)
    for group in groups:
        turns.append(Turn(group, rest[at : at + 5], here, plan))
        at += 5
    share = Share(f_ref, low_ref, r3_ref, z_s, z_r, here)

    def fill(base, value):
        for k in range(value.shape[1] // 128):
            for j in range(3):
                pk_ref[base + 3 * k + j] = value[128 * j : 128 * j + 128, 128 * k : 128 * k + 128]

    ot_ref[...] = dot_nt(perm_ref[...], o_ref[...]).astype(BF16)
    fill(0, dot_nn(ot_ref[...], dz_ref[...]))
    for turn in turns:
        turn.clear()
    for i in range(8):
        f_ref[i, SLOTS:16, :] = jnp.zeros((16 - SLOTS, 128), F32)

    fill(9, dot_nn(ht_ref[...], dqkv_ref[:, 768 : 768 + C]))
    groups[0].start()
    backward(0)
    for r in far:
        pl.semaphore_wait(near_sem.at[r], 2)
    groups[0].spread()
    backward(1)
    groups[1].start()
    backward(2)
    for i in range(6):
        bt_ref[128 * i : 128 * i + 128, 0:64] = db_ref[:, 128 * i : 128 * i + 128].T
    lane = lax.broadcasted_iota(jnp.int32, (8, 128), 1)
    for j in range(3):
        for i in range(16):
            first = 2 * j + 24 * ((i // 2) % 4) + 12 * (i // 8) + 6 * (i % 2)
            even = bt_ref[pl.ds(first, 8, stride=96), :]
            odd = bt_ref[pl.ds(first + 1, 8, stride=96), :]
            pk_ref[36 + j, 8 * i : 8 * i + 8, :] = jnp.where(lane < 64, even, pltpu.roll(odd, 64, 1))
    groups[2].start()
    groups[1].spread()

    wide_mask = jnp.concatenate([mask_ref[...]] * 3, 1)
    x_ref[...] = wide_mask * dot_nn(o_ref[...], wproj_ref[...])
    groups[2].spread()
    turns[0].start()
    for i in range(4):
        uu_ref[i] = grid_row(x_ref, 1, i).astype(BF16)
    c_ref[...] = dot_nt(dqkv_ref[...], wqkv_ref[...])

    def back(i, carry):
        rows = pl.ds(pl.multiple_of(i * 64, 64), 64)
        dh = c_ref[rows, :]
        n = n_ref[rows, :]
        inv = jnp.concatenate([inv_ref[rows, :]] * 3, 1)
        slope = jnp.mean(dh * n, -1, keepdims=True)
        c_ref[rows, :] = inv * (dh - jnp.mean(dh, -1, keepdims=True) - n * slope)
        return carry

    lax.fori_loop(0, WB, back, 0, unroll=3)
    for i in range(4):
        ug_ref[i] = grid_row(c_ref, 1, i).astype(BF16)
    turns[1].start()
    turns[2].start()
    halo_u = send(uu_ref, hu_ref, halo_s.at[3], halo_r.at[3], after_id)
    halo_g = send(ug_ref, hg_ref, halo_s.at[4], halo_r.at[4], after_id)
    turns[0].collect(f_ref)
    for i in range(4):
        row = grid_row(x_ref, 0, i).astype(BF16).astype(F32)
        block_ref[4 + i] = (tok_ref[4 + i].astype(F32) + row).astype(BF16)
        row = grid_row(c_ref, 0, i).astype(BF16).astype(F32)
        grad_out_ref[4 + i] = (cot_ref[4 + i].astype(F32) + row).astype(BF16)
    upper, lower = pl.ds(4, 4), pl.ds(0, 4)
    keep(block_ref.at[upper], block_hbm.at[upper])
    keep(grad_out_ref.at[upper], grad_hbm.at[upper])
    turns[1].collect(f_ref)
    turns[2].collect(f_ref)
    share.start()
    inner = jnp.broadcast_to(linear, (4, 48, C)) > 0
    halo_u.wait_recv()
    low = jnp.where(inner, hu_ref[...].astype(F32), 0.0)
    block_ref[0:4] = (tok_ref[0:4].astype(F32) + low).astype(BF16)
    keep(block_ref.at[lower], block_hbm.at[lower])
    halo_g.wait_recv()
    low = jnp.where(inner, hg_ref[...].astype(F32), 0.0)
    grad_out_ref[0:4] = (cot_ref[0:4].astype(F32) + low).astype(BF16)
    keep(grad_out_ref.at[lower], grad_hbm.at[lower])
    for one in groups + turns:
        for copy in one.sent:
            copy.wait_send()
    share.finish(red_ref)
    keep(red_ref, red_hbm)
    share.drain()
    for copy in halos + [halo_u, halo_g]:
        copy.wait_send()
    for copy in kept:
        copy.wait()


def place_kernel(
    block_hbm, grad_hbm, red_hbm, block_out, grad_out, qkv_out, proj_out, bias_out,
    block_ref, grad_ref, red_ref, qkv_ref, proj_ref, bias_ref, in_sem, out_sem,
):
    load = pltpu.make_async_copy(red_hbm, red_ref, in_sem.at[4])
    load.start()
    moves = []
    for i, (src, via, dst) in enumerate(((block_hbm, block_ref, block_out), (grad_hbm, grad_ref, grad_out))):
        for j in range(2):
            part = pl.ds(4 * j, 4)
            into = pltpu.make_async_copy(src.at[part], via.at[part], in_sem.at[2 * i + j])
            into.start()
            moves.append((into, pltpu.make_async_copy(via.at[part], dst.at[part], out_sem.at[2 * i + j])))
    load.wait()
    g = lax.rem(lax.axis_index("grp"), 4)
    lane = lax.broadcasted_iota(jnp.int32, (16, 128), 1)
    red = red_ref[...]
    following = jnp.concatenate([red[1:16], red[0:1]], 0)
    rolled = [red]
    for quarter in range(1, 4):
        shift = 128 - 32 * quarter
        value = jnp.where(lane < shift, pltpu.roll(red, shift, 1), pltpu.roll(following, shift, 1))
        rolled.append(value)

    def pick(step):
        which = jnp.broadcast_to(lax.rem(step * g, 4), (16, 128))
        value = rolled[0]
        for quarter in range(1, 4):
            value = jnp.where(which == quarter, rolled[quarter], value)
        return value

    for into, out in moves:
        into.wait()
        out.start()
    small = []
    for i, (ref, out, step, first, size) in enumerate(
        (
            (qkv_ref, qkv_out, 27, 0, 864),
            (proj_ref, proj_out, 9, 8, 288),
            (bias_ref, bias_out, 3, 11, 96),
        )
    ):
        value = pick(step)
        for j in range(-(-size // 128)):
            n = min(128, size - 128 * j)
            ref[pl.ds(128 * j, n)] = value[first + j, 0:n]
        small.append(pltpu.make_async_copy(ref, out, out_sem.at[4 + i]))
        small[-1].start()
    for out in [out for into, out in moves] + small:
        out.wait()


def local(tokens, cotangent, ocean_mask, land_mask, w_qkv, w_proj, rel_bias):
    grid = jax.ShapeDtypeStruct((8, 48, C), BF16)
    dma = pltpu.SemaphoreType.DMA
    half = pltpu.VMEM((4, 48, C), BF16)
    scratch = [
        pltpu.VMEM((8, 48, C), BF16),
        pltpu.VMEM((8, 48, C), BF16),
        pltpu.VMEM((16, 128), F32),
        pltpu.VMEM((8, 48, C), BF16),
        pltpu.VMEM((8, 48, C), BF16),
        pltpu.VMEM((8, 48), jnp.int32),
        pltpu.VMEM((1, 6), jnp.int32),
        pltpu.VMEM((C, 3 * C), BF16),
        pltpu.VMEM((C, C), BF16),
        pltpu.VMEM((12, 64, 64), F32),
        half, half, pltpu.VMEM((8, 48), jnp.int32), half, half, half, half,
        pltpu.VMEM((C, C), F32),
        pltpu.VMEM((C, C), F32),
        pltpu.VMEM((C, C), F32),
        pltpu.VMEM((C, 128), F32),
        pltpu.VMEM((C, 128), F32),
        pltpu.VMEM((C, C), BF16),
        pltpu.VMEM((C, C), BF16),
        pltpu.VMEM((C, 3 * C), BF16),
        pltpu.VMEM((C, C), BF16),
        pltpu.VMEM((C, C), BF16),
        pltpu.VMEM((C, C), BF16),
        pltpu.VMEM((C, 3 * C), BF16),
        pltpu.VMEM((C, C), BF16),
        pltpu.VMEM((C, 768), F32),
        pltpu.VMEM((64, 768), F32),
        pltpu.VMEM((64, 768), F32),
        pltpu.VMEM((C, C), BF16),
        pltpu.VMEM((39, 128, 128), F32),
        pltpu.VMEM((768, 128), F32),
        pltpu.VMEM((8, 16, 128), F32),
        pltpu.VMEM((8, 16, 128), BF16),
        pltpu.VMEM((NZ, 16, 128), BF16),
        dma((15,)), dma((5,)), dma((5,)), dma((5,)), dma((8,)), dma((NZ,)),
        pltpu.SemaphoreType.REGULAR((5,)),
    ]
    for rows in GROUPS:
        scratch += group_scratch(len(rows))
    for rows in GROUPS:
        scratch += turn_scratch(len(rows))
    block_out, token_grad, red = pl.pallas_call(
        kernel,
        out_shape=[grid, grid, jax.ShapeDtypeStruct((16, 128), F32)],
        in_specs=[pl.BlockSpec(memory_space=pltpu.HBM)] * 7,
        out_specs=[pl.BlockSpec(memory_space=pltpu.HBM)] * 3,
        scratch_shapes=scratch,
        compiler_params=pltpu.CompilerParams(
            collective_id=0, has_side_effects=True, vmem_limit_bytes=VMEM_BYTES
        ),
        cost_estimate=pl.CostEstimate(flops=15 * 10**8, bytes_accessed=5 * 10**6, transcendentals=300000),
        name="window_block",
    )(tokens, cotangent, ocean_mask, land_mask, w_qkv, w_proj, rel_bias)

    hbm = pl.BlockSpec(memory_space=pltpu.HBM)
    return tuple(
        pl.pallas_call(
            place_kernel,
            out_shape=[grid, grid] + [jax.ShapeDtypeStruct((n,), F32) for n in (864, 288, 96)],
            in_specs=[hbm] * 3,
            out_specs=[hbm] * 5,
            scratch_shapes=[
                pltpu.VMEM((8, 48, C), BF16),
                pltpu.VMEM((8, 48, C), BF16),
                pltpu.VMEM((16, 128), F32),
                pltpu.VMEM((864,), F32),
                pltpu.VMEM((288,), F32),
                pltpu.VMEM((96,), F32),
                dma((5,)),
                dma((7,)),
            ],
            compiler_params=pltpu.CompilerParams(vmem_limit_bytes=VMEM_BYTES),
            cost_estimate=pl.CostEstimate(flops=10**4, bytes_accessed=12 * 10**5, transcendentals=0),
            name="outputs",
        )(block_out, token_grad, red)
    )


def solution(mesh):
    split = ("band", "grp")
    placed = (
        P(split, None, None),
        P(split, None, None),
        P(split, None),
        P(split, None),
        P(),
        P(),
        P(),
    )
    return jax.shard_map(
        local,
        mesh=mesh,
        in_specs=placed,
        out_specs=(P(split, None, None), P(split, None, None), P(split), P(split), P(split)),
        check_vma=False,
    )
```

```python
import math

import jax
import jax.numpy as jnp
from jax import lax
from jax.experimental import pallas as pl
from jax.experimental.pallas import tpu as pltpu
from jax.sharding import PartitionSpec as P

EPS = 1e-05
MASKED = -1e30
C = 384
WB = 6
HG = 3
SCALE = 1.0 / math.sqrt(32)
F32 = jnp.float32
BF16 = jnp.bfloat16
MESH = pl.DeviceIdType.MESH

NY, NX, NZ = 8, 4, 8
OWN = 192
VMEM_BYTES = 62 * 2**20


def qkv_rows(g):
    return [("qkv", j, k) for k in (g, 3 + g, 6 + g) for j in range(3)]


PROJ_ROWS = [("proj", j, k) for k in range(3) for j in range(3)]
BIAS_ROWS = [("bias", j, 0) for j in range(3)]
GROUPS = [PROJ_ROWS + qkv_rows(0), qkv_rows(1)[:8], qkv_rows(1)[8:] + qkv_rows(2) + BIAS_ROWS]
SLOTS = 13
X_ORDER = (2, 1, 3)
Y_ORDER = (4, 3, 5, 2, 6, 1, 7)
Z_ORDER = (4, 3, 5, 2, 6, 1, 7, 0)


def owned(g):
    qkv = [min(27 * g // 4 + i, 26) for i in range(8)]
    proj = [min(9 * g // 4 + i, 8) for i in range(3)]
    bias = [min(3 * g // 4 + i, 2) for i in range(2)]
    return (
        [("qkv", r // 9, r % 9) for r in qkv]
        + [("proj", r // 3, r % 3) for r in proj]
        + [("bias", r, 0) for r in bias]
    )


def dot_nt(a, b):
    return lax.dot_general(a, b, (((1,), (1,)), ((), ())), preferred_element_type=F32)


def dot_tn(a, b):
    return lax.dot_general(a, b, (((0,), (0,)), ((), ())), preferred_element_type=F32)


def dot_nn(a, b):
    return lax.dot_general(a, b, (((1,), (0,)), ((), ())), preferred_element_type=F32)


def stage_mask(ocean, land, half, mask_ref):
    place = lax.broadcasted_iota(jnp.int32, (8, 48), 0)
    column = lax.broadcasted_iota(jnp.int32, (8, 48), 1)
    for w in range(WB):
        live = 1.0 - land[:, w : w + 1]
        pick = (column == lax.rem(place + (8 * w + 4), 48)).astype(F32) * live
        for i in range(4):
            row = jnp.broadcast_to(ocean[i : i + 1, :], (8, 48))
            value = jnp.sum(row * pick, axis=1, keepdims=True)
            at = OWN * half + 32 * w + 8 * i
            mask_ref[at : at + 8, :] = jnp.broadcast_to(value, (8, 128))


def stage_rows(rows, half, out_ref):
    for i, row in enumerate(rows):
        rolled = pltpu.roll(row.astype(F32), 44, 0)
        for w in range(WB):
            at = OWN * half + 32 * w + 8 * i
            out_ref[at : at + 8, :] = rolled[8 * w : 8 * w + 8, :]


def grid_row(src_ref, half, i):
    ats = [OWN * half + 32 * w + 8 * i for w in range(WB)]
    return pltpu.roll(jnp.concatenate([src_ref[at : at + 8, :] for at in ats], 0), 4, 0)


class Group:
    def __init__(self, rows, base, pk_ref, refs, here, plan):
        self.rows, self.n, self.base, self.pk = rows, len(rows), base, pk_ref
        self.pack, self.r0, self.s1, self.rx, core_s, core_r, x_s, x_r = refs
        band, grp, y, x, z, core = here
        self.theirs = pl.ds(pl.multiple_of((1 - core) * 64, 64), 64)
        self.mine = pl.ds(pl.multiple_of(core * 64, 64), 64)
        self.own = pl.ds(pl.multiple_of(16 * x, 16), 16)
        self.core_copy = plan(self.pack, self.r0, core_s.at[0], core_r.at[0], (band, z * 2 + 1 - core))
        self.sent = []
        for d in X_ORDER:
            to = lax.rem(x + d, NX)
            part = self.s1.at[:, pl.ds(pl.multiple_of(16 * to, 16), 16), :]
            self.sent.append(plan(part, self.rx.at[d - 1], x_s.at[d - 1], x_r.at[d - 1], (y * NX + to, grp)))

    def start(self):
        def narrow(i, carry):
            self.pack[i] = self.pk[self.base + i, self.theirs, :].astype(BF16)
            return carry

        lax.fori_loop(0, self.n, narrow, 0, unroll=2)
        self.core_copy.start()

    def spread(self):
        self.core_copy.wait()

        def add(i, carry):
            total = self.pk[self.base + i, self.mine, :] + self.r0[i].astype(F32)
            self.s1[i] = total.astype(BF16)
            return carry

        lax.fori_loop(0, self.n, add, 0, unroll=2)
        for copy in self.sent:
            copy.start()

    def take(self, wide_ref, padded):
        total = self.s1[:, self.own, :].astype(F32)
        for copy, d in zip(self.sent, X_ORDER):
            copy.wait_recv()
            total = total + self.rx[d - 1].astype(F32)
        for i in range(self.n):
            for quarter in range(2):
                at = pl.ds(quarter * padded + i, NY, stride=2 * padded)
                wide_ref[at, :] = total[i, 8 * quarter : 8 * quarter + 8, :]


def padded_of(n):
    return -(-n // 8) * 8


class Turn:
    def __init__(self, group, refs, here, plan):
        self.group, self.rows, self.padded = group, group.rows, padded_of(group.n)
        self.wide, self.tb, self.ry, y_s, y_r = refs
        band, grp, y, x, z, core = here
        n = 2 * self.padded
        self.own = pl.ds(pl.multiple_of(y * n, 8), n)
        self.sent = []
        for d in Y_ORDER:
            to = lax.rem(y + d, NY)
            self.sent.append(
                plan(self.tb.at[to], self.ry.at[d - 1], y_s.at[d - 1], y_r.at[d - 1], (to * NX + x, grp))
            )

    def clear(self):
        for i in range(len(self.rows), self.padded):
            for quarter in range(2):
                at = pl.ds(quarter * self.padded + i, NY, stride=2 * self.padded)
                self.wide[at, :] = jnp.zeros((NY, 128), F32)

    def start(self):
        n = 2 * self.padded
        self.group.take(self.wide, self.padded)
        for i in range(NY):
            self.tb[i] = self.wide[n * i : n * (i + 1), :].astype(BF16)
        for copy in self.sent:
            copy.start()

    def collect(self, f_ref):
        total = self.wide[self.own, :]
        for copy, d in zip(self.sent, Y_ORDER):
            copy.wait_recv()
            total = total + self.ry[d - 1].astype(F32)
        for i in range(8):
            for at, row in enumerate(owned(i % 4)):
                if row in self.rows:
                    first = self.padded * (i // 4) + self.rows.index(row)
                    f_ref[i, at : at + 1, :] = total[first : first + 1, :]


class Share:
    def __init__(self, wide_ref, f_ref, r3_ref, z_s, z_r, here):
        self.wide, self.f, self.r3, self.z_s, self.z_r, self.here = wide_ref, f_ref, r3_ref, z_s, z_r, here

    def copies(self):
        band, grp, y, x, z, core = self.here
        for d in Z_ORDER:
            to_z = lax.rem(z + d, NZ)
            for to_core in range(2):
                i = 2 * lax.rem(to_z, 4) + to_core
                copy = pltpu.make_async_remote_copy(
                    src_ref=self.f.at[i],
                    dst_ref=self.r3.at[z],
                    send_sem=self.z_s.at[i],
                    recv_sem=self.z_r.at[z],
                    device_id=(band, to_z * 2 + to_core),
                    device_id_type=MESH,
                )
                away = to_z // 4 == core
                if d == 0:
                    away = jnp.logical_and(away, core != to_core)
                yield copy, away

    def start(self):
        self.f[...] = self.wide[...].astype(BF16)
        for copy, away in self.copies():
            pl.when(away)(copy.start)

    def finish(self, red_ref):
        band, grp, y, x, z, core = self.here
        own_core = z // 4

        @pl.when(core == own_core)
        def _():
            self.r3[z] = self.f[4 * lax.rem(z // 2, 2) + lax.rem(grp, 4)]

        for s in range(NZ):
            come = pltpu.make_async_remote_copy(
                src_ref=self.f.at[0],
                dst_ref=self.r3.at[s],
                send_sem=self.z_s.at[0],
                recv_sem=self.z_r.at[s],
                device_id=(band, z * 2 + 1 - core),
                device_id_type=MESH,
            )
            pl.when(jnp.logical_or(z != s, core != own_core))(come.wait_recv)
        total = self.r3[0].astype(F32)
        for s in range(1, NZ):
            total = total + self.r3[s].astype(F32)
        red_ref[...] = total

    def drain(self):
        for copy, away in self.copies():
            pl.when(away)(copy.wait_send)


def group_scratch(n):
    dma = pltpu.SemaphoreType.DMA
    return [
        pltpu.VMEM((n, 64, 128), BF16),
        pltpu.VMEM((n, 64, 128), BF16),
        pltpu.VMEM((n, 64, 128), BF16),
        pltpu.VMEM((NX - 1, n, 16, 128), BF16),
        dma((1,)), dma((1,)), dma((NX - 1,)), dma((NX - 1,)),
    ]


def turn_scratch(n):
    dma = pltpu.SemaphoreType.DMA
    wide = 2 * padded_of(n)
    return [
        pltpu.VMEM((NY * wide, 128), F32),
        pltpu.VMEM((NY, wide, 128), BF16),
        pltpu.VMEM((NY - 1, wide, 128), BF16),
        dma((NY - 1,)), dma((NY - 1,)),
    ]


def permutation():
    at = lax.broadcasted_iota(jnp.int32, (C, C), 0)
    feature = lax.broadcasted_iota(jnp.int32, (C, C), 1)

    def bits(low, count):
        return lax.bitwise_and(lax.shift_right_logical(at, jnp.full_like(at, low)), (1 << count) - 1)

    m = 16 * bits(0, 3) + bits(3, 1) + 4 * bits(4, 2) + 2 * bits(6, 1)
    return (feature == 3 * m + bits(7, 2)).astype(F32).astype(BF16)


def kernel(
    tok_hbm, cot_hbm, oce_hbm, land_hbm, wqkv_hbm, wproj_hbm, rb_hbm,
    block_hbm, grad_hbm, red_hbm,
    block_ref, grad_out_ref, red_ref,
    tok_ref, cot_ref, oce_ref, land_ref, wqkv_ref, wproj_ref, rb_ref,
    htok_ref, hcot_ref, hoce_ref, uu_ref, ug_ref, hu_ref, hg_ref,
    x_ref, c_ref, n_ref, inv_ref, mask_ref, h_ref, ht_ref, qkv_ref, dz_ref, do_ref, o_ref, dqkv_ref, ot_ref,
    p_ref, bias_ref, db_ref, perm_ref, pk_ref, bt_ref, f_ref, low_ref, r3_ref, load_sem, store_sem, halo_s, halo_r, z_s, z_r, near_sem, *rest,
):
    band = lax.axis_index("band")
    grp = lax.axis_index("grp")
    y, x = band // NX, lax.rem(band, NX)
    z, core = grp // 2, lax.rem(grp, 2)
    linear = band * 16 + grp
    after = lax.rem(linear + 1, 512)
    before = lax.rem(linear + 511, 512)
    after_id = (after // 16, lax.rem(after, 16))
    before_id = (before // 16, lax.rem(before, 16))

    barrier = pltpu.get_barrier_semaphore()


    def at_z(d):
        return (band, lax.rem(z + NZ + d, NZ) * 2 + core)

    def at_y(d):
        return (lax.rem(y + NY + d, NY) * NX + x, grp)

    def at_x(d):
        return (y * NX + lax.rem(x + NX + d, NX), grp)

    peers = [after_id, before_id, (band, z * 2 + 1 - core)]
    peers += [at(d) for at in (at_z, at_y, at_x) for d in (1, -1)]
    for peer in peers:
        pl.semaphore_signal(barrier, inc=1, device_id=peer, device_id_type=MESH)

    def blocks(ref, i, j):
        return ref.at[:, pl.ds(C * i + 128 * j, 128)]

    loads = []
    for i, (src, dst) in enumerate(
        [(tok_hbm, tok_ref), (oce_hbm, oce_ref), (land_hbm, land_ref), (cot_hbm, cot_ref)]
        + [(wproj_hbm, wproj_ref), (rb_hbm, rb_ref)]
        + [(blocks(wqkv_hbm, i, j), blocks(wqkv_ref, j, i)) for j in range(HG) for i in range(3)]
    ):
        loads.append(pltpu.make_async_copy(src, dst, load_sem.at[i]))
        loads[-1].start()

    def tell(r, at, d):
        for to in (at(d), at(-d)):
            pl.semaphore_signal(near_sem.at[r], inc=1, device_id=to, device_id_type=MESH)

    def plan(src, dst, s, r, to):
        return pltpu.make_async_remote_copy(
            src_ref=src, dst_ref=dst, send_sem=s, recv_sem=r, device_id=to, device_id_type=MESH
        )

    def send(*args):
        copy = plan(*args)
        copy.start()
        return copy

    kept = []

    def keep(src, dst):
        kept.append(pltpu.make_async_copy(src, dst, store_sem.at[len(kept)]))
        kept[-1].start()

    pl.semaphore_wait(barrier, len(peers))
    tell(0, at_z, 1)
    tell(1, at_y, 1)
    tell(2, at_x, 1)
    far = (2, 3, 4)
    halos = [
        send(tok_hbm.at[pl.ds(0, 4)], htok_ref, halo_s.at[0], halo_r.at[0], before_id),
        send(oce_hbm, hoce_ref, halo_s.at[1], halo_r.at[1], before_id),
        send(cot_hbm.at[pl.ds(0, 4)], hcot_ref, halo_s.at[2], halo_r.at[2], before_id),
    ]

    loads[0].wait()
    stage_rows([tok_ref[4 + i] for i in range(4)], 0, x_ref)
    perm_ref[...] = permutation()

    def norm(i, carry):
        rows = pl.ds(pl.multiple_of(i * 64, 64), 64)
        value = x_ref[rows, :]
        centered = value - jnp.mean(value, -1, keepdims=True)
        inv = lax.rsqrt(jnp.mean(centered * centered, -1, keepdims=True) + EPS)
        n = centered * inv
        n_ref[rows, :] = n
        inv_ref[rows, :] = jnp.broadcast_to(inv, (64, 128))
        h_ref[rows, :] = n.astype(BF16)
        return carry

    def project(half):
        rows = slice(OWN * half, OWN * half + OWN)
        qkv_ref[rows, :] = dot_nn(h_ref[rows, :], wqkv_ref[...]).astype(BF16)

    def pull(half):
        rows = slice(OWN * half, OWN * half + OWN)
        wide = jnp.concatenate([mask_ref[rows, :]] * 3, 1)
        dz_ref[rows, :] = (wide * c_ref[rows, :]).astype(BF16)
        do_ref[rows, :] = dot_nt(dz_ref[rows, :], wproj_ref[...]).astype(BF16)

    lax.fori_loop(0, 3, norm, 0, unroll=3)
    loads[1].wait()
    loads[2].wait()
    land = land_ref[...].astype(F32)
    stage_mask(oce_ref[4:8, :].astype(F32), land, 0, mask_ref)
    for i in range(6, 15):
        loads[i].wait()
    project(0)
    loads[3].wait()
    stage_rows([cot_ref[4 + i] for i in range(4)], 0, c_ref)
    loads[4].wait()
    pull(0)
    loads[5].wait()
    for i in range(6):
        pair = jnp.concatenate([rb_ref[2 * i], rb_ref[2 * i + 1]], 0)
        bias_ref[:, 128 * i : 128 * i + 128] = pair.T
    db_ref[...] = jnp.zeros_like(db_ref)

    here_lower = jnp.broadcast_to(linear, (48, C)) < 511
    halos[0].wait_recv()
    stage_rows([jnp.where(here_lower, htok_ref[i].astype(F32), 0.0) for i in range(4)], 1, x_ref)
    lax.fori_loop(3, 6, norm, 0, unroll=3)
    project(1)
    for r in (0, 1):
        pl.semaphore_wait(near_sem.at[r], 2)
    tell(3, at_z, 2)
    tell(4, at_y, 2)
    ht_ref[...] = dot_nt(perm_ref[...], h_ref[...]).astype(BF16)
    halos[1].wait_recv()
    ocean = jnp.where(jnp.broadcast_to(linear, (4, 48)) < 511, hoce_ref[0:4, :].astype(F32), 0.0)
    stage_mask(ocean, land, 1, mask_ref)

    head = lax.broadcasted_iota(jnp.int32, (64, 128), 1) // 32
    picks = [(head == i).astype(F32) for i in range(4)]
    picks_low = [p.astype(BF16) for p in picks]

    def spread(a):
        return jnp.concatenate([a * p for p in picks_low], 0)

    def fold(value):
        total = value[0:64] * picks[0]
        for i in range(1, 4):
            total = total + value[64 * i : 64 * i + 64] * picks[i]
        return total

    def two(w):
        first = pl.ds(pl.multiple_of(w * 32, 32), 32)
        second = pl.ds(pl.multiple_of(OWN + w * 32, 32), 32)
        return first, second

    def load(ref, w, lanes):
        first, second = two(w)
        return jnp.concatenate([ref[first, lanes], ref[second, lanes]], 0)

    def store(ref, w, lanes, value):
        first, second = two(w)
        ref[first, lanes] = value[0:32]
        ref[second, lanes] = value[32:64]

    def lanes_of(g):
        return [slice(C * g + 128 * i, C * g + 128 * i + 128) for i in range(3)] + [
            slice(256 * g, 256 * g + 256),
            slice(128 * g, 128 * g + 128),
        ]

    def forward(w, carry):
        whole = pl.ds(pl.multiple_of(w * 64, 64), 64)
        live = jnp.concatenate([load(mask_ref, w, slice(0, 128))] * 2, 1) > 0.5
        for g in range(HG):
            q_lanes, k_lanes, v_lanes, wide, head_lanes = lanes_of(g)
            q4 = spread(load(qkv_ref, w, q_lanes))
            s = dot_nt(load(qkv_ref, w, k_lanes), q4) * SCALE + bias_ref[:, wide]
            s = jnp.where(live, s, MASKED)
            weights = jnp.exp(s - jnp.max(s, 0, keepdims=True))
            p = weights * (1.0 / jnp.sum(weights, 0, keepdims=True))
            p_ref[whole, wide] = p
            store(o_ref, w, head_lanes, fold(dot_tn(p.astype(BF16), load(qkv_ref, w, v_lanes))).astype(BF16))
        return carry

    def backward(g):
        q_lanes, k_lanes, v_lanes, wide, head_lanes = lanes_of(g)

        def step(w, carry):
            whole = pl.ds(pl.multiple_of(w * 64, 64), 64)
            q4 = spread(load(qkv_ref, w, q_lanes))
            do4 = spread(load(do_ref, w, head_lanes))
            p = p_ref[whole, wide]
            dp = dot_nt(load(qkv_ref, w, v_lanes), do4)
            store(dqkv_ref, w, v_lanes, dot_nn(p.astype(BF16), do4).astype(BF16))
            ds = p * (dp - jnp.sum(p * dp, 0, keepdims=True))
            db_ref[:, wide] += ds
            dsc = (ds * SCALE).astype(BF16)
            store(dqkv_ref, w, k_lanes, dot_nn(dsc, q4).astype(BF16))
            dq = fold(dot_tn(dsc, load(qkv_ref, w, k_lanes)))
            store(dqkv_ref, w, q_lanes, dq.astype(BF16))
            return carry

        lax.fori_loop(0, WB, step, 0, unroll=6)
        fill(9 + 9 * g, dot_nn(ht_ref[...], dqkv_ref[:, C * g : C * g + C]))

    lax.fori_loop(0, WB, forward, 0, unroll=3)

    halos[2].wait_recv()
    stage_rows([jnp.where(here_lower, hcot_ref[i].astype(F32), 0.0) for i in range(4)], 1, c_ref)
    pull(1)

    here = (band, grp, y, x, z, core)
    groups, turns = [], []
    at = base = 0
    for rows in GROUPS:
        groups.append(Group(rows, base, pk_ref, rest[at : at + 8], here, plan))
        at += 8
        base += len(rows)
    for group in groups:
        turns.append(Turn(group, rest[at : at + 5], here, plan))
        at += 5
    share = Share(f_ref, low_ref, r3_ref, z_s, z_r, here)

    def fill(base, value):
        for k in range(3):
            for j in range(3):
                pk_ref[base + 3 * k + j] = value[128 * j : 128 * j + 128, 128 * k : 128 * k + 128]

    ot_ref[...] = dot_nt(perm_ref[...], o_ref[...]).astype(BF16)
    fill(0, dot_nn(ot_ref[...], dz_ref[...]))
    for turn in turns:
        turn.clear()
    for i in range(8):
        f_ref[i, SLOTS:16, :] = jnp.zeros((16 - SLOTS, 128), F32)

    backward(0)
    groups[0].start()
    backward(1)
    groups[1].start()
    for r in far:
        pl.semaphore_wait(near_sem.at[r], 2)
    groups[0].spread()
    backward(2)
    for i in range(6):
        bt_ref[128 * i : 128 * i + 128, 0:64] = db_ref[:, 128 * i : 128 * i + 128].T
    lane = lax.broadcasted_iota(jnp.int32, (8, 128), 1)
    for j in range(3):
        for i in range(16):
            first = 2 * j + 24 * ((i // 2) % 4) + 12 * (i // 8) + 6 * (i % 2)
            even = bt_ref[pl.ds(first, 8, stride=96), :]
            odd = bt_ref[pl.ds(first + 1, 8, stride=96), :]
            pk_ref[36 + j, 8 * i : 8 * i + 8, :] = jnp.where(lane < 64, even, pltpu.roll(odd, 64, 1))
    groups[2].start()
    groups[1].spread()

    groups[2].spread()
    turns[0].start()
    wide_mask = jnp.concatenate([mask_ref[...]] * 3, 1)
    x_ref[...] = wide_mask * dot_nn(o_ref[...], wproj_ref[...])
    for i in range(4):
        uu_ref[i] = grid_row(x_ref, 1, i).astype(BF16)
    c_ref[...] = dot_nt(dqkv_ref[...], wqkv_ref[...])

    def back(i, carry):
        rows = pl.ds(pl.multiple_of(i * 64, 64), 64)
        dh = c_ref[rows, :]
        n = n_ref[rows, :]
        inv = jnp.concatenate([inv_ref[rows, :]] * 3, 1)
        slope = jnp.mean(dh * n, -1, keepdims=True)
        c_ref[rows, :] = inv * (dh - jnp.mean(dh, -1, keepdims=True) - n * slope)
        return carry

    lax.fori_loop(0, WB, back, 0, unroll=3)
    for i in range(4):
        ug_ref[i] = grid_row(c_ref, 1, i).astype(BF16)
    turns[1].start()
    turns[2].start()
    halo_u = send(uu_ref, hu_ref, halo_s.at[3], halo_r.at[3], after_id)
    halo_g = send(ug_ref, hg_ref, halo_s.at[4], halo_r.at[4], after_id)
    turns[0].collect(f_ref)
    for i in range(4):
        row = grid_row(x_ref, 0, i).astype(BF16).astype(F32)
        block_ref[4 + i] = (tok_ref[4 + i].astype(F32) + row).astype(BF16)
        row = grid_row(c_ref, 0, i).astype(BF16).astype(F32)
        grad_out_ref[4 + i] = (cot_ref[4 + i].astype(F32) + row).astype(BF16)
    upper, lower = pl.ds(4, 4), pl.ds(0, 4)
    keep(block_ref.at[upper], block_hbm.at[upper])
    keep(grad_out_ref.at[upper], grad_hbm.at[upper])
    turns[1].collect(f_ref)
    turns[2].collect(f_ref)
    share.start()
    inner = jnp.broadcast_to(linear, (4, 48, C)) > 0
    halo_u.wait_recv()
    low = jnp.where(inner, hu_ref[...].astype(F32), 0.0)
    block_ref[0:4] = (tok_ref[0:4].astype(F32) + low).astype(BF16)
    keep(block_ref.at[lower], block_hbm.at[lower])
    halo_g.wait_recv()
    low = jnp.where(inner, hg_ref[...].astype(F32), 0.0)
    grad_out_ref[0:4] = (cot_ref[0:4].astype(F32) + low).astype(BF16)
    keep(grad_out_ref.at[lower], grad_hbm.at[lower])
    for one in groups + turns:
        for copy in one.sent:
            copy.wait_send()
    share.finish(red_ref)
    keep(red_ref, red_hbm)
    share.drain()
    for copy in halos + [halo_u, halo_g]:
        copy.wait_send()
    for copy in kept:
        copy.wait()


def place_kernel(
    block_hbm, grad_hbm, red_hbm, block_out, grad_out, qkv_out, proj_out, bias_out,
    block_ref, grad_ref, red_ref, qkv_ref, proj_ref, bias_ref, in_sem, out_sem,
):
    load = pltpu.make_async_copy(red_hbm, red_ref, in_sem.at[4])
    load.start()
    moves = []
    for i, (src, via, dst) in enumerate(((block_hbm, block_ref, block_out), (grad_hbm, grad_ref, grad_out))):
        for j in range(2):
            part = pl.ds(4 * j, 4)
            into = pltpu.make_async_copy(src.at[part], via.at[part], in_sem.at[2 * i + j])
            into.start()
            moves.append((into, pltpu.make_async_copy(via.at[part], dst.at[part], out_sem.at[2 * i + j])))
    load.wait()
    g = lax.rem(lax.axis_index("grp"), 4)
    lane = lax.broadcasted_iota(jnp.int32, (16, 128), 1)
    red = red_ref[...]
    following = jnp.concatenate([red[1:16], red[0:1]], 0)
    rolled = [red]
    for quarter in range(1, 4):
        shift = 128 - 32 * quarter
        value = jnp.where(lane < shift, pltpu.roll(red, shift, 1), pltpu.roll(following, shift, 1))
        rolled.append(value)

    def pick(step):
        which = jnp.broadcast_to(lax.rem(step * g, 4), (16, 128))
        value = rolled[0]
        for quarter in range(1, 4):
            value = jnp.where(which == quarter, rolled[quarter], value)
        return value

    for into, out in moves:
        into.wait()
        out.start()
    small = []
    for i, (ref, out, step, first, size) in enumerate(
        (
            (qkv_ref, qkv_out, 27, 0, 864),
            (proj_ref, proj_out, 9, 8, 288),
            (bias_ref, bias_out, 3, 11, 96),
        )
    ):
        value = pick(step)
        for j in range(-(-size // 128)):
            n = min(128, size - 128 * j)
            ref[pl.ds(128 * j, n)] = value[first + j, 0:n]
        small.append(pltpu.make_async_copy(ref, out, out_sem.at[4 + i]))
        small[-1].start()
    for out in [out for into, out in moves] + small:
        out.wait()


def local(tokens, cotangent, ocean_mask, land_mask, w_qkv, w_proj, rel_bias):
    grid = jax.ShapeDtypeStruct((8, 48, C), BF16)
    dma = pltpu.SemaphoreType.DMA
    half = pltpu.VMEM((4, 48, C), BF16)
    scratch = [
        pltpu.VMEM((8, 48, C), BF16),
        pltpu.VMEM((8, 48, C), BF16),
        pltpu.VMEM((16, 128), F32),
        pltpu.VMEM((8, 48, C), BF16),
        pltpu.VMEM((8, 48, C), BF16),
        pltpu.VMEM((8, 48), jnp.int32),
        pltpu.VMEM((1, 6), jnp.int32),
        pltpu.VMEM((C, 3 * C), BF16),
        pltpu.VMEM((C, C), BF16),
        pltpu.VMEM((12, 64, 64), F32),
        half, half, pltpu.VMEM((8, 48), jnp.int32), half, half, half, half,
        pltpu.VMEM((C, C), F32),
        pltpu.VMEM((C, C), F32),
        pltpu.VMEM((C, C), F32),
        pltpu.VMEM((C, 128), F32),
        pltpu.VMEM((C, 128), F32),
        pltpu.VMEM((C, C), BF16),
        pltpu.VMEM((C, C), BF16),
        pltpu.VMEM((C, 3 * C), BF16),
        pltpu.VMEM((C, C), BF16),
        pltpu.VMEM((C, C), BF16),
        pltpu.VMEM((C, C), BF16),
        pltpu.VMEM((C, 3 * C), BF16),
        pltpu.VMEM((C, C), BF16),
        pltpu.VMEM((C, 768), F32),
        pltpu.VMEM((64, 768), F32),
        pltpu.VMEM((64, 768), F32),
        pltpu.VMEM((C, C), BF16),
        pltpu.VMEM((39, 128, 128), F32),
        pltpu.VMEM((768, 128), F32),
        pltpu.VMEM((8, 16, 128), F32),
        pltpu.VMEM((8, 16, 128), BF16),
        pltpu.VMEM((NZ, 16, 128), BF16),
        dma((15,)), dma((5,)), dma((5,)), dma((5,)), dma((8,)), dma((NZ,)),
        pltpu.SemaphoreType.REGULAR((5,)),
    ]
    for rows in GROUPS:
        scratch += group_scratch(len(rows))
    for rows in GROUPS:
        scratch += turn_scratch(len(rows))
    block_out, token_grad, red = pl.pallas_call(
        kernel,
        out_shape=[grid, grid, jax.ShapeDtypeStruct((16, 128), F32)],
        in_specs=[pl.BlockSpec(memory_space=pltpu.HBM)] * 7,
        out_specs=[pl.BlockSpec(memory_space=pltpu.HBM)] * 3,
        scratch_shapes=scratch,
        compiler_params=pltpu.CompilerParams(
            collective_id=0, has_side_effects=True, vmem_limit_bytes=VMEM_BYTES
        ),
        cost_estimate=pl.CostEstimate(flops=15 * 10**8, bytes_accessed=5 * 10**6, transcendentals=300000),
        name="window_block",
    )(tokens, cotangent, ocean_mask, land_mask, w_qkv, w_proj, rel_bias)

    hbm = pl.BlockSpec(memory_space=pltpu.HBM)
    return tuple(
        pl.pallas_call(
            place_kernel,
            out_shape=[grid, grid] + [jax.ShapeDtypeStruct((n,), F32) for n in (864, 288, 96)],
            in_specs=[hbm] * 3,
            out_specs=[hbm] * 5,
            scratch_shapes=[
                pltpu.VMEM((8, 48, C), BF16),
                pltpu.VMEM((8, 48, C), BF16),
                pltpu.VMEM((16, 128), F32),
                pltpu.VMEM((864,), F32),
                pltpu.VMEM((288,), F32),
                pltpu.VMEM((96,), F32),
                dma((5,)),
                dma((7,)),
            ],
            compiler_params=pltpu.CompilerParams(vmem_limit_bytes=VMEM_BYTES),
            cost_estimate=pl.CostEstimate(flops=10**4, bytes_accessed=12 * 10**5, transcendentals=0),
            name="outputs",
        )(block_out, token_grad, red)
    )


def solution(mesh):
    split = ("band", "grp")
    placed = (
        P(split, None, None),
        P(split, None, None),
        P(split, None),
        P(split, None),
        P(),
        P(),
        P(),
    )
    return jax.shard_map(
        local,
        mesh=mesh,
        in_specs=placed,
        out_specs=(P(split, None, None), P(split, None, None), P(split), P(split), P(split)),
        check_vma=False,
    )
```

```python
import math

import jax
import jax.numpy as jnp
from jax import lax
from jax.experimental import pallas as pl
from jax.experimental.pallas import tpu as pltpu
from jax.sharding import PartitionSpec as P

EPS = 1e-05
MASKED = -1e30
C = 384
WB = 6
HG = 3
SCALE = 1.0 / math.sqrt(32)
F32 = jnp.float32
BF16 = jnp.bfloat16
MESH = pl.DeviceIdType.MESH

NY, NX, NZ = 8, 4, 8
OWN = 192
VMEM_BYTES = 62 * 2**20


def qkv_rows(g):
    return [("qkv", j, k) for k in (g, 3 + g, 6 + g) for j in range(3)]


PROJ_ROWS = [("proj", j, k) for k in range(3) for j in range(3)]
BIAS_ROWS = [("bias", j, 0) for j in range(3)]
GROUPS = [PROJ_ROWS + qkv_rows(0), qkv_rows(1)[:8], qkv_rows(1)[8:] + qkv_rows(2) + BIAS_ROWS]
SLOTS = 13
X_ORDER = (2, 1, 3)
Y_ORDER = (4, 3, 5, 2, 6, 1, 7)
Z_ORDER = (4, 3, 5, 2, 6, 1, 7, 0)


def owned(g):
    qkv = [min(27 * g // 4 + i, 26) for i in range(8)]
    proj = [min(9 * g // 4 + i, 8) for i in range(3)]
    bias = [min(3 * g // 4 + i, 2) for i in range(2)]
    return (
        [("qkv", r // 9, r % 9) for r in qkv]
        + [("proj", r // 3, r % 3) for r in proj]
        + [("bias", r, 0) for r in bias]
    )


def dot_nt(a, b):
    return lax.dot_general(a, b, (((1,), (1,)), ((), ())), preferred_element_type=F32)


def dot_tn(a, b):
    return lax.dot_general(a, b, (((0,), (0,)), ((), ())), preferred_element_type=F32)


def dot_nn(a, b):
    return lax.dot_general(a, b, (((1,), (0,)), ((), ())), preferred_element_type=F32)


def stage_mask(ocean, land, half, mask_ref):
    place = lax.broadcasted_iota(jnp.int32, (8, 48), 0)
    column = lax.broadcasted_iota(jnp.int32, (8, 48), 1)
    for w in range(WB):
        live = 1.0 - land[:, w : w + 1]
        pick = (column == lax.rem(place + (8 * w + 4), 48)).astype(F32) * live
        for i in range(4):
            row = jnp.broadcast_to(ocean[i : i + 1, :], (8, 48))
            value = jnp.sum(row * pick, axis=1, keepdims=True)
            at = OWN * half + 32 * w + 8 * i
            mask_ref[at : at + 8, :] = jnp.broadcast_to(value, (8, 128))


def stage_rows(rows, half, out_ref):
    for i, row in enumerate(rows):
        rolled = pltpu.roll(row.astype(F32), 44, 0)
        for w in range(WB):
            at = OWN * half + 32 * w + 8 * i
            out_ref[at : at + 8, :] = rolled[8 * w : 8 * w + 8, :]


def grid_row(src_ref, half, i):
    ats = [OWN * half + 32 * w + 8 * i for w in range(WB)]
    return pltpu.roll(jnp.concatenate([src_ref[at : at + 8, :] for at in ats], 0), 4, 0)


class Group:
    def __init__(self, rows, base, pk_ref, refs, here, plan):
        self.rows, self.n, self.base, self.pk = rows, len(rows), base, pk_ref
        self.pack, self.r0, self.s1, self.rx, core_s, core_r, x_s, x_r = refs
        band, grp, y, x, z, core = here
        self.theirs = pl.ds(pl.multiple_of((1 - core) * 64, 64), 64)
        self.mine = pl.ds(pl.multiple_of(core * 64, 64), 64)
        self.own = pl.ds(pl.multiple_of(16 * x, 16), 16)
        self.core_copy = plan(self.pack, self.r0, core_s.at[0], core_r.at[0], (band, z * 2 + 1 - core))
        self.sent = []
        for d in X_ORDER:
            to = lax.rem(x + d, NX)
            part = self.s1.at[:, pl.ds(pl.multiple_of(16 * to, 16), 16), :]
            self.sent.append(plan(part, self.rx.at[d - 1], x_s.at[d - 1], x_r.at[d - 1], (y * NX + to, grp)))

    def start(self):
        def narrow(i, carry):
            self.pack[i] = self.pk[self.base + i, self.theirs, :].astype(BF16)
            return carry

        lax.fori_loop(0, self.n, narrow, 0, unroll=2)
        self.core_copy.start()

    def spread(self):
        self.core_copy.wait()

        def add(i, carry):
            total = self.pk[self.base + i, self.mine, :] + self.r0[i].astype(F32)
            self.s1[i] = total.astype(BF16)
            return carry

        lax.fori_loop(0, self.n, add, 0, unroll=2)
        for copy in self.sent:
            copy.start()

    def take(self, wide_ref, padded):
        total = self.s1[:, self.own, :].astype(F32)
        for copy, d in zip(self.sent, X_ORDER):
            copy.wait_recv()
            total = total + self.rx[d - 1].astype(F32)
        for i in range(self.n):
            for quarter in range(2):
                at = pl.ds(quarter * padded + i, NY, stride=2 * padded)
                wide_ref[at, :] = total[i, 8 * quarter : 8 * quarter + 8, :]


def padded_of(n):
    return -(-n // 8) * 8


class Turn:
    def __init__(self, group, refs, here, plan):
        self.group, self.rows, self.padded = group, group.rows, padded_of(group.n)
        self.wide, self.tb, self.ry, y_s, y_r = refs
        band, grp, y, x, z, core = here
        n = 2 * self.padded
        self.own = pl.ds(pl.multiple_of(y * n, 8), n)
        self.sent = []
        for d in Y_ORDER:
            to = lax.rem(y + d, NY)
            self.sent.append(
                plan(self.tb.at[to], self.ry.at[d - 1], y_s.at[d - 1], y_r.at[d - 1], (to * NX + x, grp))
            )

    def clear(self):
        for i in range(len(self.rows), self.padded):
            for quarter in range(2):
                at = pl.ds(quarter * self.padded + i, NY, stride=2 * self.padded)
                self.wide[at, :] = jnp.zeros((NY, 128), F32)

    def start(self):
        n = 2 * self.padded
        self.group.take(self.wide, self.padded)
        for i in range(NY):
            self.tb[i] = self.wide[n * i : n * (i + 1), :].astype(BF16)
        for copy in self.sent:
            copy.start()

    def collect(self, f_ref):
        total = self.wide[self.own, :]
        for copy, d in zip(self.sent, Y_ORDER):
            copy.wait_recv()
            total = total + self.ry[d - 1].astype(F32)
        for i in range(8):
            for at, row in enumerate(owned(i % 4)):
                if row in self.rows:
                    first = self.padded * (i // 4) + self.rows.index(row)
                    f_ref[i, at : at + 1, :] = total[first : first + 1, :]


class Share:
    def __init__(self, wide_ref, f_ref, r3_ref, z_s, z_r, here):
        self.wide, self.f, self.r3, self.z_s, self.z_r, self.here = wide_ref, f_ref, r3_ref, z_s, z_r, here

    def copies(self):
        band, grp, y, x, z, core = self.here
        for d in Z_ORDER:
            to_z = lax.rem(z + d, NZ)
            for to_core in range(2):
                i = 2 * lax.rem(to_z, 4) + to_core
                copy = pltpu.make_async_remote_copy(
                    src_ref=self.f.at[i],
                    dst_ref=self.r3.at[z],
                    send_sem=self.z_s.at[i],
                    recv_sem=self.z_r.at[z],
                    device_id=(band, to_z * 2 + to_core),
                    device_id_type=MESH,
                )
                away = to_z // 4 == core
                if d == 0:
                    away = jnp.logical_and(away, core != to_core)
                yield copy, away

    def start(self):
        self.f[...] = self.wide[...].astype(BF16)
        for copy, away in self.copies():
            pl.when(away)(copy.start)

    def finish(self, red_ref):
        band, grp, y, x, z, core = self.here
        own_core = z // 4

        @pl.when(core == own_core)
        def _():
            self.r3[z] = self.f[4 * lax.rem(z // 2, 2) + lax.rem(grp, 4)]

        for s in range(NZ):
            come = pltpu.make_async_remote_copy(
                src_ref=self.f.at[0],
                dst_ref=self.r3.at[s],
                send_sem=self.z_s.at[0],
                recv_sem=self.z_r.at[s],
                device_id=(band, z * 2 + 1 - core),
                device_id_type=MESH,
            )
            pl.when(jnp.logical_or(z != s, core != own_core))(come.wait_recv)
        total = self.r3[0].astype(F32)
        for s in range(1, NZ):
            total = total + self.r3[s].astype(F32)
        red_ref[...] = total

    def drain(self):
        for copy, away in self.copies():
            pl.when(away)(copy.wait_send)


def group_scratch(n):
    dma = pltpu.SemaphoreType.DMA
    return [
        pltpu.VMEM((n, 64, 128), BF16),
        pltpu.VMEM((n, 64, 128), BF16),
        pltpu.VMEM((n, 64, 128), BF16),
        pltpu.VMEM((NX - 1, n, 16, 128), BF16),
        dma((1,)), dma((1,)), dma((NX - 1,)), dma((NX - 1,)),
    ]


def turn_scratch(n):
    dma = pltpu.SemaphoreType.DMA
    wide = 2 * padded_of(n)
    return [
        pltpu.VMEM((NY * wide, 128), F32),
        pltpu.VMEM((NY, wide, 128), BF16),
        pltpu.VMEM((NY - 1, wide, 128), BF16),
        dma((NY - 1,)), dma((NY - 1,)),
    ]


def permutation():
    at = lax.broadcasted_iota(jnp.int32, (C, C), 0)
    feature = lax.broadcasted_iota(jnp.int32, (C, C), 1)

    def bits(low, count):
        return lax.bitwise_and(lax.shift_right_logical(at, jnp.full_like(at, low)), (1 << count) - 1)

    m = 16 * bits(0, 3) + bits(3, 1) + 4 * bits(4, 2) + 2 * bits(6, 1)
    return (feature == 3 * m + bits(7, 2)).astype(F32).astype(BF16)


def kernel(
    tok_hbm, cot_hbm, oce_hbm, land_hbm, wqkv_hbm, wproj_hbm, rb_hbm,
    block_hbm, grad_hbm, red_hbm,
    block_ref, grad_out_ref, red_ref,
    tok_ref, cot_ref, oce_ref, land_ref, wqkv_ref, wproj_ref, rb_ref,
    htok_ref, hcot_ref, hoce_ref, uu_ref, ug_ref, hu_ref, hg_ref,
    x_ref, c_ref, n_ref, inv_ref, mask_ref, h_ref, ht_ref, qkv_ref, dz_ref, do_ref, o_ref, dqkv_ref, ot_ref,
    p_ref, bias_ref, db_ref, perm_ref, pk_ref, bt_ref, f_ref, low_ref, r3_ref, load_sem, store_sem, halo_s, halo_r, z_s, z_r, near_sem, *rest,
):
    band = lax.axis_index("band")
    grp = lax.axis_index("grp")
    y, x = band // NX, lax.rem(band, NX)
    z, core = grp // 2, lax.rem(grp, 2)
    linear = band * 16 + grp
    after = lax.rem(linear + 1, 512)
    before = lax.rem(linear + 511, 512)
    after_id = (after // 16, lax.rem(after, 16))
    before_id = (before // 16, lax.rem(before, 16))

    barrier = pltpu.get_barrier_semaphore()


    def at_z(d):
        return (band, lax.rem(z + NZ + d, NZ) * 2 + core)

    def at_y(d):
        return (lax.rem(y + NY + d, NY) * NX + x, grp)

    def at_x(d):
        return (y * NX + lax.rem(x + NX + d, NX), grp)

    peers = [after_id, before_id, (band, z * 2 + 1 - core)]
    peers += [at(d) for at in (at_z, at_y, at_x) for d in (1, -1)]
    for peer in peers:
        pl.semaphore_signal(barrier, inc=1, device_id=peer, device_id_type=MESH)

    def blocks(ref, i, j):
        return ref.at[:, pl.ds(C * i + 128 * j, 128)]

    loads = []
    for i, (src, dst) in enumerate(
        [(tok_hbm, tok_ref), (oce_hbm, oce_ref), (land_hbm, land_ref), (cot_hbm, cot_ref)]
        + [(wproj_hbm, wproj_ref), (rb_hbm, rb_ref)]
        + [(blocks(wqkv_hbm, i, j), blocks(wqkv_ref, j, i)) for j in range(HG) for i in range(3)]
    ):
        loads.append(pltpu.make_async_copy(src, dst, load_sem.at[i]))
        loads[-1].start()

    def tell(r, at, d):
        for to in (at(d), at(-d)):
            pl.semaphore_signal(near_sem.at[r], inc=1, device_id=to, device_id_type=MESH)

    def plan(src, dst, s, r, to):
        return pltpu.make_async_remote_copy(
            src_ref=src, dst_ref=dst, send_sem=s, recv_sem=r, device_id=to, device_id_type=MESH
        )

    def send(*args):
        copy = plan(*args)
        copy.start()
        return copy

    kept = []

    def keep(src, dst):
        kept.append(pltpu.make_async_copy(src, dst, store_sem.at[len(kept)]))
        kept[-1].start()

    pl.semaphore_wait(barrier, len(peers))
    tell(0, at_z, 1)
    tell(1, at_y, 1)
    tell(2, at_x, 1)
    far = (2, 3, 4)
    halos = [
        send(tok_hbm.at[pl.ds(0, 4)], htok_ref, halo_s.at[0], halo_r.at[0], before_id),
        send(oce_hbm, hoce_ref, halo_s.at[1], halo_r.at[1], before_id),
        send(cot_hbm.at[pl.ds(0, 4)], hcot_ref, halo_s.at[2], halo_r.at[2], before_id),
    ]

    loads[0].wait()
    stage_rows([tok_ref[4 + i] for i in range(4)], 0, x_ref)
    perm_ref[...] = permutation()

    def norm(i, carry):
        rows = pl.ds(pl.multiple_of(i * 64, 64), 64)
        value = x_ref[rows, :]
        centered = value - jnp.mean(value, -1, keepdims=True)
        inv = lax.rsqrt(jnp.mean(centered * centered, -1, keepdims=True) + EPS)
        n = centered * inv
        n_ref[rows, :] = n
        inv_ref[rows, :] = jnp.broadcast_to(inv, (64, 128))
        h_ref[rows, :] = n.astype(BF16)
        return carry

    def project(half):
        rows = slice(OWN * half, OWN * half + OWN)
        qkv_ref[rows, :] = dot_nn(h_ref[rows, :], wqkv_ref[...]).astype(BF16)

    def pull(half):
        rows = slice(OWN * half, OWN * half + OWN)
        wide = jnp.concatenate([mask_ref[rows, :]] * 3, 1)
        dz_ref[rows, :] = (wide * c_ref[rows, :]).astype(BF16)
        do_ref[rows, :] = dot_nt(dz_ref[rows, :], wproj_ref[...]).astype(BF16)

    lax.fori_loop(0, 3, norm, 0, unroll=3)
    loads[1].wait()
    loads[2].wait()
    land = land_ref[...].astype(F32)
    stage_mask(oce_ref[4:8, :].astype(F32), land, 0, mask_ref)
    for i in range(6, 15):
        loads[i].wait()
    project(0)
    loads[3].wait()
    stage_rows([cot_ref[4 + i] for i in range(4)], 0, c_ref)
    loads[4].wait()
    pull(0)
    loads[5].wait()
    for i in range(6):
        pair = jnp.concatenate([rb_ref[2 * i], rb_ref[2 * i + 1]], 0)
        bias_ref[:, 128 * i : 128 * i + 128] = pair.T
    db_ref[...] = jnp.zeros_like(db_ref)

    here_lower = jnp.broadcast_to(linear, (48, C)) < 511
    halos[0].wait_recv()
    stage_rows([jnp.where(here_lower, htok_ref[i].astype(F32), 0.0) for i in range(4)], 1, x_ref)
    lax.fori_loop(3, 6, norm, 0, unroll=3)
    project(1)
    for r in (0, 1):
        pl.semaphore_wait(near_sem.at[r], 2)
    tell(3, at_z, 2)
    tell(4, at_y, 2)
    ht_ref[...] = dot_nt(perm_ref[...], h_ref[...]).astype(BF16)
    halos[1].wait_recv()
    ocean = jnp.where(jnp.broadcast_to(linear, (4, 48)) < 511, hoce_ref[0:4, :].astype(F32), 0.0)
    stage_mask(ocean, land, 1, mask_ref)

    head = lax.broadcasted_iota(jnp.int32, (64, 128), 1) // 32
    picks = [(head == i).astype(F32) for i in range(4)]
    picks_low = [p.astype(BF16) for p in picks]

    def spread(a):
        return jnp.concatenate([a * p for p in picks_low], 0)

    def fold(value):
        total = value[0:64] * picks[0]
        for i in range(1, 4):
            total = total + value[64 * i : 64 * i + 64] * picks[i]
        return total

    def two(w):
        first = pl.ds(pl.multiple_of(w * 32, 32), 32)
        second = pl.ds(pl.multiple_of(OWN + w * 32, 32), 32)
        return first, second

    def load(ref, w, lanes):
        first, second = two(w)
        return jnp.concatenate([ref[first, lanes], ref[second, lanes]], 0)

    def store(ref, w, lanes, value):
        first, second = two(w)
        ref[first, lanes] = value[0:32]
        ref[second, lanes] = value[32:64]

    def lanes_of(g):
        return [slice(C * g + 128 * i, C * g + 128 * i + 128) for i in range(3)] + [
            slice(256 * g, 256 * g + 256),
            slice(128 * g, 128 * g + 128),
        ]

    def forward(w, carry):
        whole = pl.ds(pl.multiple_of(w * 64, 64), 64)
        live = jnp.concatenate([load(mask_ref, w, slice(0, 128))] * 2, 1) > 0.5
        for g in range(HG):
            q_lanes, k_lanes, v_lanes, wide, head_lanes = lanes_of(g)
            q4 = spread(load(qkv_ref, w, q_lanes))
            s = dot_nt(load(qkv_ref, w, k_lanes), q4) * SCALE + bias_ref[:, wide]
            s = jnp.where(live, s, MASKED)
            weights = jnp.exp(s - jnp.max(s, 0, keepdims=True))
            p = weights * (1.0 / jnp.sum(weights, 0, keepdims=True))
            p_ref[whole, wide] = p
            store(o_ref, w, head_lanes, fold(dot_tn(p.astype(BF16), load(qkv_ref, w, v_lanes))).astype(BF16))
        return carry

    def backward(g):
        q_lanes, k_lanes, v_lanes, wide, head_lanes = lanes_of(g)

        def step(w, carry):
            whole = pl.ds(pl.multiple_of(w * 64, 64), 64)
            q4 = spread(load(qkv_ref, w, q_lanes))
            do4 = spread(load(do_ref, w, head_lanes))
            p = p_ref[whole, wide]
            dp = dot_nt(load(qkv_ref, w, v_lanes), do4)
            store(dqkv_ref, w, v_lanes, dot_nn(p.astype(BF16), do4).astype(BF16))
            ds = p * (dp - jnp.sum(p * dp, 0, keepdims=True))
            db_ref[:, wide] += ds
            dsc = (ds * SCALE).astype(BF16)
            store(dqkv_ref, w, k_lanes, dot_nn(dsc, q4).astype(BF16))
            dq = fold(dot_tn(dsc, load(qkv_ref, w, k_lanes)))
            store(dqkv_ref, w, q_lanes, dq.astype(BF16))
            return carry

        lax.fori_loop(0, WB, step, 0, unroll=6)
        fill(9 + 9 * g, dot_nn(ht_ref[...], dqkv_ref[:, C * g : C * g + C]))

    lax.fori_loop(0, WB, forward, 0, unroll=6)

    halos[2].wait_recv()
    stage_rows([jnp.where(here_lower, hcot_ref[i].astype(F32), 0.0) for i in range(4)], 1, c_ref)
    pull(1)

    here = (band, grp, y, x, z, core)
    groups, turns = [], []
    at = base = 0
    for rows in GROUPS:
        groups.append(Group(rows, base, pk_ref, rest[at : at + 8], here, plan))
        at += 8
        base += len(rows)
    for group in groups:
        turns.append(Turn(group, rest[at : at + 5], here, plan))
        at += 5
    share = Share(f_ref, low_ref, r3_ref, z_s, z_r, here)

    def fill(base, value):
        for k in range(3):
            for j in range(3):
                pk_ref[base + 3 * k + j] = value[128 * j : 128 * j + 128, 128 * k : 128 * k + 128]

    ot_ref[...] = dot_nt(perm_ref[...], o_ref[...]).astype(BF16)
    fill(0, dot_nn(ot_ref[...], dz_ref[...]))
    for turn in turns:
        turn.clear()
    for i in range(8):
        f_ref[i, SLOTS:16, :] = jnp.zeros((16 - SLOTS, 128), F32)

    backward(0)
    groups[0].start()
    backward(1)
    groups[1].start()
    for r in far:
        pl.semaphore_wait(near_sem.at[r], 2)
    groups[0].spread()
    backward(2)
    for i in range(6):
        bt_ref[128 * i : 128 * i + 128, 0:64] = db_ref[:, 128 * i : 128 * i + 128].T
    lane = lax.broadcasted_iota(jnp.int32, (8, 128), 1)
    for j in range(3):
        for i in range(16):
            first = 2 * j + 24 * ((i // 2) % 4) + 12 * (i // 8) + 6 * (i % 2)
            even = bt_ref[pl.ds(first, 8, stride=96), :]
            odd = bt_ref[pl.ds(first + 1, 8, stride=96), :]
            pk_ref[36 + j, 8 * i : 8 * i + 8, :] = jnp.where(lane < 64, even, pltpu.roll(odd, 64, 1))
    groups[2].start()
    groups[1].spread()

    groups[2].spread()
    turns[0].start()
    wide_mask = jnp.concatenate([mask_ref[...]] * 3, 1)
    x_ref[...] = wide_mask * dot_nn(o_ref[...], wproj_ref[...])
    for i in range(4):
        uu_ref[i] = grid_row(x_ref, 1, i).astype(BF16)
    c_ref[...] = dot_nt(dqkv_ref[...], wqkv_ref[...])

    def back(i, carry):
        rows = pl.ds(pl.multiple_of(i * 64, 64), 64)
        dh = c_ref[rows, :]
        n = n_ref[rows, :]
        inv = jnp.concatenate([inv_ref[rows, :]] * 3, 1)
        slope = jnp.mean(dh * n, -1, keepdims=True)
        c_ref[rows, :] = inv * (dh - jnp.mean(dh, -1, keepdims=True) - n * slope)
        return carry

    lax.fori_loop(0, WB, back, 0, unroll=3)
    for i in range(4):
        ug_ref[i] = grid_row(c_ref, 1, i).astype(BF16)
    turns[1].start()
    turns[2].start()
    halo_u = send(uu_ref, hu_ref, halo_s.at[3], halo_r.at[3], after_id)
    halo_g = send(ug_ref, hg_ref, halo_s.at[4], halo_r.at[4], after_id)
    turns[0].collect(f_ref)
    for i in range(4):
        row = grid_row(x_ref, 0, i).astype(BF16).astype(F32)
        block_ref[4 + i] = (tok_ref[4 + i].astype(F32) + row).astype(BF16)
        row = grid_row(c_ref, 0, i).astype(BF16).astype(F32)
        grad_out_ref[4 + i] = (cot_ref[4 + i].astype(F32) + row).astype(BF16)
    upper, lower = pl.ds(4, 4), pl.ds(0, 4)
    keep(block_ref.at[upper], block_hbm.at[upper])
    keep(grad_out_ref.at[upper], grad_hbm.at[upper])
    turns[1].collect(f_ref)
    turns[2].collect(f_ref)
    share.start()
    inner = jnp.broadcast_to(linear, (4, 48, C)) > 0
    halo_u.wait_recv()
    low = jnp.where(inner, hu_ref[...].astype(F32), 0.0)
    block_ref[0:4] = (tok_ref[0:4].astype(F32) + low).astype(BF16)
    keep(block_ref.at[lower], block_hbm.at[lower])
    halo_g.wait_recv()
    low = jnp.where(inner, hg_ref[...].astype(F32), 0.0)
    grad_out_ref[0:4] = (cot_ref[0:4].astype(F32) + low).astype(BF16)
    keep(grad_out_ref.at[lower], grad_hbm.at[lower])
    for one in groups + turns:
        for copy in one.sent:
            copy.wait_send()
    share.finish(red_ref)
    keep(red_ref, red_hbm)
    share.drain()
    for copy in halos + [halo_u, halo_g]:
        copy.wait_send()
    for copy in kept:
        copy.wait()


def place_kernel(
    block_hbm, grad_hbm, red_hbm, block_out, grad_out, qkv_out, proj_out, bias_out,
    block_ref, grad_ref, red_ref, qkv_ref, proj_ref, bias_ref, in_sem, out_sem,
):
    load = pltpu.make_async_copy(red_hbm, red_ref, in_sem.at[4])
    load.start()
    moves = []
    for i, (src, via, dst) in enumerate(((block_hbm, block_ref, block_out), (grad_hbm, grad_ref, grad_out))):
        for j in range(2):
            part = pl.ds(4 * j, 4)
            into = pltpu.make_async_copy(src.at[part], via.at[part], in_sem.at[2 * i + j])
            into.start()
            moves.append((into, pltpu.make_async_copy(via.at[part], dst.at[part], out_sem.at[2 * i + j])))
    load.wait()
    g = lax.rem(lax.axis_index("grp"), 4)
    lane = lax.broadcasted_iota(jnp.int32, (16, 128), 1)
    red = red_ref[...]
    following = jnp.concatenate([red[1:16], red[0:1]], 0)
    rolled = [red]
    for quarter in range(1, 4):
        shift = 128 - 32 * quarter
        value = jnp.where(lane < shift, pltpu.roll(red, shift, 1), pltpu.roll(following, shift, 1))
        rolled.append(value)

    def pick(step):
        which = jnp.broadcast_to(lax.rem(step * g, 4), (16, 128))
        value = rolled[0]
        for quarter in range(1, 4):
            value = jnp.where(which == quarter, rolled[quarter], value)
        return value

    for into, out in moves:
        into.wait()
        out.start()
    small = []
    for i, (ref, out, step, first, size) in enumerate(
        (
            (qkv_ref, qkv_out, 27, 0, 864),
            (proj_ref, proj_out, 9, 8, 288),
            (bias_ref, bias_out, 3, 11, 96),
        )
    ):
        value = pick(step)
        for j in range(-(-size // 128)):
            n = min(128, size - 128 * j)
            ref[pl.ds(128 * j, n)] = value[first + j, 0:n]
        small.append(pltpu.make_async_copy(ref, out, out_sem.at[4 + i]))
        small[-1].start()
    for out in [out for into, out in moves] + small:
        out.wait()


def local(tokens, cotangent, ocean_mask, land_mask, w_qkv, w_proj, rel_bias):
    grid = jax.ShapeDtypeStruct((8, 48, C), BF16)
    dma = pltpu.SemaphoreType.DMA
    half = pltpu.VMEM((4, 48, C), BF16)
    scratch = [
        pltpu.VMEM((8, 48, C), BF16),
        pltpu.VMEM((8, 48, C), BF16),
        pltpu.VMEM((16, 128), F32),
        pltpu.VMEM((8, 48, C), BF16),
        pltpu.VMEM((8, 48, C), BF16),
        pltpu.VMEM((8, 48), jnp.int32),
        pltpu.VMEM((1, 6), jnp.int32),
        pltpu.VMEM((C, 3 * C), BF16),
        pltpu.VMEM((C, C), BF16),
        pltpu.VMEM((12, 64, 64), F32),
        half, half, pltpu.VMEM((8, 48), jnp.int32), half, half, half, half,
        pltpu.VMEM((C, C), F32),
        pltpu.VMEM((C, C), F32),
        pltpu.VMEM((C, C), F32),
        pltpu.VMEM((C, 128), F32),
        pltpu.VMEM((C, 128), F32),
        pltpu.VMEM((C, C), BF16),
        pltpu.VMEM((C, C), BF16),
        pltpu.VMEM((C, 3 * C), BF16),
        pltpu.VMEM((C, C), BF16),
        pltpu.VMEM((C, C), BF16),
        pltpu.VMEM((C, C), BF16),
        pltpu.VMEM((C, 3 * C), BF16),
        pltpu.VMEM((C, C), BF16),
        pltpu.VMEM((C, 768), F32),
        pltpu.VMEM((64, 768), F32),
        pltpu.VMEM((64, 768), F32),
        pltpu.VMEM((C, C), BF16),
        pltpu.VMEM((39, 128, 128), F32),
        pltpu.VMEM((768, 128), F32),
        pltpu.VMEM((8, 16, 128), F32),
        pltpu.VMEM((8, 16, 128), BF16),
        pltpu.VMEM((NZ, 16, 128), BF16),
        dma((15,)), dma((5,)), dma((5,)), dma((5,)), dma((8,)), dma((NZ,)),
        pltpu.SemaphoreType.REGULAR((5,)),
    ]
    for rows in GROUPS:
        scratch += group_scratch(len(rows))
    for rows in GROUPS:
        scratch += turn_scratch(len(rows))
    block_out, token_grad, red = pl.pallas_call(
        kernel,
        out_shape=[grid, grid, jax.ShapeDtypeStruct((16, 128), F32)],
        in_specs=[pl.BlockSpec(memory_space=pltpu.HBM)] * 7,
        out_specs=[pl.BlockSpec(memory_space=pltpu.HBM)] * 3,
        scratch_shapes=scratch,
        compiler_params=pltpu.CompilerParams(
            collective_id=0, has_side_effects=True, vmem_limit_bytes=VMEM_BYTES
        ),
        cost_estimate=pl.CostEstimate(flops=15 * 10**8, bytes_accessed=5 * 10**6, transcendentals=300000),
        name="window_block",
    )(tokens, cotangent, ocean_mask, land_mask, w_qkv, w_proj, rel_bias)

    hbm = pl.BlockSpec(memory_space=pltpu.HBM)
    return tuple(
        pl.pallas_call(
            place_kernel,
            out_shape=[grid, grid] + [jax.ShapeDtypeStruct((n,), F32) for n in (864, 288, 96)],
            in_specs=[hbm] * 3,
            out_specs=[hbm] * 5,
            scratch_shapes=[
                pltpu.VMEM((8, 48, C), BF16),
                pltpu.VMEM((8, 48, C), BF16),
                pltpu.VMEM((16, 128), F32),
                pltpu.VMEM((864,), F32),
                pltpu.VMEM((288,), F32),
                pltpu.VMEM((96,), F32),
                dma((5,)),
                dma((7,)),
            ],
            compiler_params=pltpu.CompilerParams(vmem_limit_bytes=VMEM_BYTES),
            cost_estimate=pl.CostEstimate(flops=10**4, bytes_accessed=12 * 10**5, transcendentals=0),
            name="outputs",
        )(block_out, token_grad, red)
    )


def solution(mesh):
    split = ("band", "grp")
    placed = (
        P(split, None, None),
        P(split, None, None),
        P(split, None),
        P(split, None),
        P(),
        P(),
        P(),
    )
    return jax.shard_map(
        local,
        mesh=mesh,
        in_specs=placed,
        out_specs=(P(split, None, None), P(split, None, None), P(split), P(split), P(split)),
        check_vma=False,
    )
```
